512 devices in a mesh: row: 8 (over y), col: 16 (over z, core), own: 4 (over x).
Axes of the slice: x: 4, y: 8, z: 8, core: 2. Of those that a mesh axis runs over, the one named last changes fastest.
Arguments:
- viscosity: float32 [8192, 2048], P(('row', 'own'), 'col'), may hold values from 0.5 to 8
- friction: float32 [8192, 2048], P(('row', 'own'), 'col'), may hold values from 0.3 to 6
- driving: float32 [2, 8192, 2048], P(None, ('row', 'own'), 'col'), may hold values from -32 to 32
- observed: float32 [2, 8192, 2048], P(None, ('row', 'own'), 'col'), may hold values from -6 to 6
- ice_mask: int32 [8192, 2048], P(('row', 'own'), 'col'), may hold values 0 or 1
- tile_block: int32 [64, 16], P(('row', 'own'), 'col'), may hold values from 0 to 63, as said below
- owner_list: int32 [64], replicated, may hold values from 0 to 63, each once
Outputs:
- velocity: float32 [2, 8192, 2048], P(None, ('row', 'own'), 'col')
- block_gradient: float32 [4, 16, 1024], P('own')
The draws below stay inside these ranges and needn't reach their ends.
Inputs may be any that keep to these rules, and one draw needn't show every extreme that they name: `tile_block`: tile rows 2r and 2r+1 carry the same ids; along the tile columns they run through r*2 to r*2 + 1 in order, each id on one run of consecutive tile columns of ragged length. `owner_list`: every block appears once.
All inputs are finite; a program needn't handle non-finite values. No bound on the sum of `ice_mask` on one device may be relied on, other than what follows from the above.
Results may differ from the reference program's by a relative error of at most 0.000088.
Values sent between devices are 32-bit elements; how exact they have to be, the bound alone decides.
A program may use at most 64 MiB of HBM per device.

```python
import math
import jax
import jax.numpy as jnp
from jax import lax

TILE = 128
MODES = 32
NX = 8192
NY = 2048
GROUPS = 2
NB = 64
N_OWN = 4


def draw_tile_block(key, part):
    tile_rows = NX // TILE
    tile_cols = NY // TILE
    pairs = tile_rows // 2

    def one_pair(pair_index):
        sub_key = jax.random.fold_in(key, pair_index)
        cuts = jax.random.permutation(sub_key, tile_cols - 1)[:GROUPS - 1] + 1
        columns = jnp.arange(tile_cols)
        group = jnp.sum((cuts[:, None] <= columns[None, :]).astype(jnp.int32), axis=0)
        return pair_index * GROUPS + group
    labels = jax.vmap(one_pair)(jnp.arange(pairs))
    return jnp.repeat(labels, 2, axis=0).astype(jnp.int32)


def plant(drawn, stream_key, smallest, largest):
    index_at = [jax.random.randint(jax.random.fold_in(stream_key, axis), (), 0, length) for axis, length in enumerate(drawn.shape)]
    main_axis = drawn.shape.index(max(drawn.shape))
    beside = index_at[:main_axis] + [(index_at[main_axis] + 1) % drawn.shape[main_axis]] + index_at[main_axis + 1:]
    return drawn.at[tuple(index_at)].set(smallest).at[tuple(beside)].set(largest)


def level_of(own_key, dims, shards, low, top_value):
    level, own = 1.0, jax.random.fold_in(own_key, 6)
    for position, parts in shards:
        steps = jnp.exp(jax.random.uniform(jax.random.fold_in(own, position), (parts,), jnp.float32, low / len(shards), top_value / len(shards)))
        level = level * jnp.repeat(steps, dims[position] // parts).reshape([-1 if axis == position else 1 for axis in range(len(dims))])
    return level


def gaussian(stream_key, extent, width, limit, pieces=(), kind=jnp.bfloat16):
    gain = level_of(stream_key, extent, pieces, -0.22, 0.18) if pieces else 1.0
    array = jax.random.normal(stream_key, extent, jnp.float32) * width * gain
    return jnp.minimum(jnp.maximum(array, -limit), limit).astype(kind)


def setup_inputs(seed: int = 0) -> dict:
    streams_of = jax.random.split(jax.random.key(seed), 8)
    viscosity = jnp.clip(jnp.exp(math.log(8.0) - 2.7725887 * jax.random.uniform(streams_of[0], (NX, NY), jnp.float32) ** level_of(streams_of[0], (NX, NY), ((0, 32), (1, 16)), -0.2, 0.2)), 0.5, 8.0)
    friction = jnp.clip(jnp.exp(math.log(6.0) - 2.9957322 * jax.random.uniform(streams_of[1], (NX, NY), jnp.float32) ** level_of(streams_of[1], (NX, NY), ((0, 32), (1, 16)), -0.2, 0.2)), 0.3, 6.0)
    driving = gaussian(streams_of[2], (2, NX, NY), 6.0, 32.0, ((1, 32), (2, 16)), jnp.float32)
    observed = gaussian(streams_of[3], (2, NX, NY), 1.0, 6.0, ((1, 32), (2, 16)), jnp.float32)
    ice_mask = plant((jax.random.randint(streams_of[4], (NX, NY), 0, 8) < 7).astype(jnp.int32), jax.random.fold_in(streams_of[4], 1), 0, 1)
    tile_block = draw_tile_block(jax.random.fold_in(streams_of[7], 71), 0)
    owner_list = jax.random.permutation(streams_of[6], NB).astype(jnp.int32)
    return dict(viscosity=viscosity, friction=friction, driving=driving, observed=observed, ice_mask=ice_mask, tile_block=tile_block, owner_list=owner_list)


damping = 0.5


def along_x(field):
    return 0.5 * ((field[1:, :-1] - field[:-1, :-1]) + (field[1:, 1:] - field[:-1, 1:]))


def along_y(field):
    return 0.5 * ((field[:-1, 1:] - field[:-1, :-1]) + (field[1:, 1:] - field[1:, :-1]))


def back_x(corner):
    return 0.5 * ((corner[:-1, :-1] + corner[:-1, 1:]) - (corner[1:, :-1] + corner[1:, 1:]))


def back_y(corner):
    return 0.5 * ((corner[:-1, :-1] + corner[1:, :-1]) - (corner[:-1, 1:] + corner[1:, 1:]))


def apply_operator(state, viscous, friction_in):
    first_x = along_x(state[0])
    first_y = along_y(state[0])
    second_x = along_x(state[1])
    second_y = along_y(state[1])
    corner_visc = viscous[:-1, :-1]
    normal_one = corner_visc * (4.0 * first_x + 2.0 * second_y)
    shear = corner_visc * (first_y + second_x)
    normal_two = corner_visc * (4.0 * second_y + 2.0 * first_x)
    inner = state[:, 1:-1, 1:-1]
    out_first = back_x(normal_one) + back_y(shear) + friction_in * inner[0]
    out_second = back_y(normal_two) + back_x(shear) + friction_in * inner[1]
    return jnp.stack([out_first, out_second])


def diagonal_of(viscous, friction_in):
    corner = viscous[:-1, :-1]
    return 1.25 * (corner[:-1, :-1] + corner[:-1, 1:] + corner[1:, :-1] + corner[1:, 1:]) + friction_in


def relax(state, viscous, friction_in, target, safe_diag, keep):
    inner = state[:, 1:-1, 1:-1]
    image = apply_operator(state, viscous, friction_in)
    return jnp.where(keep, inner + damping * (target - image) / safe_diag, 0.0)


def cosine_basis():
    places = jnp.arange(TILE, dtype=jnp.float32) + 0.5
    orders = jnp.arange(MODES, dtype=jnp.float32)
    return jnp.cos(math.pi * places[:, None] * orders[None, :] / TILE)


def reference(viscosity, friction, driving, observed, ice_mask, tile_block, owner_list):
    keep = ice_mask > 0
    visc_pad = jnp.pad(viscosity, 1)
    safe_diag = jnp.where(keep, diagonal_of(visc_pad, friction), 1.0)
    state = jnp.where(keep, driving / safe_diag, 0.0)
    for sweep_index in range(3):
        state = relax(jnp.pad(state, ((0, 0), (1, 1), (1, 1))), visc_pad, friction, driving, safe_diag, keep)
    misfit = jnp.where(keep, state - observed, 0.0)
    adjoint = jnp.where(keep, misfit / safe_diag, 0.0)
    for sweep_index in range(3):
        adjoint = relax(jnp.pad(adjoint, ((0, 0), (1, 1), (1, 1))), visc_pad, friction, misfit, safe_diag, keep)
    density = -friction * (adjoint[0] * state[0] + adjoint[1] * state[1])
    tiles = density.reshape(NX // TILE, TILE, NY // TILE, TILE)
    basis = cosine_basis()
    projected = jnp.einsum("ip,aicj,jq->acpq", basis, tiles, basis, precision=lax.Precision.HIGHEST) / TILE
    flat = projected.reshape(-1, MODES * MODES)
    sums = jax.ops.segment_sum(flat, tile_block.reshape(-1).astype(jnp.int32), num_segments=NB)
    picked = sums[owner_list.astype(jnp.int32)]
    return state, picked.reshape(N_OWN, NB // N_OWN, MODES * MODES)
```

```python
import functools
import math

import jax
import jax.numpy as jnp
import numpy as np
from jax import lax
from jax.experimental import pallas as pl
from jax.experimental.pallas import tpu as pltpu
from jax.sharding import PartitionSpec as P

TILE = 128
MODES = 32
LANES = 128
HALO = 8
FIELDS = 7
SWEEPS = 3
MESH = pl.DeviceIdType.MESH
HIGHEST = lax.Precision.HIGHEST


def bases(chunks):
    per = MODES // chunks
    places = np.arange(TILE) + 0.5
    orders = np.arange(MODES)
    cosine = np.cos(math.pi * orders[:, None] * places[None, :] / TILE)
    first = np.concatenate([cosine[s::per] for s in range(per)], axis=0)
    second = np.zeros((per * TILE, LANES))
    for s in range(per):
        for group in range(2):
            at = group * per * MODES + s * MODES
            second[s * TILE : (s + 1) * TILE, at : at + MODES] = cosine.T / TILE
    return first.astype(np.float32), second.astype(np.float32)


def kernel(
    sizes,
    visc,
    fric,
    drv,
    obs,
    mask,
    tile_block,
    owner_list,
    basis_1,
    basis_2,
    vel,
    grad,
    fm,
    mk,
    fs,
    pack,
    pack_t,
    recv_t,
    diag,
    coef,
    hb,
    w,
    v,
    dens,
    b1,
    b2,
    tb,
    ol,
    send_a,
    recv_a,
    table,
    recv_c,
    out,
    load_sem,
    halo_send,
    halo_recv,
    phase_send,
    phase_recv,
    out_sem,
):
    n_row, n_own, n_col = sizes
    n_line = n_row * n_own
    rows = visc.shape[0]
    chunks = (rows + 2 * HALO) // 8
    row_at, own_at, col = (
        lax.axis_index("row"),
        lax.axis_index("own"),
        lax.axis_index("col"),
    )
    line = row_at * n_own + own_at

    def device(line_to, col_to):
        return {
            "row": lax.div(line_to, n_own),
            "own": lax.rem(line_to, n_own),
            "col": col_to,
        }

    def line_by(step):
        return lax.rem(line + (step + n_line), n_line)

    def col_by(step):
        return lax.rem(col + (step + n_col), n_col)

    barrier = pltpu.get_barrier_semaphore()

    def greet(line_to, col_to):
        pl.semaphore_signal(
            barrier, inc=1, device_id=device(line_to, col_to), device_id_type=MESH
        )

    for up in (-1, 1):
        for side in (-1, 1):
            greet(line_by(up), col_by(side))

    def greet_col(i, _):
        greet(line, col_by(i))
        return 0

    def greet_line(i, _):
        greet(line_by(i), col)
        return 0

    lax.fori_loop(1, n_col, greet_col, 0)
    lax.fori_loop(1, n_line, greet_line, 0)

    own_rows = pl.ds(HALO, rows)
    loads = [
        (visc, fm.at[0, own_rows, :]),
        (fric, fm.at[1, own_rows, :]),
        (drv, fm.at[2:4, own_rows, :]),
        (obs, fm.at[4:6, own_rows, :]),
        (mask, mk.at[own_rows, :]),
        (basis_1, b1),
        (basis_2, b2),
        (tile_block, tb),
        (owner_list, ol),
    ]
    loads = [
        pltpu.make_async_copy(src, dst, load_sem.at[i])
        for i, (src, dst) in enumerate(loads)
    ]
    for copy in loads:
        copy.start()

    pl.semaphore_wait(barrier, 4 + (n_col - 1) + (n_line - 1))

    lane = lax.broadcasted_iota(jnp.int32, (8, LANES), 1)
    sub = lax.broadcasted_iota(jnp.int32, (8, LANES), 0)
    last_lane, first_lane, first_sub = lane == LANES - 1, lane == 0, sub == 0

    copies = []

    def send(src, dst, line_to, col_to):
        at = len(copies)
        copy = pltpu.make_async_remote_copy(
            src_ref=src,
            dst_ref=dst,
            send_sem=halo_send.at[at],
            recv_sem=halo_recv.at[at],
            device_id=device(line_to, col_to),
            device_id_type=MESH,
        )
        copy.start()
        copies.append(copy)

    for step, source, target in (
        (-1, 0, HALO + rows),
        (1, rows - HALO, 0),
    ):
        to, take = pl.ds(target, HALO), pl.ds(source, HALO)
        send(visc.at[take, :], fm.at[0, to, :], line_by(step), col)
        send(fric.at[take, :], fm.at[1, to, :], line_by(step), col)
        send(drv.at[:, take, :], fm.at[2:4, to, :], line_by(step), col)
        send(obs.at[:, take, :], fm.at[4:6, to, :], line_by(step), col)
        send(mask.at[take, :], mk.at[to, :], line_by(step), col)

    for copy in loads[:5]:
        copy.wait()

    for t in range(rows // 8):
        at = pl.ds(HALO + 8 * t, 8)
        packed = pltpu.roll(fm[0, at, :], 8, 1)
        for f in range(1, FIELDS):
            piece = fm[f, at, :] if f < 6 else mk[at, :].astype(jnp.float32)
            packed = jnp.where(lane < 16 * f, packed, pltpu.roll(piece, 16 * f + 8, 1))
        pack[8 * t : 8 * t + 8, :] = packed

    for up, source, slot in ((-1, 0, 2), (1, rows - 8, 0)):
        for side in (-1, 1):
            send(
                pack.at[pl.ds(source, 8), :],
                diag.at[slot + (1 if side < 0 else 0)],
                line_by(up),
                col_by(side),
            )

    for part in range(rows // LANES):
        block = pack[part * LANES : (part + 1) * LANES, :]
        pack_t[:, :, part * LANES : (part + 1) * LANES] = block.T.reshape(8, 16, LANES)
    recv_t[FIELDS, :, :] = jnp.zeros((16, rows), jnp.float32)
    send(
        pack_t.at[0:FIELDS, 0:8, :],
        recv_t.at[0:FIELDS, 0:8, :],
        line,
        col_by(1),
    )
    send(
        pack_t.at[0:FIELDS, 8:16, :],
        recv_t.at[0:FIELDS, 8:16, :],
        line,
        col_by(-1),
    )

    for copy in copies:
        copy.wait_recv()

    def unpack(at, packed):
        for f in range(FIELDS):
            fs[f, at, :] = pltpu.roll(packed, LANES - (16 * f + 8), 1)

    from_left = lax.rem(lane, 16) < 8
    unpack(pl.ds(0, 8), jnp.where(from_left, diag[0], diag[1]))
    unpack(pl.ds(HALO + rows, 8), jnp.where(from_left, diag[2], diag[3]))
    for part in range(rows // LANES):
        turned = (
            recv_t[:, :, part * LANES : (part + 1) * LANES].reshape(LANES, LANES).T
        )
        for t in range(LANES // 8):
            unpack(
                pl.ds(HALO + part * LANES + 8 * t, 8), turned[8 * t : 8 * t + 8, :]
            )

    def plus(x):
        a, b = pltpu.roll(x[0], LANES - 1, 1), pltpu.roll(x[1], LANES - 1, 1)
        return jnp.where(last_lane, b, a), jnp.where(last_lane, a, b)

    def minus(x):
        a, b = pltpu.roll(x[0], 1, 1), pltpu.roll(x[1], 1, 1)
        return jnp.where(first_lane, b, a), jnp.where(first_lane, a, b)

    def both(fn, *args):
        return tuple(fn(*parts) for parts in zip(*args))

    def down(x, kept):
        turned = tuple(pltpu.roll(part, 1, 0) for part in x)
        moved = both(lambda k, r: jnp.where(first_sub, k, r), kept, turned)
        return moved, turned

    side_inside = ((lane < 64) & (col < n_col - 1)) | ((lane >= 64) & (col > 0))
    zero = jnp.zeros((8, LANES), jnp.float32)
    kept = (zero, zero)
    for t in range(chunks):
        at = pl.ds(8 * t, 8)
        n = (fm[0, at, :], fs[0, at, :])
        ice = (mk[at, :] > 0, fs[6, at, :] > 0.5)
        inside = (None, side_inside)
        if t == 0 or t == chunks - 1:
            there = line > 0 if t == 0 else line < n_line - 1
            inside = (jnp.broadcast_to(there, (8, LANES)), side_inside & there)
            n = (jnp.where(inside[0], n[0], 0.0), n[1])
            ice = (ice[0] & inside[0], ice[1])
        n = (n[0], jnp.where(inside[1], n[1], 0.0))
        ice = (ice[0], ice[1] & inside[1])
        summed = both(lambda x, y: x + y, n, minus(n))
        moved, kept = down(summed, kept)
        for i, source in ((0, fm), (1, fs)):
            f = source[1, at, :]
            half = jnp.where(
                ice[i], 0.5 / (1.25 * (summed[i] + moved[i]) + f), 0.0
            )
            coef[i, 0, at, :] = 0.5 * n[i]
            coef[i, 1, at, :] = 0.25 * n[i]
            coef[i, 2, at, :] = half
            coef[i, 3, at, :] = 1.0 - half * f
            for k in range(2):
                scaled = half * source[2 + k, at, :]
                hb[i, k, at, :] = scaled
                w[i, k, at, :] = scaled + scaled
    for i in range(2):
        for k in range(2):
            w[i, k, 8 * chunks : 8 * chunks + 8, :] = zero

    def sweep(s, _):
        @pl.when(s == SWEEPS)
        def _():
            for t in range(chunks):
                at = pl.ds(8 * t, 8)
                for i, source in ((0, fm), (1, fs)):
                    for k in range(2):
                        now = w[i, k, at, :]
                        if i == 0 and 0 < t < chunks - 1:
                            v[k, 8 * t - HALO : 8 * t - HALO + 8, :] = now
                        scaled = coef[i, 2, at, :] * (now - source[4 + k, at, :])
                        hb[i, k, at, :] = scaled
                        w[i, k, at, :] = scaled + scaled

        kept = [(zero, zero), (zero, zero)]
        for t in range(chunks):
            at, after = pl.ds(8 * t, 8), pl.ds(8 * t + 1, 8)
            now, dx, dy = [], [], []
            for k in range(2):
                here = (w[0, k, at, :], w[1, k, at, :])
                ahead = (w[0, k, after, :], w[1, k, after, :])
                e = both(lambda a, b: a - b, ahead, here)
                f = both(lambda a, b: a + b, ahead, here)
                now.append(here)
                dx.append(both(lambda a, b: a + b, e, plus(e)))
                dy.append(both(lambda a, b: a - b, plus(f), f))
            m = (coef[0, 0, at, :], coef[1, 0, at, :])
            q = (coef[0, 1, at, :], coef[1, 1, at, :])
            s_xy = both(lambda a, b: a + b, dx[0], dy[1])
            one = both(lambda a, b, c: a * (b + c), m, s_xy, dx[0])
            two = both(lambda a, b, c: a * (b + c), m, s_xy, dy[1])
            shear = both(lambda a, b, c: a * (b + c), q, dy[0], dx[1])
            one_m, two_m, shear_m = minus(one), minus(two), minus(shear)
            s_one = both(lambda a, b: a + b, one, one_m)
            d_two = both(lambda a, b: a - b, two_m, two)
            s_shear = both(lambda a, b: a + b, shear, shear_m)
            d_shear = both(lambda a, b: a - b, shear_m, shear)
            before = (
                both(lambda a, b: a + b, s_one, d_shear),
                both(lambda a, b: a + b, d_two, s_shear),
            )
            behind = (
                both(lambda a, b: a - b, d_shear, s_one),
                both(lambda a, b: a - b, d_two, s_shear),
            )
            for k in range(2):
                moved, kept[k] = down(before[k], kept[k])
                for i in range(2):
                    image = moved[i] + behind[k][i]
                    w[i, k, at, :] = (
                        coef[i, 3, at, :] * now[k][i] + hb[i, k, at, :]
                    ) - coef[i, 2, at, :] * image
        return 0

    lax.fori_loop(0, 2 * SWEEPS, sweep, 0)

    vel_copy = pltpu.make_async_copy(v, vel, out_sem.at[0])
    vel_copy.start()

    for t in range(TILE // 8):
        total = None
        for start in range(0, rows, TILE):
            at = pl.ds(start + 8 * t, 8)
            ext = pl.ds(HALO + start + 8 * t, 8)
            piece = fm[1, ext, :] * (
                w[0, 0, ext, :] * v[0, at, :] + w[0, 1, ext, :] * v[1, at, :]
            )
            total = piece if total is None else total + piece
        dens[8 * t : 8 * t + 8, :] = -total

    for copy in loads[5:]:
        copy.wait()
    per = MODES // n_col
    half_row = jnp.dot(
        b1[...], dens[...], precision=HIGHEST, preferred_element_type=jnp.float32
    )
    half_row = jnp.concatenate(
        [half_row[s * n_col : (s + 1) * n_col] for s in range(per)], axis=1
    )
    part = jnp.dot(
        half_row, b2[...], precision=HIGHEST, preferred_element_type=jnp.float32
    )
    group = tb[0, 0] - 2 * line
    wide = lax.broadcasted_iota(jnp.int32, (n_col, LANES), 1)
    part = jnp.where((wide >= 64) == (group > 0), part, 0.0)
    for i in range(n_col):
        send_a[i] = part[i : i + 1, :]

    def spread(phase, src, dst, count, to):
        def start(i, _):
            line_to, col_to, index = to(i)
            pltpu.make_async_remote_copy(
                src_ref=src(index),
                dst_ref=dst,
                send_sem=phase_send.at[phase],
                recv_sem=phase_recv.at[phase],
                device_id=device(line_to, col_to),
                device_id_type=MESH,
            ).start()
            return 0

        lax.fori_loop(1, count, start, 0)

    def arrived(phase, ref):
        pltpu.make_async_copy(ref, ref, phase_recv.at[phase]).wait()

    def departed(phase, ref):
        pltpu.make_async_copy(ref, ref, phase_send.at[phase]).wait()

    spread(
        0,
        lambda i: send_a.at[i],
        recv_a.at[col],
        n_col,
        lambda i: (line, col_by(i), col_by(i)),
    )
    recv_a[col] = send_a[col]
    arrived(0, recv_a.at[0 : n_col - 1])
    total = recv_a[0]
    for i in range(1, n_col):
        total = total + recv_a[i]

    table[line] = total
    spread(
        1,
        lambda i: table.at[line],
        table.at[line],
        n_line,
        lambda i: (line_by(i), col, i),
    )
    arrived(1, table.at[0 : n_line - 1])

    per_owner = ol.shape[0] // n_own
    left_half = lax.broadcasted_iota(jnp.int32, (1, LANES), 1) < 64
    for k in range(per_owner // 2):
        found = []
        for j in range(2):
            block = ol[own_at * per_owner + k + j * (per_owner // 2)]
            entry = table[lax.shift_right_logical(block, 1)]
            turn = lax.bitwise_and(block, 1) != j
            found.append(jnp.where(turn, pltpu.roll(entry, 64, 1), entry))
        recv_c[col, k : k + 1, :] = jnp.where(left_half, found[0], found[1])

    spread(
        2,
        lambda i: recv_c.at[col],
        recv_c.at[col],
        n_col,
        lambda i: (line, col_by(i), i),
    )
    arrived(2, recv_c.at[0 : n_col - 1])
    for z in range(n_col // 2):
        at = pl.ds(z * LANES, LANES)
        a, b = recv_c[2 * z], recv_c[2 * z + 1]
        out[0:8, at] = jnp.where(lane < 64, a, pltpu.roll(b, 64, 1))
        out[8:16, at] = jnp.where(lane < 64, pltpu.roll(a, 64, 1), b)
    grad_copy = pltpu.make_async_copy(out, grad.at[0], out_sem.at[1])
    grad_copy.start()

    for copy in copies:
        copy.wait_send()
    departed(0, recv_a.at[0 : n_col - 1])
    departed(1, table.at[0 : n_line - 1])
    departed(2, recv_c.at[0 : n_col - 1])
    vel_copy.wait()
    grad_copy.wait()


def solution(mesh):
    sizes = tuple(mesh.shape[a] for a in ("row", "own", "col"))
    n_line, n_col = sizes[0] * sizes[1], sizes[2]

    def local(viscosity, friction, driving, observed, ice_mask, tile_block, owner_list):
        rows = viscosity.shape[0]
        ext = rows + 2 * HALO
        first, second = bases(n_col)
        per_owner = owner_list.shape[0] // sizes[1]
        f32 = jnp.float32
        vmem = pltpu.VMEM
        return pl.pallas_call(
            functools.partial(kernel, sizes),
            out_shape=(
                jax.ShapeDtypeStruct((2, rows, LANES), f32),
                jax.ShapeDtypeStruct((1, per_owner, MODES * MODES), f32),
            ),
            in_specs=[pl.BlockSpec(memory_space=pltpu.HBM)] * 9,
            out_specs=[pl.BlockSpec(memory_space=pl.ANY)] * 2,
            scratch_shapes=[
                vmem((6, ext, LANES), f32),
                vmem((ext, LANES), jnp.int32),
                vmem((FIELDS, ext, LANES), f32),
                vmem((rows, LANES), f32),
                vmem((8, 16, rows), f32),
                vmem((8, 16, rows), f32),
                vmem((4, 8, LANES), f32),
                vmem((2, 4, ext, LANES), f32),
                vmem((2, 2, ext, LANES), f32),
                vmem((2, 2, ext + 8, LANES), f32),
                vmem((2, rows, LANES), f32),
                vmem((TILE, LANES), f32),
                vmem(first.shape, f32),
                vmem(second.shape, f32),
                pltpu.SMEM(tile_block.shape, jnp.int32),
                pltpu.SMEM(owner_list.shape, jnp.int32),
                vmem((n_col, 1, LANES), f32),
                vmem((n_col, 1, LANES), f32),
                vmem((n_line, 1, LANES), f32),
                vmem((n_col, 8, LANES), f32),
                vmem((per_owner, MODES * MODES), f32),
                pltpu.SemaphoreType.DMA((9,)),
                pltpu.SemaphoreType.DMA((16,)),
                pltpu.SemaphoreType.DMA((16,)),
                pltpu.SemaphoreType.DMA((3,)),
                pltpu.SemaphoreType.DMA((3,)),
                pltpu.SemaphoreType.DMA((2,)),
            ],
            compiler_params=pltpu.CompilerParams(
                collective_id=0,
                has_side_effects=True,
                vmem_limit_bytes=32 * 2**20,
            ),
        )(
            viscosity,
            friction,
            driving,
            observed,
            ice_mask,
            tile_block,
            owner_list,
            jnp.asarray(first),
            jnp.asarray(second),
        )

    return jax.shard_map(
        local,
        mesh=mesh,
        in_specs=(
            P(("row", "own"), "col"),
            P(("row", "own"), "col"),
            P(None, ("row", "own"), "col"),
            P(None, ("row", "own"), "col"),
            P(("row", "own"), "col"),
            P(("row", "own"), "col"),
            P(),
        ),
        out_specs=(P(None, ("row", "own"), "col"), P("own", None, None)),
        check_vma=False,
    )
```

```python
import functools
import math

import jax
import jax.numpy as jnp
import numpy as np
from jax import lax
from jax.experimental import pallas as pl
from jax.experimental.pallas import tpu as pltpu
from jax.sharding import PartitionSpec as P

TILE = 128
MODES = 32
LANES = 128
HALO = 8
FIELDS = 7
SWEEPS = 3
PER = LANES // MODES
SHARES = 4
LAG = 3
MESH = pl.DeviceIdType.MESH
HIGHEST = lax.Precision.HIGHEST


def bases():
    places = np.arange(TILE) + 0.5
    orders = np.arange(MODES)
    cosine = np.cos(math.pi * orders[:, None] * places[None, :] / TILE)
    first = np.concatenate([cosine[s::PER] for s in range(PER)], axis=0)
    second = np.zeros((PER * TILE, LANES))
    for s in range(PER):
        second[s * TILE : (s + 1) * TILE, s * MODES : (s + 1) * MODES] = cosine.T / TILE
    return first.astype(np.float32), second.astype(np.float32)


def around(step, size):
    return min(step % size, -step % size)


def pipeline(count, lag, *stages):
    held = {}
    for step in range(count + lag * (len(stages) - 1)):
        for i, stage in reversed(list(enumerate(stages))):
            t = step - i * lag
            if 0 <= t < count:
                held[t] = stage(t, held.pop(t, None))


def kernel(
    sizes,
    visc,
    fric,
    drv,
    obs,
    mask,
    tile_block,
    owner_list,
    basis_1,
    basis_2,
    v,
    grad,
    fm,
    mk,
    fs,
    pack,
    pack_t,
    recv_t,
    diag,
    coef,
    hb,
    w,
    w2,
    dens,
    b1,
    b2,
    tb,
    ol,
    send_a,
    recv_a,
    table,
    load_sem,
    halo_send,
    halo_recv,
    phase_send,
    phase_recv,
):
    n_row, n_own, n_col = sizes
    n_line = n_row * n_own
    rows = visc.shape[0]
    chunks = (rows + 2 * HALO) // 8
    row_at, own_at, col = (
        lax.axis_index("row"),
        lax.axis_index("own"),
        lax.axis_index("col"),
    )
    line = row_at * n_own + own_at

    def by(rows_on, owns_on, cols_on):
        return {
            "row": lax.rem(row_at + (rows_on + n_row), n_row),
            "own": lax.rem(own_at + (owns_on + n_own), n_own),
            "col": lax.rem(col + (cols_on + n_col), n_col),
        }

    def next_to(line_on, cols_on):
        to = lax.rem(line + (line_on + n_line), n_line)
        return {
            "row": lax.div(to, n_own),
            "own": lax.rem(to, n_own),
            "col": lax.rem(col + (cols_on + n_col), n_col),
        }

    col_steps = sorted(range(1, n_col), key=lambda i: -around(i, n_col))
    plane_steps = [(i, j) for i in range(n_row) for j in range(n_own) if i or j]
    plane_steps.sort(key=lambda s: -(around(s[0], n_row) + around(s[1], n_own)))

    own_rows = pl.ds(HALO, rows)
    loads = [
        (visc, fm.at[0, own_rows, :]),
        (fric, fm.at[1, own_rows, :]),
        (drv, fm.at[2:4, own_rows, :]),
        (obs, fm.at[4:6, own_rows, :]),
        (mask, mk.at[own_rows, :]),
        (basis_1, b1),
        (basis_2, b2),
        (tile_block, tb),
        (owner_list, ol),
    ]
    loads = [
        pltpu.make_async_copy(src, dst, load_sem.at[i])
        for i, (src, dst) in enumerate(loads)
    ]
    for copy in loads:
        copy.start()

    barrier = pltpu.get_barrier_semaphore()
    greeted = [next_to(i, j) for i in (-1, 1) for j in (-1, 1)]
    greeted += [by(0, 0, i) for i in reversed(col_steps)]
    greeted += [by(i, j, 0) for i, j in reversed(plane_steps)]
    for to in greeted:
        pl.semaphore_signal(barrier, inc=1, device_id=to, device_id_type=MESH)

    lane = lax.broadcasted_iota(jnp.int32, (8, LANES), 1)
    sub = lax.broadcasted_iota(jnp.int32, (8, LANES), 0)
    last_lane, first_lane, first_sub = lane == LANES - 1, lane == 0, sub == 0

    for copy in loads[:5]:
        copy.wait()

    def gather(t, _):
        at = pl.ds(HALO + 8 * t, 8)
        found = [fm[f, at, :] for f in range(6)] + [mk[at, :].astype(jnp.float32)]
        return [pltpu.roll(piece, 16 * f + 8, 1) for f, piece in enumerate(found)]

    def merge(t, pieces):
        packed = pieces[0]
        for f in range(1, FIELDS):
            packed = jnp.where(lane < 16 * f, packed, pieces[f])
        pack[8 * t : 8 * t + 8, :] = packed

    pipeline(rows // 8, 4, gather, merge)
    for part in range(rows // LANES):
        block = pack[part * LANES : (part + 1) * LANES, :]
        pack_t[:, :, part * LANES : (part + 1) * LANES] = block.T.reshape(8, 16, LANES)
    recv_t[FIELDS, :, :] = jnp.zeros((16, rows), jnp.float32)

    pl.semaphore_wait(barrier, len(greeted))
    copies = []

    def send(src, dst, to):
        at = len(copies)
        copy = pltpu.make_async_remote_copy(
            src_ref=src,
            dst_ref=dst,
            send_sem=halo_send.at[at],
            recv_sem=halo_recv.at[at],
            device_id=to,
            device_id_type=MESH,
        )
        copy.start()
        copies.append(copy)

    for line_on, source, slot in ((-1, 0, 2), (1, rows - 8, 0)):
        for cols_on in (-1, 1):
            send(
                pack.at[pl.ds(source, 8), :],
                diag.at[slot + (1 if cols_on < 0 else 0)],
                next_to(line_on, cols_on),
            )
    send(
        pack_t.at[0:FIELDS, 0:8, :], recv_t.at[0:FIELDS, 0:8, :], by(0, 0, 1)
    )
    send(
        pack_t.at[0:FIELDS, 8:16, :], recv_t.at[0:FIELDS, 8:16, :], by(0, 0, -1)
    )
    for line_on, source, target in ((-1, HALO, HALO + rows), (1, rows, 0)):
        to, take = pl.ds(target, HALO), pl.ds(source, HALO)
        send(fm.at[:, take, :], fm.at[:, to, :], next_to(line_on, 0))
        send(mk.at[take, :], mk.at[to, :], next_to(line_on, 0))

    for copy in copies:
        copy.wait_recv()

    def unpack(at, packed):
        for f in range(FIELDS):
            fs[f, at, :] = pltpu.roll(packed, LANES - (16 * f + 8), 1)

    from_left = lax.rem(lane, 16) < 8
    unpack(pl.ds(0, 8), jnp.where(from_left, diag[0], diag[1]))
    unpack(pl.ds(HALO + rows, 8), jnp.where(from_left, diag[2], diag[3]))
    for part in range(rows // LANES):
        turned = (
            recv_t[:, :, part * LANES : (part + 1) * LANES].reshape(LANES, LANES).T
        )
        for t in range(LANES // 8):
            unpack(
                pl.ds(HALO + part * LANES + 8 * t, 8), turned[8 * t : 8 * t + 8, :]
            )

    def both(fn, *args):
        return tuple(fn(*parts) for parts in zip(*args))

    def down(x, kept):
        turned = tuple(pltpu.roll(part, 1, 0) for part in x)
        moved = both(lambda k, r: jnp.where(first_sub, k, r), kept, turned)
        return moved, turned

    side_inside = ((lane < 64) & (col < n_col - 1)) | ((lane >= 64) & (col > 0))
    zero = jnp.zeros((8, LANES), jnp.float32)
    add = functools.partial(both, lambda x, y: x + y)
    sub_ = functools.partial(both, lambda x, y: x - y)

    def rolls(x, by_lanes):
        return tuple(pltpu.roll(part, by_lanes, 1) for part in x)

    def from_next(x):
        return jnp.where(last_lane, x[1], x[0]), jnp.where(last_lane, x[0], x[1])

    def from_last(x):
        return jnp.where(first_lane, x[1], x[0]), jnp.where(first_lane, x[0], x[1])

    def store_state(to, t, k, now):
        for i in range(2):
            to[i, k, 8 * t : 8 * t + 8, :] = now[i]
        return rolls(now, LANES - 1)

    def store_ahead(to, t, k, turned):
        ahead = from_next(turned)
        for i in range(2):
            to[i, 2 + k, 8 * t : 8 * t + 8, :] = ahead[i]

    def store_both_ahead(to):
        def stage(t, turned):
            for k in range(2):
                store_ahead(to, t, k, turned[k])

        return stage

    def open_(t, _):
        at = pl.ds(8 * t, 8)
        n = (fm[0, at, :], fs[0, at, :])
        inside = (None, side_inside)
        if t == 0 or t == chunks - 1:
            there = line > 0 if t == 0 else line < n_line - 1
            inside = (jnp.broadcast_to(there, (8, LANES)), side_inside & there)
            n = (jnp.where(inside[0], n[0], 0.0), n[1])
        n = (n[0], jnp.where(inside[1], n[1], 0.0))
        return n, inside, rolls(n, 1)

    summed_kept = [(zero, zero)]

    def settle(t, given):
        n, inside, turned = given
        at = pl.ds(8 * t, 8)
        ice = (mk[at, :] > 0, (fs[6, at, :] > 0.5) & inside[1])
        if inside[0] is not None:
            ice = (ice[0] & inside[0], ice[1])
        summed = add(n, from_last(turned))
        moved, summed_kept[0] = down(summed, summed_kept[0])
        states = []
        for i, source in ((0, fm), (1, fs)):
            f = source[1, at, :]
            half = jnp.where(
                ice[i], 0.5 / (1.25 * (summed[i] + moved[i]) + f), 0.0
            )
            coef[i, 0, at, :] = 0.5 * n[i]
            coef[i, 1, at, :] = 0.25 * n[i]
            coef[i, 2, at, :] = half
            coef[i, 3, at, :] = 1.0 - half * f
            scaled = [half * source[2 + k, at, :] for k in range(2)]
            for k in range(2):
                hb[i, k, at, :] = scaled[k]
            states.append([part + part for part in scaled])
        return [store_state(w, t, k, (states[0][k], states[1][k])) for k in range(2)]

    pipeline(chunks, LAG, open_, settle, store_both_ahead(w))
    for i in range(2):
        for k in range(4):
            w[i, k, 8 * chunks : 8 * chunks + 8, :] = zero
            w2[i, k, 8 * chunks : 8 * chunks + 8, :] = zero

    def turn():
        def begin(t, _):
            at = pl.ds(8 * t, 8)
            states = []
            for k in range(2):
                state = []
                for i, source in ((0, fm), (1, fs)):
                    now = w2[i, k, at, :]
                    if i == 0 and 0 < t < chunks - 1:
                        v[k, 8 * t - HALO : 8 * t - HALO + 8, :] = now
                    scaled = coef[i, 2, at, :] * (now - source[4 + k, at, :])
                    hb[i, k, at, :] = scaled
                    state.append(scaled + scaled)
                states.append(store_state(w2, t, k, tuple(state)))
            return states

        pipeline(chunks, LAG, begin, store_both_ahead(w2))

    def sweep(w_from, w_to):
        kept = [(zero, zero)] * 4

        def pull(ref, k, at):
            return ref[0, k, at, :], ref[1, k, at, :]

        def front(t, _):
            at, after = pl.ds(8 * t, 8), pl.ds(8 * t + 1, 8)
            dx, dy = [], []
            for k in range(2):
                here, here_next = pull(w_from, k, at), pull(w_from, 2 + k, at)
                below, below_next = pull(w_from, k, after), pull(w_from, 2 + k, after)
                dx.append(add(sub_(below, here), sub_(below_next, here_next)))
                dy.append(sub_(add(here_next, below_next), add(here, below)))
            m, q = pull(coef, 0, at), pull(coef, 1, at)
            total = add(dx[0], dy[1])
            product = functools.partial(both, lambda a, b: a * b)
            one = product(m, add(total, dx[0]))
            two = product(m, add(total, dy[1]))
            shear = product(q, add(dy[0], dx[1]))
            fields = (
                add(one, shear),
                sub_(one, shear),
                add(two, shear),
                sub_(shear, two),
            )
            moved = []
            for i in range(4):
                got, kept[i] = down(fields[i], kept[i])
                moved.append(got)
            stay = (sub_(moved[1], fields[0]), sub_(moved[3], fields[2]))
            go = (sub_(moved[0], fields[1]), sub_(moved[2], fields[3]))
            return stay, tuple(rolls(x, 1) for x in go)

        def close(t, given):
            at = pl.ds(8 * t, 8)
            turned = []
            for k in range(2):
                image = add(given[0][k], from_last(given[1][k]))
                now = tuple(
                    (coef[i, 3, at, :] * w_from[i, k, at, :] + hb[i, k, at, :])
                    - coef[i, 2, at, :] * image[i]
                    for i in range(2)
                )
                turned.append(store_state(w_to, t, k, now))
            return turned

        pipeline(chunks, LAG, front, close, store_both_ahead(w_to))

    def pair(s, _):
        sweep(w, w2)

        @pl.when(s == 1)
        def _():
            turn()

        sweep(w2, w)
        return 0

    lax.fori_loop(0, SWEEPS, pair, 0)

    for t in range(TILE // 8):
        total = None
        for start in range(0, rows, TILE):
            at = pl.ds(start + 8 * t, 8)
            ext = pl.ds(HALO + start + 8 * t, 8)
            piece = fm[1, ext, :] * (
                w[0, 0, ext, :] * v[0, at, :] + w[0, 1, ext, :] * v[1, at, :]
            )
            total = piece if total is None else total + piece
        dens[8 * t : 8 * t + 8, :] = -total

    for copy in loads[5:]:
        copy.wait()
    first = jnp.dot(
        b1[...], dens[...], precision=HIGHEST, preferred_element_type=jnp.float32
    )
    first = jnp.concatenate([first[8 * i : 8 * i + 8] for i in range(PER)], axis=1)
    part = jnp.dot(
        first, b2[...], precision=HIGHEST, preferred_element_type=jnp.float32
    )
    in_second = tb[0, 0] > 2 * line
    parts = jnp.where(in_second, 0.0, part), jnp.where(in_second, part, 0.0)
    per_share = 8 // SHARES
    for i in range(SHARES):
        for j in range(2):
            at = pl.ds(j * per_share, per_share)
            send_a[i, at, :] = parts[j][i * per_share : (i + 1) * per_share, :]

    def start(phase, src, dst, to):
        pltpu.make_async_remote_copy(
            src_ref=src,
            dst_ref=dst,
            send_sem=phase_send.at[phase],
            recv_sem=phase_recv.at[phase],
            device_id=to,
            device_id_type=MESH,
        ).start()

    def arrived(phase, ref):
        pltpu.make_async_copy(ref, ref, phase_recv.at[phase]).wait()

    def departed(phase, ref):
        pltpu.make_async_copy(ref, ref, phase_send.at[phase]).wait()

    share = lax.rem(col, SHARES)
    for i in col_steps:
        to = by(0, 0, i)
        start(0, send_a.at[lax.rem(to["col"], SHARES)], recv_a.at[col], to)
    recv_a[col] = send_a[share]
    arrived(0, recv_a.at[0 : n_col - 1])
    total = recv_a[0]
    for i in range(1, n_col):
        total = total + recv_a[i]

    mine = table.at[pl.ds(2 * line, 2)]
    for j in range(2):
        table[2 * line + j] = total[j * per_share : (j + 1) * per_share, :]
    for i, j in plane_steps:
        start(1, mine, mine, by(i, j, 0))
    arrived(1, table.at[0 : 2 * n_line - 2])

    per_owner = ol.shape[0] // n_own
    width = per_share * LANES
    for k in range(per_owner):
        entry = table[ol[own_at * per_owner + k]]
        for j in range(per_share):
            at = pl.ds(pl.multiple_of(share * width + j * LANES, LANES), LANES)
            grad[0, k : k + 1, at] = entry[j : j + 1, :]

    mine_c = grad.at[0, :, pl.ds(pl.multiple_of(share * width, LANES), width)]
    for i in range(1, SHARES):
        to = {"row": row_at, "own": own_at, "col": lax.bitwise_xor(col, i)}
        start(2, mine_c, mine_c, to)
    arrived(2, grad.at[0, :, 0 : (SHARES - 1) * width])

    for copy in copies:
        copy.wait_send()
    departed(0, recv_a.at[0 : n_col - 1])
    departed(1, table.at[0 : 2 * n_line - 2])
    departed(2, grad.at[0, :, 0 : (SHARES - 1) * width])


def solution(mesh):
    sizes = tuple(mesh.shape[a] for a in ("row", "own", "col"))
    n_line, n_col = sizes[0] * sizes[1], sizes[2]

    def local(viscosity, friction, driving, observed, ice_mask, tile_block, owner_list):
        rows = viscosity.shape[0]
        ext = rows + 2 * HALO
        first, second = bases()
        per_owner = owner_list.shape[0] // sizes[1]
        f32 = jnp.float32
        vmem = pltpu.VMEM
        tile_block = tile_block.reshape(1, -1)
        operands = (
            viscosity,
            friction,
            driving,
            observed,
            ice_mask,
            tile_block,
            owner_list,
            jnp.asarray(first),
            jnp.asarray(second),
        )
        return pl.pallas_call(
            functools.partial(kernel, sizes),
            out_shape=(
                jax.ShapeDtypeStruct((2, rows, LANES), f32),
                jax.ShapeDtypeStruct((1, per_owner, MODES * MODES), f32),
            ),
            in_specs=[pl.BlockSpec(memory_space=pltpu.HBM)] * 9,
            out_specs=[pl.BlockSpec(memory_space=pltpu.VMEM)] * 2,
            scratch_shapes=[
                vmem((6, ext, LANES), f32),
                vmem((ext, LANES), jnp.int32),
                vmem((FIELDS, ext, LANES), f32),
                vmem((rows, LANES), f32),
                vmem((8, 16, rows), f32),
                vmem((8, 16, rows), f32),
                vmem((4, 8, LANES), f32),
                vmem((2, 4, ext, LANES), f32),
                vmem((2, 2, ext, LANES), f32),
                vmem((2, 4, ext + 8, LANES), f32),
                vmem((2, 4, ext + 8, LANES), f32),
                vmem((TILE, LANES), f32),
                vmem(first.shape, f32),
                vmem(second.shape, f32),
                pltpu.SMEM(tile_block.shape, jnp.int32),
                pltpu.SMEM(owner_list.shape, jnp.int32),
                vmem((SHARES, 2 * 8 // SHARES, LANES), f32),
                vmem((n_col, 2 * 8 // SHARES, LANES), f32),
                vmem((2 * n_line, 8 // SHARES, LANES), f32),
                pltpu.SemaphoreType.DMA((9,)),
                pltpu.SemaphoreType.DMA((10,)),
                pltpu.SemaphoreType.DMA((10,)),
                pltpu.SemaphoreType.DMA((3,)),
                pltpu.SemaphoreType.DMA((3,)),
            ],
            compiler_params=pltpu.CompilerParams(
                collective_id=0,
                has_side_effects=True,
                vmem_limit_bytes=32 * 2**20,
            ),
        )(*(pltpu.with_memory_space_constraint(x, pltpu.HBM) for x in operands))

    return jax.shard_map(
        local,
        mesh=mesh,
        in_specs=(
            P(("row", "own"), "col"),
            P(("row", "own"), "col"),
            P(None, ("row", "own"), "col"),
            P(None, ("row", "own"), "col"),
            P(("row", "own"), "col"),
            P(("row", "own"), "col"),
            P(),
        ),
        out_specs=(P(None, ("row", "own"), "col"), P("own", None, None)),
        check_vma=False,
    )
```

```python
import functools
import math

import jax
import jax.numpy as jnp
import numpy as np
from jax import lax
from jax.experimental import pallas as pl
from jax.experimental.pallas import tpu as pltpu
from jax.sharding import PartitionSpec as P

TILE = 128
MODES = 32
LANES = 128
HALO = 8
FIELDS = 7
SWEEPS = 3
PER = LANES // MODES
SHARES = 4
LAG = 8
MESH = pl.DeviceIdType.MESH
HIGHEST = lax.Precision.HIGHEST


def bases():
    places = np.arange(TILE) + 0.5
    orders = np.arange(MODES)
    cosine = np.cos(math.pi * orders[:, None] * places[None, :] / TILE)
    first = np.concatenate([cosine[s::PER] for s in range(PER)], axis=0)
    second = np.zeros((PER * TILE, LANES))
    for s in range(PER):
        second[s * TILE : (s + 1) * TILE, s * MODES : (s + 1) * MODES] = cosine.T / TILE
    return first.astype(np.float32), second.astype(np.float32)


def around(step, size):
    return min(step % size, -step % size)


def pipeline(count, lag, *stages):
    held = {}
    for step in range(count + lag * (len(stages) - 1)):
        for i, stage in reversed(list(enumerate(stages))):
            t = step - i * lag
            if 0 <= t < count:
                held[t] = stage(t, held.pop(t, None))


def exchange(
    sizes,
    visc,
    fric,
    drv,
    obs,
    mask,
    fm,
    mk,
    recv_t,
    diag,
    pack,
    pack_t,
    load_sem,
    halo_send,
    halo_recv,
):
    n_row, n_own, n_col = sizes
    n_line = n_row * n_own
    rows = visc.shape[0]
    row_at, own_at, col = (
        lax.axis_index("row"),
        lax.axis_index("own"),
        lax.axis_index("col"),
    )
    line = row_at * n_own + own_at

    def by(rows_on, owns_on, cols_on):
        return {
            "row": lax.rem(row_at + (rows_on + n_row), n_row),
            "own": lax.rem(own_at + (owns_on + n_own), n_own),
            "col": lax.rem(col + (cols_on + n_col), n_col),
        }

    def next_to(line_on, cols_on):
        to = lax.rem(line + (line_on + n_line), n_line)
        return {
            "row": lax.div(to, n_own),
            "own": lax.rem(to, n_own),
            "col": lax.rem(col + (cols_on + n_col), n_col),
        }

    own_rows = pl.ds(HALO, rows)
    loads = [
        (visc, fm.at[0, own_rows, :]),
        (fric, fm.at[1, own_rows, :]),
        (drv, fm.at[2:4, own_rows, :]),
        (obs, fm.at[4:6, own_rows, :]),
        (mask, mk.at[own_rows, :]),
    ]
    loads = [
        pltpu.make_async_copy(src, dst, load_sem.at[i])
        for i, (src, dst) in enumerate(loads)
    ]
    for copy in loads:
        copy.start()

    barrier = pltpu.get_barrier_semaphore()
    greeted = [next_to(i, j) for i in (-1, 1) for j in (-1, 0, 1)]
    greeted += [by(0, 0, i) for i in (-1, 1)]
    for to in greeted:
        pl.semaphore_signal(barrier, inc=1, device_id=to, device_id_type=MESH)

    lane = lax.broadcasted_iota(jnp.int32, (8, LANES), 1)

    for copy in loads:
        copy.wait()

    def gather(t, _):
        at = pl.ds(HALO + 8 * t, 8)
        found = [fm[f, at, :] for f in range(6)] + [mk[at, :].astype(jnp.float32)]
        return [pltpu.roll(piece, 16 * f + 8, 1) for f, piece in enumerate(found)]

    def merge(t, pieces):
        packed = pieces[0]
        for f in range(1, FIELDS):
            packed = jnp.where(lane < 16 * f, packed, pieces[f])
        pack[8 * t : 8 * t + 8, :] = packed

    pipeline(rows // 8, 4, gather, merge)
    for part in range(rows // LANES):
        block = pack[part * LANES : (part + 1) * LANES, :]
        pack_t[:, :, part * LANES : (part + 1) * LANES] = block.T.reshape(8, 16, LANES)
    recv_t[FIELDS, :, :] = jnp.zeros((16, rows), jnp.float32)

    pl.semaphore_wait(barrier, len(greeted))
    copies = []

    def send(src, dst, to):
        at = len(copies)
        copy = pltpu.make_async_remote_copy(
            src_ref=src,
            dst_ref=dst,
            send_sem=halo_send.at[at],
            recv_sem=halo_recv.at[at],
            device_id=to,
            device_id_type=MESH,
        )
        copy.start()
        copies.append(copy)

    for line_on, source, slot in ((-1, 0, 2), (1, rows - 8, 0)):
        for cols_on in (-1, 1):
            send(
                pack.at[pl.ds(source, 8), :],
                diag.at[slot + (1 if cols_on < 0 else 0)],
                next_to(line_on, cols_on),
            )
    send(
        pack_t.at[0:FIELDS, 0:8, :], recv_t.at[0:FIELDS, 0:8, :], by(0, 0, 1)
    )
    send(
        pack_t.at[0:FIELDS, 8:16, :], recv_t.at[0:FIELDS, 8:16, :], by(0, 0, -1)
    )
    for line_on, source, target in ((-1, HALO, HALO + rows), (1, rows, 0)):
        to, take = pl.ds(target, HALO), pl.ds(source, HALO)
        send(fm.at[:, take, :], fm.at[:, to, :], next_to(line_on, 0))
        send(mk.at[take, :], mk.at[to, :], next_to(line_on, 0))

    for copy in copies:
        copy.wait()


def kernel(
    sizes,
    fm,
    mk,
    recv_t,
    diag,
    tile_block,
    owner_list,
    basis_1,
    basis_2,
    v,
    grad,
    fs,
    coef,
    hb,
    w,
    w2,
    dens,
    b1,
    b2,
    tb,
    ol,
    send_a,
    recv_a,
    table,
    load_sem,
    phase_send,
    phase_recv,
):
    n_row, n_own, n_col = sizes
    n_line = n_row * n_own
    rows = fm.shape[1] - 2 * HALO
    chunks = (rows + 2 * HALO) // 8
    row_at, own_at, col = (
        lax.axis_index("row"),
        lax.axis_index("own"),
        lax.axis_index("col"),
    )
    line = row_at * n_own + own_at

    def by(rows_on, owns_on, cols_on):
        return {
            "row": lax.rem(row_at + (rows_on + n_row), n_row),
            "own": lax.rem(own_at + (owns_on + n_own), n_own),
            "col": lax.rem(col + (cols_on + n_col), n_col),
        }

    col_steps = sorted(range(1, n_col), key=lambda i: -around(i, n_col))
    plane_steps = [(i, j) for i in range(n_row) for j in range(n_own) if i or j]
    plane_steps.sort(key=lambda s: -(around(s[0], n_row) + around(s[1], n_own)))

    loads = [
        (basis_1, b1),
        (basis_2, b2),
        (tile_block, tb),
        (owner_list, ol),
    ]
    loads = [
        pltpu.make_async_copy(src, dst, load_sem.at[i])
        for i, (src, dst) in enumerate(loads)
    ]
    for copy in loads:
        copy.start()

    barrier = pltpu.get_barrier_semaphore()
    greeted = [by(0, 0, i) for i in col_steps]
    greeted += [by(i, j, 0) for i, j in plane_steps]
    for to in greeted:
        pl.semaphore_signal(barrier, inc=1, device_id=to, device_id_type=MESH)

    lane = lax.broadcasted_iota(jnp.int32, (8, LANES), 1)
    sub = lax.broadcasted_iota(jnp.int32, (8, LANES), 0)
    last_lane, first_lane, first_sub = lane == LANES - 1, lane == 0, sub == 0

    def unpack(at, packed):
        for f in range(FIELDS):
            fs[f, at, :] = pltpu.roll(packed, LANES - (16 * f + 8), 1)

    from_left = lax.rem(lane, 16) < 8
    unpack(pl.ds(0, 8), jnp.where(from_left, diag[0], diag[1]))
    unpack(pl.ds(HALO + rows, 8), jnp.where(from_left, diag[2], diag[3]))
    for part in range(rows // LANES):
        turned = (
            recv_t[:, :, part * LANES : (part + 1) * LANES].reshape(LANES, LANES).T
        )
        for t in range(LANES // 8):
            unpack(
                pl.ds(HALO + part * LANES + 8 * t, 8), turned[8 * t : 8 * t + 8, :]
            )

    def both(fn, *args):
        return tuple(fn(*parts) for parts in zip(*args))

    def down(x, kept):
        turned = tuple(pltpu.roll(part, 1, 0) for part in x)
        moved = both(lambda k, r: jnp.where(first_sub, k, r), kept, turned)
        return moved, turned

    side_inside = ((lane < 64) & (col < n_col - 1)) | ((lane >= 64) & (col > 0))
    zero = jnp.zeros((8, LANES), jnp.float32)
    add = functools.partial(both, lambda x, y: x + y)
    sub_ = functools.partial(both, lambda x, y: x - y)

    def rolls(x, by_lanes):
        return tuple(pltpu.roll(part, by_lanes, 1) for part in x)

    def from_next(x):
        return jnp.where(last_lane, x[1], x[0]), jnp.where(last_lane, x[0], x[1])

    def from_last(x):
        return jnp.where(first_lane, x[1], x[0]), jnp.where(first_lane, x[0], x[1])

    def store_state(to, t, k, now):
        for i in range(2):
            to[i, k, 8 * t : 8 * t + 8, :] = now[i]
        return rolls(now, LANES - 1)

    def store_ahead(to, t, k, turned):
        ahead = from_next(turned)
        for i in range(2):
            to[i, 2 + k, 8 * t : 8 * t + 8, :] = ahead[i]

    def store_both_ahead(to):
        def stage(t, turned):
            for k in range(2):
                store_ahead(to, t, k, turned[k])

        return stage

    def open_(t, _):
        at = pl.ds(8 * t, 8)
        n = (fm[0, at, :], fs[0, at, :])
        inside = (None, side_inside)
        if t == 0 or t == chunks - 1:
            there = line > 0 if t == 0 else line < n_line - 1
            inside = (jnp.broadcast_to(there, (8, LANES)), side_inside & there)
            n = (jnp.where(inside[0], n[0], 0.0), n[1])
        n = (n[0], jnp.where(inside[1], n[1], 0.0))
        return n, inside, rolls(n, 1)

    summed_kept = [(zero, zero)]

    def settle(t, given):
        n, inside, turned = given
        at = pl.ds(8 * t, 8)
        ice = (mk[at, :] > 0, (fs[6, at, :] > 0.5) & inside[1])
        if inside[0] is not None:
            ice = (ice[0] & inside[0], ice[1])
        summed = add(n, from_last(turned))
        moved, summed_kept[0] = down(summed, summed_kept[0])
        states = []
        for i, source in ((0, fm), (1, fs)):
            f = source[1, at, :]
            half = jnp.where(
                ice[i], 0.5 / (1.25 * (summed[i] + moved[i]) + f), 0.0
            )
            coef[i, 0, at, :] = 0.5 * n[i]
            coef[i, 1, at, :] = 0.25 * n[i]
            coef[i, 2, at, :] = half
            coef[i, 3, at, :] = 1.0 - half * f
            scaled = [half * source[2 + k, at, :] for k in range(2)]
            for k in range(2):
                hb[i, k, at, :] = scaled[k]
            states.append([part + part for part in scaled])
        return [store_state(w, t, k, (states[0][k], states[1][k])) for k in range(2)]

    pipeline(chunks, LAG, open_, settle, store_both_ahead(w))
    for i in range(2):
        for k in range(4):
            w[i, k, 8 * chunks : 8 * chunks + 8, :] = zero
            w2[i, k, 8 * chunks : 8 * chunks + 8, :] = zero

    def turn():
        def begin(t, _):
            at = pl.ds(8 * t, 8)
            states = []
            for k in range(2):
                state = []
                for i, source in ((0, fm), (1, fs)):
                    now = w2[i, k, at, :]
                    if i == 0 and 0 < t < chunks - 1:
                        v[k, 8 * t - HALO : 8 * t - HALO + 8, :] = now
                    scaled = coef[i, 2, at, :] * (now - source[4 + k, at, :])
                    hb[i, k, at, :] = scaled
                    state.append(scaled + scaled)
                states.append(store_state(w2, t, k, tuple(state)))
            return states

        pipeline(chunks, LAG, begin, store_both_ahead(w2))

    def sweep(w_from, w_to):
        kept = [(zero, zero)] * 4

        def pull(ref, k, at):
            return ref[0, k, at, :], ref[1, k, at, :]

        def front(t, _):
            at, after = pl.ds(8 * t, 8), pl.ds(8 * t + 1, 8)
            dx, dy = [], []
            for k in range(2):
                here, here_next = pull(w_from, k, at), pull(w_from, 2 + k, at)
                below, below_next = pull(w_from, k, after), pull(w_from, 2 + k, after)
                dx.append(add(sub_(below, here), sub_(below_next, here_next)))
                dy.append(sub_(add(here_next, below_next), add(here, below)))
            m, q = pull(coef, 0, at), pull(coef, 1, at)
            total = add(dx[0], dy[1])
            product = functools.partial(both, lambda a, b: a * b)
            one = product(m, add(total, dx[0]))
            two = product(m, add(total, dy[1]))
            shear = product(q, add(dy[0], dx[1]))
            fields = (
                add(one, shear),
                sub_(one, shear),
                add(two, shear),
                sub_(shear, two),
            )
            moved = []
            for i in range(4):
                got, kept[i] = down(fields[i], kept[i])
                moved.append(got)
            stay = (sub_(moved[1], fields[0]), sub_(moved[3], fields[2]))
            go = (sub_(moved[0], fields[1]), sub_(moved[2], fields[3]))
            return stay, tuple(rolls(x, 1) for x in go)

        def close(t, given):
            at = pl.ds(8 * t, 8)
            turned = []
            for k in range(2):
                image = add(given[0][k], from_last(given[1][k]))
                now = tuple(
                    (coef[i, 3, at, :] * w_from[i, k, at, :] + hb[i, k, at, :])
                    - coef[i, 2, at, :] * image[i]
                    for i in range(2)
                )
                turned.append(store_state(w_to, t, k, now))
            return turned

        pipeline(chunks, LAG, front, close, store_both_ahead(w_to))

    def pair(s, _):
        sweep(w, w2)

        @pl.when(s == 1)
        def _():
            turn()

        sweep(w2, w)
        return 0

    lax.fori_loop(0, SWEEPS, pair, 0)

    for t in range(TILE // 8):
        total = None
        for start in range(0, rows, TILE):
            at = pl.ds(start + 8 * t, 8)
            ext = pl.ds(HALO + start + 8 * t, 8)
            piece = fm[1, ext, :] * (
                w[0, 0, ext, :] * v[0, at, :] + w[0, 1, ext, :] * v[1, at, :]
            )
            total = piece if total is None else total + piece
        dens[8 * t : 8 * t + 8, :] = -total

    for copy in loads:
        copy.wait()
    first = jnp.dot(
        b1[...], dens[...], precision=HIGHEST, preferred_element_type=jnp.float32
    )
    first = jnp.concatenate([first[8 * i : 8 * i + 8] for i in range(PER)], axis=1)
    part = jnp.dot(
        first, b2[...], precision=HIGHEST, preferred_element_type=jnp.float32
    )
    in_second = tb[0, 0] > 2 * line
    parts = jnp.where(in_second, 0.0, part), jnp.where(in_second, part, 0.0)
    per_share = 8 // SHARES
    for i in range(SHARES):
        for j in range(2):
            at = pl.ds(j * per_share, per_share)
            send_a[i, at, :] = parts[j][i * per_share : (i + 1) * per_share, :]

    def start(phase, src, dst, to):
        pltpu.make_async_remote_copy(
            src_ref=src,
            dst_ref=dst,
            send_sem=phase_send.at[phase],
            recv_sem=phase_recv.at[phase],
            device_id=to,
            device_id_type=MESH,
        ).start()

    def arrived(phase, ref):
        pltpu.make_async_copy(ref, ref, phase_recv.at[phase]).wait()

    def departed(phase, ref):
        pltpu.make_async_copy(ref, ref, phase_send.at[phase]).wait()

    pl.semaphore_wait(barrier, len(greeted))
    share = lax.rem(col, SHARES)
    for i in col_steps:
        to = by(0, 0, i)
        start(0, send_a.at[lax.rem(to["col"], SHARES)], recv_a.at[col], to)
    recv_a[col] = send_a[share]
    arrived(0, recv_a.at[0 : n_col - 1])
    total = recv_a[0]
    for i in range(1, n_col):
        total = total + recv_a[i]

    mine = table.at[pl.ds(2 * line, 2)]
    for j in range(2):
        table[2 * line + j] = total[j * per_share : (j + 1) * per_share, :]
    for i, j in plane_steps:
        start(1, mine, mine, by(i, j, 0))
    arrived(1, table.at[0 : 2 * n_line - 2])

    per_owner = ol.shape[0] // n_own
    width = per_share * LANES
    for k in range(per_owner):
        entry = table[ol[own_at * per_owner + k]]
        for j in range(per_share):
            at = pl.ds(pl.multiple_of(share * width + j * LANES, LANES), LANES)
            grad[0, k : k + 1, at] = entry[j : j + 1, :]

    mine_c = grad.at[0, :, pl.ds(pl.multiple_of(share * width, LANES), width)]
    for i in range(1, SHARES):
        to = {"row": row_at, "own": own_at, "col": lax.bitwise_xor(col, i)}
        start(2, mine_c, mine_c, to)
    arrived(2, grad.at[0, :, 0 : (SHARES - 1) * width])

    departed(0, recv_a.at[0 : n_col - 1])
    departed(1, table.at[0 : 2 * n_line - 2])
    departed(2, grad.at[0, :, 0 : (SHARES - 1) * width])


def solution(mesh):
    sizes = tuple(mesh.shape[a] for a in ("row", "own", "col"))
    n_line, n_col = sizes[0] * sizes[1], sizes[2]

    def local(viscosity, friction, driving, observed, ice_mask, tile_block, owner_list):
        rows = viscosity.shape[0]
        ext = rows + 2 * HALO
        first, second = bases()
        per_owner = owner_list.shape[0] // sizes[1]
        f32 = jnp.float32
        vmem = pltpu.VMEM
        fields = (viscosity, friction, driving, observed, ice_mask)
        tile_block = tile_block.reshape(1, -1)
        small = (tile_block, owner_list, jnp.asarray(first), jnp.asarray(second))
        hbm = pl.BlockSpec(memory_space=pltpu.HBM)
        here = pl.BlockSpec(memory_space=pltpu.VMEM)
        dma = pltpu.SemaphoreType.DMA

        def pinned(operands):
            return [pltpu.with_memory_space_constraint(x, pltpu.HBM) for x in operands]

        padded = pl.pallas_call(
            functools.partial(exchange, sizes),
            out_shape=(
                jax.ShapeDtypeStruct((6, ext, LANES), f32),
                jax.ShapeDtypeStruct((ext, LANES), jnp.int32),
                jax.ShapeDtypeStruct((8, 16, rows), f32),
                jax.ShapeDtypeStruct((4, 8, LANES), f32),
            ),
            in_specs=[hbm] * 5,
            out_specs=[here] * 4,
            scratch_shapes=[
                vmem((rows, LANES), f32),
                vmem((8, 16, rows), f32),
                dma((5,)),
                dma((10,)),
                dma((10,)),
            ],
            compiler_params=pltpu.CompilerParams(
                collective_id=0,
                has_side_effects=True,
                vmem_limit_bytes=16 * 2**20,
            ),
        )(*pinned(fields))
        return pl.pallas_call(
            functools.partial(kernel, sizes),
            out_shape=(
                jax.ShapeDtypeStruct((2, rows, LANES), f32),
                jax.ShapeDtypeStruct((1, per_owner, MODES * MODES), f32),
            ),
            in_specs=[here] * 4 + [hbm] * 4,
            out_specs=[here] * 2,
            scratch_shapes=[
                vmem((FIELDS, ext, LANES), f32),
                vmem((2, 4, ext, LANES), f32),
                vmem((2, 2, ext, LANES), f32),
                vmem((2, 4, ext + 8, LANES), f32),
                vmem((2, 4, ext + 8, LANES), f32),
                vmem((TILE, LANES), f32),
                vmem(first.shape, f32),
                vmem(second.shape, f32),
                pltpu.SMEM(tile_block.shape, jnp.int32),
                pltpu.SMEM(owner_list.shape, jnp.int32),
                vmem((SHARES, 2 * 8 // SHARES, LANES), f32),
                vmem((n_col, 2 * 8 // SHARES, LANES), f32),
                vmem((2 * n_line, 8 // SHARES, LANES), f32),
                dma((4,)),
                dma((3,)),
                dma((3,)),
            ],
            compiler_params=pltpu.CompilerParams(
                collective_id=1,
                has_side_effects=True,
                vmem_limit_bytes=32 * 2**20,
            ),
        )(*padded, *pinned(small))

    return jax.shard_map(
        local,
        mesh=mesh,
        in_specs=(
            P(("row", "own"), "col"),
            P(("row", "own"), "col"),
            P(None, ("row", "own"), "col"),
            P(None, ("row", "own"), "col"),
            P(("row", "own"), "col"),
            P(("row", "own"), "col"),
            P(),
        ),
        out_specs=(P(None, ("row", "own"), "col"), P("own", None, None)),
        check_vma=False,
    )
```

```python
import functools
import math

import jax
import jax.numpy as jnp
import numpy as np
from jax import lax
from jax.experimental import pallas as pl
from jax.experimental.pallas import tpu as pltpu
from jax.sharding import PartitionSpec as P

TILE = 128
MODES = 32
LANES = 128
HALO = 8
FIELDS = 7
SWEEPS = 3
PER = LANES // MODES
SHARES = 4
LAG = 12
MESH = pl.DeviceIdType.MESH
HIGHEST = lax.Precision.HIGHEST


def bases():
    places = np.arange(TILE) + 0.5
    orders = np.arange(MODES)
    cosine = np.cos(math.pi * orders[:, None] * places[None, :] / TILE)
    first = np.concatenate([cosine[s::PER] for s in range(PER)], axis=0)
    second = np.zeros((PER * TILE, LANES))
    for s in range(PER):
        second[s * TILE : (s + 1) * TILE, s * MODES : (s + 1) * MODES] = cosine.T / TILE
    return first.astype(np.float32), second.astype(np.float32)


def around(step, size):
    return min(step % size, -step % size)


def pipeline(count, lag, *stages):
    held = {}
    for step in range(count + lag * (len(stages) - 1)):
        for i, stage in reversed(list(enumerate(stages))):
            t = step - i * lag
            if 0 <= t < count:
                held[t] = stage(t, held.pop(t, None))


def solve(chunks, refs, n_of, ice_of, field, keep):
    coef, hb, w, w2 = refs
    first_sub = lax.broadcasted_iota(jnp.int32, (8, LANES), 0) == 0
    zero = jnp.zeros((8, LANES), jnp.float32)

    def rows_of(t):
        return slice(8 * t, 8 * t + 8)

    def down(x, kept):
        turned = pltpu.roll(x, 1, 0)
        return jnp.where(first_sub, kept, turned), turned

    def store_state(to, t, k, now):
        to[k, rows_of(t), :] = now
        return pltpu.roll(now, LANES - 1, 1)

    def store_ahead(to):
        def stage(t, turned):
            for k in range(2):
                to[2 + k, rows_of(t), :] = turned[k]

        return stage

    def open_(t, _):
        n = n_of(t)
        return n, pltpu.roll(n, 1, 1)

    summed_kept = [zero]

    def settle(t, given):
        n, turned = given
        at = rows_of(t)
        summed = n + turned
        moved, summed_kept[0] = down(summed, summed_kept[0])
        f = field(1, t)
        half = jnp.where(ice_of(t), 0.5 / (1.25 * (summed + moved) + f), 0.0)
        coef[0, at, :] = 0.5 * n
        coef[1, at, :] = 0.25 * n
        coef[2, at, :] = half
        coef[3, at, :] = 1.0 - half * f
        out = []
        for k in range(2):
            scaled = half * field(2 + k, t)
            hb[k, at, :] = scaled
            out.append(store_state(w, t, k, scaled + scaled))
        return out

    pipeline(chunks, LAG, open_, settle, store_ahead(w))
    for k in range(4):
        w[k, rows_of(chunks), :] = zero
        w2[k, rows_of(chunks), :] = zero

    def turn():
        def begin(t, _):
            at = rows_of(t)
            out = []
            for k in range(2):
                now = w2[k, at, :]
                keep(t, k, now)
                scaled = coef[2, at, :] * (now - field(4 + k, t))
                hb[k, at, :] = scaled
                out.append(store_state(w2, t, k, scaled + scaled))
            return out

        pipeline(chunks, LAG, begin, store_ahead(w2))

    def sweep(w_from, w_to):
        kept = [zero] * 4

        def front(t, _):
            at, after = rows_of(t), slice(8 * t + 1, 8 * t + 9)
            dx, dy = [], []
            for k in range(2):
                here, here_next = w_from[k, at, :], w_from[2 + k, at, :]
                below, below_next = w_from[k, after, :], w_from[2 + k, after, :]
                dx.append((below - here) + (below_next - here_next))
                dy.append((here_next + below_next) - (here + below))
            m, q = coef[0, at, :], coef[1, at, :]
            total = dx[0] + dy[1]
            one = m * (total + dx[0])
            two = m * (total + dy[1])
            shear = q * (dy[0] + dx[1])
            fields = (one + shear, one - shear, two + shear, shear - two)
            moved = []
            for i in range(4):
                got, kept[i] = down(fields[i], kept[i])
                moved.append(got)
            stay = (moved[1] - fields[0], moved[3] - fields[2])
            go = (moved[0] - fields[1], moved[2] - fields[3])
            return stay, tuple(pltpu.roll(x, 1, 1) for x in go)

        def close(t, given):
            at = rows_of(t)
            turned = []
            for k in range(2):
                image = given[0][k] + given[1][k]
                now = (
                    coef[3, at, :] * w_from[k, at, :] + hb[k, at, :]
                ) - coef[2, at, :] * image
                turned.append(store_state(w_to, t, k, now))
            return turned

        pipeline(chunks, LAG, front, close, store_ahead(w_to))

    def pair(s, _):
        sweep(w, w2)

        @pl.when(s == 1)
        def _():
            turn()

        sweep(w2, w)
        return 0

    lax.fori_loop(0, SWEEPS, pair, 0)


def exchange(
    sizes,
    visc,
    fric,
    drv,
    obs,
    mask,
    fm,
    mk,
    recv_t,
    diag,
    beside,
    v,
    dm,
    pack,
    pack_t,
    coef,
    hb,
    w,
    w2,
    load_sem,
    halo_send,
    halo_recv,
):
    n_row, n_own, n_col = sizes
    n_line = n_row * n_own
    rows = visc.shape[0]
    row_at, own_at, col = (
        lax.axis_index("row"),
        lax.axis_index("own"),
        lax.axis_index("col"),
    )
    line = row_at * n_own + own_at

    def by(rows_on, owns_on, cols_on):
        return {
            "row": lax.rem(row_at + (rows_on + n_row), n_row),
            "own": lax.rem(own_at + (owns_on + n_own), n_own),
            "col": lax.rem(col + (cols_on + n_col), n_col),
        }

    def next_to(line_on, cols_on):
        to = lax.rem(line + (line_on + n_line), n_line)
        return {
            "row": lax.div(to, n_own),
            "own": lax.rem(to, n_own),
            "col": lax.rem(col + (cols_on + n_col), n_col),
        }

    own_rows = pl.ds(HALO, rows)
    loads = [
        (visc, fm.at[0, own_rows, :]),
        (fric, fm.at[1, own_rows, :]),
        (drv, fm.at[2:4, own_rows, :]),
        (obs, fm.at[4:6, own_rows, :]),
        (mask, mk.at[own_rows, :]),
    ]
    loads = [
        pltpu.make_async_copy(src, dst, load_sem.at[i])
        for i, (src, dst) in enumerate(loads)
    ]
    for copy in loads:
        copy.start()

    barrier = pltpu.get_barrier_semaphore()
    greeted = [next_to(i, j) for i in (-1, 1) for j in (-1, 0, 1)]
    greeted += [by(0, 0, i) for i in (-1, 1)]
    for to in greeted:
        pl.semaphore_signal(barrier, inc=1, device_id=to, device_id_type=MESH)

    lane = lax.broadcasted_iota(jnp.int32, (8, LANES), 1)

    for copy in loads:
        copy.wait()

    def gather(t, _):
        at = pl.ds(HALO + 8 * t, 8)
        found = [fm[f, at, :] for f in range(6)] + [mk[at, :].astype(jnp.float32)]
        return [pltpu.roll(piece, 16 * f + 8, 1) for f, piece in enumerate(found)]

    def merge(t, pieces):
        packed = pieces[0]
        for f in range(1, FIELDS):
            packed = jnp.where(lane < 16 * f, packed, pieces[f])
        pack[8 * t : 8 * t + 8, :] = packed

    pipeline(rows // 8, 4, gather, merge)
    for part in range(rows // LANES):
        block = pack[part * LANES : (part + 1) * LANES, :]
        pack_t[:, :, part * LANES : (part + 1) * LANES] = block.T.reshape(8, 16, LANES)
    recv_t[FIELDS : 16 - FIELDS] = jnp.zeros((2, 8, rows), jnp.float32)

    pl.semaphore_wait(barrier, len(greeted))
    copies = []

    def send(src, dst, to):
        at = len(copies)
        copy = pltpu.make_async_remote_copy(
            src_ref=src,
            dst_ref=dst,
            send_sem=halo_send.at[at],
            recv_sem=halo_recv.at[at],
            device_id=to,
            device_id_type=MESH,
        )
        copy.start()
        copies.append(copy)

    for line_on, source, slot in ((-1, 0, 2), (1, rows - 8, 0)):
        for cols_on in (-1, 1):
            send(
                pack.at[pl.ds(source, 8), :],
                diag.at[slot + (1 if cols_on < 0 else 0)],
                next_to(line_on, cols_on),
            )
    send(pack_t.at[0:FIELDS, 0:8, :], recv_t.at[0:FIELDS], by(0, 0, 1))
    send(pack_t.at[0:FIELDS, 8:16, :], recv_t.at[16 - FIELDS : 16], by(0, 0, -1))
    for line_on, source, target in ((-1, HALO, HALO + rows), (1, rows, 0)):
        to, take = pl.ds(target, HALO), pl.ds(source, HALO)
        send(fm.at[:, take, :], fm.at[:, to, :], next_to(line_on, 0))
        send(mk.at[take, :], mk.at[to, :], next_to(line_on, 0))

    def turn_half(t, _):
        at = pl.ds(HALO + 8 * t, 8)
        found = [fm[f, at, :] for f in range(6)] + [mk[at, :].astype(jnp.float32)]
        return [(x, pltpu.roll(x, 64, 1)) for x in found]

    def put_half(t, pieces):
        for f, (x, turned) in enumerate(pieces):
            beside[f, 8 * t : 8 * t + 8, :] = jnp.where(lane < 32, x, turned)

    pipeline(rows // 8, 2, turn_half, put_half)

    def field(f, t):
        return fm[f, HALO + 8 * t : HALO + 8 * t + 8, :]

    def keep(t, k, now):
        v[k, 8 * t : 8 * t + 8, :] = now

    solve(
        rows // 8,
        (coef, hb, w, w2),
        lambda t: field(0, t),
        lambda t: mk[HALO + 8 * t : HALO + 8 * t + 8, :] > 0,
        field,
        keep,
    )
    for t in range(1, rows // 8 - 1):
        at = slice(8 * t, 8 * t + 8)
        dm[at, :] = field(1, t) * (
            w[0, at, :] * v[0, at, :] + w[1, at, :] * v[1, at, :]
        )

    for copy in copies:
        copy.wait()


def kernel(
    sizes,
    fm,
    mk,
    recv_t,
    diag,
    beside,
    v_in,
    dm,
    tile_block,
    owner_list,
    basis_1,
    basis_2,
    v,
    grad,
    fs,
    coef,
    hb,
    w,
    w2,
    vx,
    dens,
    b1,
    b2,
    tb,
    ol,
    send_a,
    recv_a,
    table,
    load_sem,
    phase_send,
    phase_recv,
):
    n_row, n_own, n_col = sizes
    n_line = n_row * n_own
    rows = fm.shape[1] - 2 * HALO
    chunks = (rows + 2 * HALO) // 8
    row_at, own_at, col = (
        lax.axis_index("row"),
        lax.axis_index("own"),
        lax.axis_index("col"),
    )
    line = row_at * n_own + own_at

    def by(rows_on, owns_on, cols_on):
        return {
            "row": lax.rem(row_at + (rows_on + n_row), n_row),
            "own": lax.rem(own_at + (owns_on + n_own), n_own),
            "col": lax.rem(col + (cols_on + n_col), n_col),
        }

    col_steps = sorted(range(1, n_col), key=lambda i: -around(i, n_col))
    plane_steps = [(i, j) for i in range(n_row) for j in range(n_own) if i or j]
    plane_steps.sort(key=lambda s: -(around(s[0], n_row) + around(s[1], n_own)))

    loads = [
        (basis_1, b1),
        (basis_2, b2),
        (tile_block, tb),
        (owner_list, ol),
    ]
    loads = [
        pltpu.make_async_copy(src, dst, load_sem.at[i])
        for i, (src, dst) in enumerate(loads)
    ]
    for copy in loads:
        copy.start()

    barrier = pltpu.get_barrier_semaphore()
    greeted = [by(0, 0, i) for i in col_steps]
    greeted += [by(i, j, 0) for i, j in plane_steps]
    for to in greeted:
        pl.semaphore_signal(barrier, inc=1, device_id=to, device_id_type=MESH)

    lane = lax.broadcasted_iota(jnp.int32, (8, LANES), 1)

    def corners(e, left, right):
        at = pl.ds(8 * e, 8)
        for f in range(FIELDS):
            x = fm[f, at, :] if f < 6 else mk[at, :].astype(jnp.float32)
            own = jnp.where(lane < 32, x, pltpu.roll(x, 64, 1))
            far = jnp.where(
                lane < 96,
                pltpu.roll(right, (56 - 16 * f) % LANES, 1),
                pltpu.roll(left, (120 - 16 * f) % LANES, 1),
            )
            fs[f, at, :] = jnp.where(lane < 64, own, far)

    corners(0, diag[0], diag[1])
    corners(chunks - 1, diag[2], diag[3])
    blocks = [
        recv_t[:, :, part * LANES : (part + 1) * LANES].reshape(LANES, LANES).T
        for part in range(rows // LANES)
    ]

    def spread(t, _):
        packed = blocks[8 * t // LANES][8 * t % LANES : 8 * t % LANES + 8, :]
        return [pltpu.roll(packed, (120 - 8 * f) % LANES, 1) for f in range(FIELDS)]

    def put(t, turned):
        at = slice(8 * t, 8 * t + 8)
        for f in range(FIELDS):
            fs[f, HALO + 8 * t : HALO + 8 * t + 8, :] = jnp.where(
                lane < 64, beside[f, at, :], turned[f]
            )

    pipeline(rows // 8, 4, spread, put)

    ends = [0, 1, 2, chunks - 3, chunks - 2, chunks - 1]
    upper, lower, strips = 1, 4, len(ends)

    def place(t):
        return (fm, ends[t]) if t < strips else (fs, t - strips)

    def field(f, t):
        source, e = place(t)
        return source[f, 8 * e : 8 * e + 8, :]

    strip_inside = (
        (lane < 64)
        | ((lane < 96) & (col < n_col - 1))
        | ((lane >= 96) & (col > 0))
    )

    def inside(t):
        e = place(t)[1]
        mask = strip_inside if t >= strips else None
        if e == 0 or e == chunks - 1:
            there = jnp.broadcast_to(
                line > 0 if e == 0 else line < n_line - 1, (8, LANES)
            )
            mask = there if mask is None else mask & there
        return mask

    def n_of(t):
        mask = inside(t)
        return field(0, t) if mask is None else jnp.where(mask, field(0, t), 0.0)

    def ice_of(t):
        e = place(t)[1]
        ice = mk[8 * e : 8 * e + 8, :] > 0 if t < strips else field(6, t) > 0.5
        mask = inside(t)
        return ice if mask is None else ice & mask

    def keep(t, k, now):
        vx[k, 8 * t : 8 * t + 8, :] = now

    solve(strips + chunks, (coef, hb, w, w2), n_of, ice_of, field, keep)

    def product(t):
        at = slice(8 * t, 8 * t + 8)
        return field(1, t) * (
            w[0, at, :] * vx[0, at, :] + w[1, at, :] * vx[1, at, :]
        )

    def merged(strip, turned, base):
        return jnp.where(lane < 8, strip, jnp.where(lane >= 120, turned, base))

    def strip_product(t, _):
        strip = product(strips + 1 + t)
        return strip, pltpu.roll(strip, 64, 1)

    def put_product(t, given):
        if t == 0 or t == rows // 8 - 1:
            base = product(upper if t == 0 else lower)
        else:
            base = dm[8 * t : 8 * t + 8, :]
        u = 8 * t % TILE
        piece = merged(*given, base)
        if 8 * t < TILE:
            dens[u : u + 8, :] = -piece
        else:
            dens[u : u + 8, :] = dens[u : u + 8, :] - piece

    pipeline(rows // 8, 8, strip_product, put_product)

    for copy in loads:
        copy.wait()
    first = jnp.dot(
        b1[...], dens[...], precision=HIGHEST, preferred_element_type=jnp.float32
    )
    first = jnp.concatenate([first[8 * i : 8 * i + 8] for i in range(PER)], axis=1)
    part = jnp.dot(
        first, b2[...], precision=HIGHEST, preferred_element_type=jnp.float32
    )
    in_second = tb[0, 0] > 2 * line
    parts = jnp.where(in_second, 0.0, part), jnp.where(in_second, part, 0.0)
    per_share = 8 // SHARES
    for i in range(SHARES):
        for j in range(2):
            at = pl.ds(j * per_share, per_share)
            send_a[i, at, :] = parts[j][i * per_share : (i + 1) * per_share, :]

    def start(phase, src, dst, to):
        pltpu.make_async_remote_copy(
            src_ref=src,
            dst_ref=dst,
            send_sem=phase_send.at[phase],
            recv_sem=phase_recv.at[phase],
            device_id=to,
            device_id_type=MESH,
        ).start()

    def arrived(phase, ref):
        pltpu.make_async_copy(ref, ref, phase_recv.at[phase]).wait()

    def departed(phase, ref):
        pltpu.make_async_copy(ref, ref, phase_send.at[phase]).wait()

    pl.semaphore_wait(barrier, len(greeted))
    share = lax.rem(col, SHARES)
    for i in col_steps:
        to = by(0, 0, i)
        start(0, send_a.at[lax.rem(to["col"], SHARES)], recv_a.at[col], to)
    recv_a[col] = send_a[share]

    def strip_velocity(t, _):
        found = []
        for k in range(2):
            at = 8 * (strips + 1 + t)
            strip = vx[k, at : at + 8, :]
            found.append((strip, pltpu.roll(strip, 64, 1)))
        return found

    def put_velocity(t, given):
        at = slice(8 * t, 8 * t + 8)
        for k in range(2):
            if t == 0 or t == rows // 8 - 1:
                e = 8 * (upper if t == 0 else lower)
                base = vx[k, e : e + 8, :]
            else:
                base = v_in[k, at, :]
            v[k, at, :] = merged(*given[k], base)

    pipeline(rows // 8, 8, strip_velocity, put_velocity)
    arrived(0, recv_a.at[0 : n_col - 1])
    total = recv_a[0]
    for i in range(1, n_col):
        total = total + recv_a[i]

    mine = table.at[pl.ds(2 * line, 2)]
    for j in range(2):
        table[2 * line + j] = total[j * per_share : (j + 1) * per_share, :]
    for i, j in plane_steps:
        start(1, mine, mine, by(i, j, 0))
    arrived(1, table.at[0 : 2 * n_line - 2])

    per_owner = ol.shape[0] // n_own
    width = per_share * LANES
    for k in range(per_owner):
        entry = table[ol[own_at * per_owner + k]]
        for j in range(per_share):
            at = pl.ds(pl.multiple_of(share * width + j * LANES, LANES), LANES)
            grad[0, k : k + 1, at] = entry[j : j + 1, :]

    mine_c = grad.at[0, :, pl.ds(pl.multiple_of(share * width, LANES), width)]
    for i in range(1, SHARES):
        to = {"row": row_at, "own": own_at, "col": lax.bitwise_xor(col, i)}
        start(2, mine_c, mine_c, to)
    arrived(2, grad.at[0, :, 0 : (SHARES - 1) * width])

    departed(0, recv_a.at[0 : n_col - 1])
    departed(1, table.at[0 : 2 * n_line - 2])
    departed(2, grad.at[0, :, 0 : (SHARES - 1) * width])


def solution(mesh):
    sizes = tuple(mesh.shape[a] for a in ("row", "own", "col"))
    n_line, n_col = sizes[0] * sizes[1], sizes[2]

    def local(viscosity, friction, driving, observed, ice_mask, tile_block, owner_list):
        rows = viscosity.shape[0]
        ext = rows + 2 * HALO
        first, second = bases()
        per_owner = owner_list.shape[0] // sizes[1]
        f32 = jnp.float32
        vmem = pltpu.VMEM
        fields = (viscosity, friction, driving, observed, ice_mask)
        tile_block = tile_block.reshape(1, -1)
        small = (tile_block, owner_list, jnp.asarray(first), jnp.asarray(second))
        hbm = pl.BlockSpec(memory_space=pltpu.HBM)
        here = pl.BlockSpec(memory_space=pltpu.VMEM)
        dma = pltpu.SemaphoreType.DMA

        def pinned(operands):
            return [pltpu.with_memory_space_constraint(x, pltpu.HBM) for x in operands]

        padded = pl.pallas_call(
            functools.partial(exchange, sizes),
            out_shape=(
                jax.ShapeDtypeStruct((6, ext, LANES), f32),
                jax.ShapeDtypeStruct((ext, LANES), jnp.int32),
                jax.ShapeDtypeStruct((16, 8, rows), f32),
                jax.ShapeDtypeStruct((4, 8, LANES), f32),
                jax.ShapeDtypeStruct((FIELDS, rows, LANES), f32),
                jax.ShapeDtypeStruct((2, rows, LANES), f32),
                jax.ShapeDtypeStruct((rows, LANES), f32),
            ),
            in_specs=[hbm] * 5,
            out_specs=[here] * 7,
            scratch_shapes=[
                vmem((rows, LANES), f32),
                vmem((8, 16, rows), f32),
                vmem((4, rows, LANES), f32),
                vmem((2, rows, LANES), f32),
                vmem((4, rows + 8, LANES), f32),
                vmem((4, rows + 8, LANES), f32),
                dma((5,)),
                dma((10,)),
                dma((10,)),
            ],
            compiler_params=pltpu.CompilerParams(
                collective_id=0,
                has_side_effects=True,
                vmem_limit_bytes=16 * 2**20,
            ),
        )(*pinned(fields))
        return pl.pallas_call(
            functools.partial(kernel, sizes),
            out_shape=(
                jax.ShapeDtypeStruct((2, rows, LANES), f32),
                jax.ShapeDtypeStruct((1, per_owner, MODES * MODES), f32),
            ),
            in_specs=[here] * 7 + [hbm] * 4,
            out_specs=[here] * 2,
            scratch_shapes=[
                vmem((FIELDS, ext, LANES), f32),
                vmem((4, ext + 48, LANES), f32),
                vmem((2, ext + 48, LANES), f32),
                vmem((4, ext + 56, LANES), f32),
                vmem((4, ext + 56, LANES), f32),
                vmem((2, ext + 48, LANES), f32),
                vmem((TILE, LANES), f32),
                vmem(first.shape, f32),
                vmem(second.shape, f32),
                pltpu.SMEM(tile_block.shape, jnp.int32),
                pltpu.SMEM(owner_list.shape, jnp.int32),
                vmem((SHARES, 2 * 8 // SHARES, LANES), f32),
                vmem((n_col, 2 * 8 // SHARES, LANES), f32),
                vmem((2 * n_line, 8 // SHARES, LANES), f32),
                dma((4,)),
                dma((3,)),
                dma((3,)),
            ],
            compiler_params=pltpu.CompilerParams(
                collective_id=1,
                has_side_effects=True,
                vmem_limit_bytes=32 * 2**20,
            ),
        )(*padded, *pinned(small))

    return jax.shard_map(
        local,
        mesh=mesh,
        in_specs=(
            P(("row", "own"), "col"),
            P(("row", "own"), "col"),
            P(None, ("row", "own"), "col"),
            P(None, ("row", "own"), "col"),
            P(("row", "own"), "col"),
            P(("row", "own"), "col"),
            P(),
        ),
        out_specs=(P(None, ("row", "own"), "col"), P("own", None, None)),
        check_vma=False,
    )
```

```python
import functools
import math

import jax
import jax.numpy as jnp
import numpy as np
from jax import lax
from jax.experimental import pallas as pl
from jax.experimental.pallas import tpu as pltpu
from jax.sharding import PartitionSpec as P

TILE = 128
MODES = 32
LANES = 128
HALO = 8
FIELDS = 7
SWEEPS = 3
PER = LANES // MODES
SHARES = 4
LAG = 12
MESH = pl.DeviceIdType.MESH
HIGHEST = lax.Precision.HIGHEST


def bases():
    places = np.arange(TILE) + 0.5
    orders = np.arange(MODES)
    cosine = np.cos(math.pi * orders[:, None] * places[None, :] / TILE)
    first = np.concatenate([cosine[s::PER] for s in range(PER)], axis=0)
    second = np.zeros((PER * TILE, LANES))
    for s in range(PER):
        second[s * TILE : (s + 1) * TILE, s * MODES : (s + 1) * MODES] = cosine.T / TILE
    return first.astype(np.float32), second.astype(np.float32)


def around(step, size):
    return min(step % size, -step % size)


def pipeline(count, lag, *stages):
    held = {}
    for step in range(count + lag * (len(stages) - 1)):
        for i, stage in reversed(list(enumerate(stages))):
            t = step - i * lag
            if 0 <= t < count:
                held[t] = stage(t, held.pop(t, None))


def solve(chunks, refs, n_of, ice_of, field, keep):
    coef, hb, w, w2 = refs
    first_sub = lax.broadcasted_iota(jnp.int32, (8, LANES), 0) == 0
    zero = jnp.zeros((8, LANES), jnp.float32)

    def rows_of(t):
        return slice(8 * t, 8 * t + 8)

    def down(x, kept):
        turned = pltpu.roll(x, 1, 0)
        return jnp.where(first_sub, kept, turned), turned

    def store_state(to, t, k, now):
        to[k, rows_of(t), :] = now
        return pltpu.roll(now, LANES - 1, 1)

    def store_ahead(to):
        def stage(t, turned):
            for k in range(2):
                to[2 + k, rows_of(t), :] = turned[k]

        return stage

    def open_(t, _):
        n = n_of(t)
        return n, pltpu.roll(n, 1, 1)

    summed_kept = [zero]

    def settle(t, given):
        n, turned = given
        at = rows_of(t)
        summed = n + turned
        moved, summed_kept[0] = down(summed, summed_kept[0])
        f = field(1, t)
        half = jnp.where(ice_of(t), 0.5 / (1.25 * (summed + moved) + f), 0.0)
        coef[0, at, :] = 0.5 * n
        coef[1, at, :] = 0.25 * n
        coef[2, at, :] = half
        coef[3, at, :] = 1.0 - half * f
        out = []
        for k in range(2):
            scaled = half * field(2 + k, t)
            hb[k, at, :] = scaled
            out.append(store_state(w, t, k, scaled + scaled))
        return out

    pipeline(chunks, LAG, open_, settle, store_ahead(w))
    for k in range(4):
        w[k, rows_of(chunks), :] = zero
        w2[k, rows_of(chunks), :] = zero

    def turn():
        def begin(t, _):
            at = rows_of(t)
            out = []
            for k in range(2):
                now = w2[k, at, :]
                keep(t, k, now)
                scaled = coef[2, at, :] * (now - field(4 + k, t))
                hb[k, at, :] = scaled
                out.append(store_state(w2, t, k, scaled + scaled))
            return out

        pipeline(chunks, LAG, begin, store_ahead(w2))

    def sweep(w_from, w_to):
        kept = [zero] * 4

        def front(t, _):
            at, after = rows_of(t), slice(8 * t + 1, 8 * t + 9)
            dx, dy = [], []
            for k in range(2):
                here, here_next = w_from[k, at, :], w_from[2 + k, at, :]
                below, below_next = w_from[k, after, :], w_from[2 + k, after, :]
                dx.append((below - here) + (below_next - here_next))
                dy.append((here_next + below_next) - (here + below))
            m, q = coef[0, at, :], coef[1, at, :]
            total = dx[0] + dy[1]
            one = m * (total + dx[0])
            two = m * (total + dy[1])
            shear = q * (dy[0] + dx[1])
            fields = (one + shear, one - shear, two + shear, shear - two)
            moved = []
            for i in range(4):
                got, kept[i] = down(fields[i], kept[i])
                moved.append(got)
            stay = (moved[1] - fields[0], moved[3] - fields[2])
            go = (moved[0] - fields[1], moved[2] - fields[3])
            return stay, tuple(pltpu.roll(x, 1, 1) for x in go)

        def close(t, given):
            at = rows_of(t)
            turned = []
            for k in range(2):
                image = given[0][k] + given[1][k]
                now = (
                    coef[3, at, :] * w_from[k, at, :] + hb[k, at, :]
                ) - coef[2, at, :] * image
                turned.append(store_state(w_to, t, k, now))
            return turned

        pipeline(chunks, LAG, front, close, store_ahead(w_to))

    def pair(s, _):
        sweep(w, w2)

        @pl.when(s == 1)
        def _():
            turn()

        sweep(w2, w)
        return 0

    lax.fori_loop(0, SWEEPS, pair, 0)


def kernel(
    sizes,
    visc,
    fric,
    drv,
    obs,
    mask,
    tile_block,
    owner_list,
    basis_1,
    basis_2,
    v,
    grad,
    fm,
    mk,
    recv_t,
    diag,
    beside,
    v_in,
    dm,
    pack,
    pack_t,
    fs,
    coef,
    hb,
    w,
    w2,
    vx,
    dens,
    b1,
    b2,
    tb,
    ol,
    send_a,
    recv_a,
    table,
    load_sem,
    halo_send,
    halo_recv,
    phase_send,
    phase_recv,
):
    n_row, n_own, n_col = sizes
    n_line = n_row * n_own
    rows = visc.shape[0]
    chunks = (rows + 2 * HALO) // 8
    row_at, own_at, col = (
        lax.axis_index("row"),
        lax.axis_index("own"),
        lax.axis_index("col"),
    )
    line = row_at * n_own + own_at

    def by(rows_on, owns_on, cols_on):
        return {
            "row": lax.rem(row_at + (rows_on + n_row), n_row),
            "own": lax.rem(own_at + (owns_on + n_own), n_own),
            "col": lax.rem(col + (cols_on + n_col), n_col),
        }

    def next_to(line_on, cols_on):
        to = lax.rem(line + (line_on + n_line), n_line)
        return {
            "row": lax.div(to, n_own),
            "own": lax.rem(to, n_own),
            "col": lax.rem(col + (cols_on + n_col), n_col),
        }

    col_steps = sorted(range(1, n_col), key=lambda i: -around(i, n_col))
    plane_steps = [(i, j) for i in range(n_row) for j in range(n_own) if i or j]
    plane_steps.sort(key=lambda s: -(around(s[0], n_row) + around(s[1], n_own)))

    barrier = pltpu.get_barrier_semaphore()
    greeted = [by(i, j, 0) for i, j in plane_steps]
    greeted += [by(0, 0, i) for i in col_steps]
    greeted += [next_to(i, j) for i in (-1, 1) for j in (-1, 1)]
    for to in greeted:
        pl.semaphore_signal(barrier, inc=1, device_id=to, device_id_type=MESH)

    own_rows = pl.ds(HALO, rows)
    loads = [
        (visc, fm.at[0, own_rows, :]),
        (fric, fm.at[1, own_rows, :]),
        (drv, fm.at[2:4, own_rows, :]),
        (obs, fm.at[4:6, own_rows, :]),
        (mask, mk.at[own_rows, :]),
        (basis_1, b1),
        (basis_2, b2),
        (tile_block, tb),
        (owner_list, ol),
    ]
    loads = [
        pltpu.make_async_copy(src, dst, load_sem.at[i])
        for i, (src, dst) in enumerate(loads)
    ]
    for copy in loads:
        copy.start()

    lane = lax.broadcasted_iota(jnp.int32, (8, LANES), 1)

    for copy in loads[:5]:
        copy.wait()

    def gather(t, _):
        at = pl.ds(HALO + 8 * t, 8)
        found = [fm[f, at, :] for f in range(6)] + [mk[at, :].astype(jnp.float32)]
        return [pltpu.roll(piece, 16 * f + 8, 1) for f, piece in enumerate(found)]

    def merge(t, pieces):
        packed = pieces[0]
        for f in range(1, FIELDS):
            packed = jnp.where(lane < 16 * f, packed, pieces[f])
        pack[8 * t : 8 * t + 8, :] = packed

    pipeline(rows // 8, 4, gather, merge)
    for part in range(rows // LANES):
        block = pack[part * LANES : (part + 1) * LANES, :]
        pack_t[:, :, part * LANES : (part + 1) * LANES] = block.T.reshape(8, 16, LANES)
    recv_t[FIELDS : 16 - FIELDS] = jnp.zeros((2, 8, rows), jnp.float32)

    pl.semaphore_wait(barrier, len(greeted))
    copies = []

    def send(src, dst, to):
        at = len(copies)
        copy = pltpu.make_async_remote_copy(
            src_ref=src,
            dst_ref=dst,
            send_sem=halo_send.at[at],
            recv_sem=halo_recv.at[at],
            device_id=to,
            device_id_type=MESH,
        )
        copy.start()
        copies.append(copy)

    for line_on, source, slot in ((-1, 0, 2), (1, rows - 8, 0)):
        for cols_on in (-1, 1):
            send(
                pack.at[pl.ds(source, 8), :],
                diag.at[slot + (1 if cols_on < 0 else 0)],
                next_to(line_on, cols_on),
            )
    send(pack_t.at[0:FIELDS, 0:8, :], recv_t.at[0:FIELDS], by(0, 0, 1))
    send(pack_t.at[0:FIELDS, 8:16, :], recv_t.at[16 - FIELDS : 16], by(0, 0, -1))
    for line_on, source, target in ((-1, HALO, HALO + rows), (1, rows, 0)):
        to, take = pl.ds(target, HALO), pl.ds(source, HALO)
        send(fm.at[:, take, :], fm.at[:, to, :], next_to(line_on, 0))
        send(mk.at[take, :], mk.at[to, :], next_to(line_on, 0))

    def turn_half(t, _):
        at = pl.ds(HALO + 8 * t, 8)
        found = [fm[f, at, :] for f in range(6)] + [mk[at, :].astype(jnp.float32)]
        return [(x, pltpu.roll(x, 64, 1)) for x in found]

    def put_half(t, pieces):
        for f, (x, turned) in enumerate(pieces):
            beside[f, 8 * t : 8 * t + 8, :] = jnp.where(lane < 32, x, turned)

    pipeline(rows // 8, 2, turn_half, put_half)

    def block_field(f, t):
        return fm[f, HALO + 8 * t : HALO + 8 * t + 8, :]

    def block_keep(t, k, now):
        v_in[k, 8 * t : 8 * t + 8, :] = now

    solve(
        rows // 8,
        (coef, hb, w, w2),
        lambda t: block_field(0, t),
        lambda t: mk[HALO + 8 * t : HALO + 8 * t + 8, :] > 0,
        block_field,
        block_keep,
    )
    for t in range(1, rows // 8 - 1):
        at = slice(8 * t, 8 * t + 8)
        dm[at, :] = block_field(1, t) * (
            w[0, at, :] * v_in[0, at, :] + w[1, at, :] * v_in[1, at, :]
        )

    for copy in copies:
        copy.wait_recv()

    def corners(e, left, right):
        at = pl.ds(8 * e, 8)
        for f in range(FIELDS):
            x = fm[f, at, :] if f < 6 else mk[at, :].astype(jnp.float32)
            own = jnp.where(lane < 32, x, pltpu.roll(x, 64, 1))
            far = jnp.where(
                lane < 96,
                pltpu.roll(right, (56 - 16 * f) % LANES, 1),
                pltpu.roll(left, (120 - 16 * f) % LANES, 1),
            )
            fs[f, at, :] = jnp.where(lane < 64, own, far)

    corners(0, diag[0], diag[1])
    corners(chunks - 1, diag[2], diag[3])
    blocks = [
        recv_t[:, :, part * LANES : (part + 1) * LANES].reshape(LANES, LANES).T
        for part in range(rows // LANES)
    ]

    def spread(t, _):
        packed = blocks[8 * t // LANES][8 * t % LANES : 8 * t % LANES + 8, :]
        return [pltpu.roll(packed, (120 - 8 * f) % LANES, 1) for f in range(FIELDS)]

    def put(t, turned):
        at = slice(8 * t, 8 * t + 8)
        for f in range(FIELDS):
            fs[f, HALO + 8 * t : HALO + 8 * t + 8, :] = jnp.where(
                lane < 64, beside[f, at, :], turned[f]
            )

    pipeline(rows // 8, 4, spread, put)

    ends = [0, 1, 2, chunks - 3, chunks - 2, chunks - 1]
    upper, lower, strips = 1, 4, len(ends)

    def place(t):
        return (fm, ends[t]) if t < strips else (fs, t - strips)

    def field(f, t):
        source, e = place(t)
        return source[f, 8 * e : 8 * e + 8, :]

    strip_inside = (
        (lane < 64)
        | ((lane < 96) & (col < n_col - 1))
        | ((lane >= 96) & (col > 0))
    )

    def inside(t):
        e = place(t)[1]
        mask = strip_inside if t >= strips else None
        if e == 0 or e == chunks - 1:
            there = jnp.broadcast_to(
                line > 0 if e == 0 else line < n_line - 1, (8, LANES)
            )
            mask = there if mask is None else mask & there
        return mask

    def n_of(t):
        mask = inside(t)
        return field(0, t) if mask is None else jnp.where(mask, field(0, t), 0.0)

    def ice_of(t):
        e = place(t)[1]
        ice = mk[8 * e : 8 * e + 8, :] > 0 if t < strips else field(6, t) > 0.5
        mask = inside(t)
        return ice if mask is None else ice & mask

    def keep(t, k, now):
        vx[k, 8 * t : 8 * t + 8, :] = now

    solve(strips + chunks, (coef, hb, w, w2), n_of, ice_of, field, keep)

    def product(t):
        at = slice(8 * t, 8 * t + 8)
        return field(1, t) * (
            w[0, at, :] * vx[0, at, :] + w[1, at, :] * vx[1, at, :]
        )

    def merged(strip, turned, base):
        return jnp.where(lane < 8, strip, jnp.where(lane >= 120, turned, base))

    def strip_product(t, _):
        strip = product(strips + 1 + t)
        return strip, pltpu.roll(strip, 64, 1)

    def put_product(t, given):
        if t == 0 or t == rows // 8 - 1:
            base = product(upper if t == 0 else lower)
        else:
            base = dm[8 * t : 8 * t + 8, :]
        u = 8 * t % TILE
        piece = merged(*given, base)
        if 8 * t < TILE:
            dens[u : u + 8, :] = -piece
        else:
            dens[u : u + 8, :] = dens[u : u + 8, :] - piece

    pipeline(rows // 8, 8, strip_product, put_product)

    for copy in loads[5:]:
        copy.wait()
    first = jnp.dot(
        b1[...], dens[...], precision=HIGHEST, preferred_element_type=jnp.float32
    )
    first = jnp.concatenate([first[8 * i : 8 * i + 8] for i in range(PER)], axis=1)
    part = jnp.dot(
        first, b2[...], precision=HIGHEST, preferred_element_type=jnp.float32
    )
    in_second = tb[0, 0] > 2 * line
    parts = jnp.where(in_second, 0.0, part), jnp.where(in_second, part, 0.0)
    per_share = 8 // SHARES
    for i in range(SHARES):
        for j in range(2):
            at = pl.ds(j * per_share, per_share)
            send_a[i, at, :] = parts[j][i * per_share : (i + 1) * per_share, :]

    def start(phase, src, dst, to):
        pltpu.make_async_remote_copy(
            src_ref=src,
            dst_ref=dst,
            send_sem=phase_send.at[phase],
            recv_sem=phase_recv.at[phase],
            device_id=to,
            device_id_type=MESH,
        ).start()

    def arrived(phase, ref):
        pltpu.make_async_copy(ref, ref, phase_recv.at[phase]).wait()

    def departed(phase, ref):
        pltpu.make_async_copy(ref, ref, phase_send.at[phase]).wait()

    share = lax.rem(col, SHARES)
    for i in col_steps:
        to = by(0, 0, i)
        start(0, send_a.at[lax.rem(to["col"], SHARES)], recv_a.at[col], to)
    recv_a[col] = send_a[share]

    def strip_velocity(t, _):
        found = []
        for k in range(2):
            at = 8 * (strips + 1 + t)
            strip = vx[k, at : at + 8, :]
            found.append((strip, pltpu.roll(strip, 64, 1)))
        return found

    def put_velocity(t, given):
        at = slice(8 * t, 8 * t + 8)
        for k in range(2):
            if t == 0 or t == rows // 8 - 1:
                e = 8 * (upper if t == 0 else lower)
                base = vx[k, e : e + 8, :]
            else:
                base = v_in[k, at, :]
            v[k, at, :] = merged(*given[k], base)

    pipeline(rows // 8, 8, strip_velocity, put_velocity)
    arrived(0, recv_a.at[0 : n_col - 1])
    total = recv_a[0]
    for i in range(1, n_col):
        total = total + recv_a[i]

    mine = table.at[pl.ds(2 * line, 2)]
    for j in range(2):
        table[2 * line + j] = total[j * per_share : (j + 1) * per_share, :]
    for i, j in plane_steps:
        start(1, mine, mine, by(i, j, 0))
    arrived(1, table.at[0 : 2 * n_line - 2])

    per_owner = ol.shape[0] // n_own
    width = per_share * LANES
    for k in range(per_owner):
        entry = table[ol[own_at * per_owner + k]]
        for j in range(per_share):
            at = pl.ds(pl.multiple_of(share * width + j * LANES, LANES), LANES)
            grad[0, k : k + 1, at] = entry[j : j + 1, :]

    mine_c = grad.at[0, :, pl.ds(pl.multiple_of(share * width, LANES), width)]
    for i in range(1, SHARES):
        to = {"row": row_at, "own": own_at, "col": lax.bitwise_xor(col, i)}
        start(2, mine_c, mine_c, to)
    arrived(2, grad.at[0, :, 0 : (SHARES - 1) * width])

    for copy in copies:
        copy.wait_send()
    departed(0, recv_a.at[0 : n_col - 1])
    departed(1, table.at[0 : 2 * n_line - 2])
    departed(2, grad.at[0, :, 0 : (SHARES - 1) * width])


def solution(mesh):
    sizes = tuple(mesh.shape[a] for a in ("row", "own", "col"))
    n_line, n_col = sizes[0] * sizes[1], sizes[2]

    def local(viscosity, friction, driving, observed, ice_mask, tile_block, owner_list):
        rows = viscosity.shape[0]
        ext = rows + 2 * HALO
        first, second = bases()
        per_owner = owner_list.shape[0] // sizes[1]
        f32 = jnp.float32
        vmem = pltpu.VMEM
        fields = (viscosity, friction, driving, observed, ice_mask)
        tile_block = tile_block.reshape(1, -1)
        small = (tile_block, owner_list, jnp.asarray(first), jnp.asarray(second))
        hbm = pl.BlockSpec(memory_space=pltpu.HBM)
        here = pl.BlockSpec(memory_space=pltpu.VMEM)
        dma = pltpu.SemaphoreType.DMA

        def pinned(operands):
            return [pltpu.with_memory_space_constraint(x, pltpu.HBM) for x in operands]

        return pl.pallas_call(
            functools.partial(kernel, sizes),
            out_shape=(
                jax.ShapeDtypeStruct((2, rows, LANES), f32),
                jax.ShapeDtypeStruct((1, per_owner, MODES * MODES), f32),
            ),
            in_specs=[hbm] * 9,
            out_specs=[here] * 2,
            scratch_shapes=[
                vmem((6, ext, LANES), f32),
                vmem((ext, LANES), jnp.int32),
                vmem((16, 8, rows), f32),
                vmem((4, 8, LANES), f32),
                vmem((FIELDS, rows, LANES), f32),
                vmem((2, rows, LANES), f32),
                vmem((rows, LANES), f32),
                vmem((rows, LANES), f32),
                vmem((8, 16, rows), f32),
                vmem((FIELDS, ext, LANES), f32),
                vmem((4, ext + 48, LANES), f32),
                vmem((2, ext + 48, LANES), f32),
                vmem((4, ext + 56, LANES), f32),
                vmem((4, ext + 56, LANES), f32),
                vmem((2, ext + 48, LANES), f32),
                vmem((TILE, LANES), f32),
                vmem(first.shape, f32),
                vmem(second.shape, f32),
                pltpu.SMEM(tile_block.shape, jnp.int32),
                pltpu.SMEM(owner_list.shape, jnp.int32),
                vmem((SHARES, 2 * 8 // SHARES, LANES), f32),
                vmem((n_col, 2 * 8 // SHARES, LANES), f32),
                vmem((2 * n_line, 8 // SHARES, LANES), f32),
                dma((9,)),
                dma((10,)),
                dma((10,)),
                dma((3,)),
                dma((3,)),
            ],
            compiler_params=pltpu.CompilerParams(
                collective_id=0,
                has_side_effects=True,
                vmem_limit_bytes=32 * 2**20,
            ),
        )(*pinned(fields + small))

    return jax.shard_map(
        local,
        mesh=mesh,
        in_specs=(
            P(("row", "own"), "col"),
            P(("row", "own"), "col"),
            P(None, ("row", "own"), "col"),
            P(None, ("row", "own"), "col"),
            P(("row", "own"), "col"),
            P(("row", "own"), "col"),
            P(),
        ),
        out_specs=(P(None, ("row", "own"), "col"), P("own", None, None)),
        check_vma=False,
    )
```

```python
import functools
import math

import jax
import jax.numpy as jnp
import numpy as np
from jax import lax
from jax.experimental import pallas as pl
from jax.experimental.pallas import tpu as pltpu
from jax.sharding import PartitionSpec as P

TILE = 128
MODES = 32
LANES = 128
HALO = 8
FIELDS = 7
SWEEPS = 3
PER = LANES // MODES
SHARES = 4
LAG = 12
MESH = pl.DeviceIdType.MESH
HIGHEST = lax.Precision.HIGHEST


def bases():
    places = np.arange(TILE) + 0.5
    orders = np.arange(MODES)
    cosine = np.cos(math.pi * orders[:, None] * places[None, :] / TILE)
    first = np.concatenate([cosine[s::PER] for s in range(PER)], axis=0)
    second = np.concatenate([cosine.T / TILE] * PER, axis=1)
    return first.astype(np.float32), second.astype(np.float32)


def around(step, size):
    return min(step % size, -step % size)


def pipeline(count, lag, *stages):
    held = {}
    for step in range(count + lag * (len(stages) - 1)):
        for i, stage in reversed(list(enumerate(stages))):
            t = step - i * lag
            if 0 <= t < count:
                held[t] = stage(t, held.pop(t, None))


def solve(chunks, refs, n_of, ice_of, field, keep):
    coef, hb, w, w2 = refs
    first_sub = lax.broadcasted_iota(jnp.int32, (8, LANES), 0) == 0
    zero = jnp.zeros((8, LANES), jnp.float32)

    def rows_of(t):
        return slice(8 * t, 8 * t + 8)

    def down(x, kept):
        turned = pltpu.roll(x, 1, 0)
        return jnp.where(first_sub, kept, turned), turned

    def store_state(to, t, k, now):
        to[k, rows_of(t), :] = now
        return pltpu.roll(now, LANES - 1, 1)

    def store_ahead(to):
        def stage(t, turned):
            for k in range(2):
                to[2 + k, rows_of(t), :] = turned[k]

        return stage

    def open_(t, _):
        n = n_of(t)
        return n, pltpu.roll(n, 1, 1)

    summed_kept = [zero]

    def settle(t, given):
        n, turned = given
        at = rows_of(t)
        summed = n + turned
        moved, summed_kept[0] = down(summed, summed_kept[0])
        f = field(1, t)
        half = jnp.where(ice_of(t), 0.5 / (1.25 * (summed + moved) + f), 0.0)
        coef[0, at, :] = 0.5 * n
        coef[1, at, :] = 0.25 * n
        coef[2, at, :] = half
        coef[3, at, :] = 1.0 - half * f
        out = []
        for k in range(2):
            scaled = half * field(2 + k, t)
            hb[k, at, :] = scaled
            out.append(store_state(w, t, k, scaled + scaled))
        return out

    pipeline(chunks, LAG, open_, settle, store_ahead(w))
    for k in range(4):
        w[k, rows_of(chunks), :] = zero
        w2[k, rows_of(chunks), :] = zero

    def turn():
        def begin(t, _):
            at = rows_of(t)
            out = []
            for k in range(2):
                now = w2[k, at, :]
                keep(t, k, now)
                scaled = coef[2, at, :] * (now - field(4 + k, t))
                hb[k, at, :] = scaled
                out.append(store_state(w2, t, k, scaled + scaled))
            return out

        pipeline(chunks, LAG, begin, store_ahead(w2))

    def sweep(w_from, w_to):
        kept = [zero] * 4

        def front(t, _):
            at, after = rows_of(t), slice(8 * t + 1, 8 * t + 9)
            dx, dy = [], []
            for k in range(2):
                here, here_next = w_from[k, at, :], w_from[2 + k, at, :]
                below, below_next = w_from[k, after, :], w_from[2 + k, after, :]
                dx.append((below - here) + (below_next - here_next))
                dy.append((here_next + below_next) - (here + below))
            m, q = coef[0, at, :], coef[1, at, :]
            total = dx[0] + dy[1]
            one = m * (total + dx[0])
            two = m * (total + dy[1])
            shear = q * (dy[0] + dx[1])
            fields = (one + shear, one - shear, two + shear, shear - two)
            moved = []
            for i in range(4):
                got, kept[i] = down(fields[i], kept[i])
                moved.append(got)
            stay = (moved[1] - fields[0], moved[3] - fields[2])
            go = (moved[0] - fields[1], moved[2] - fields[3])
            return stay, tuple(pltpu.roll(x, 1, 1) for x in go)

        def close(t, given):
            at = rows_of(t)
            turned = []
            for k in range(2):
                image = given[0][k] + given[1][k]
                now = (
                    coef[3, at, :] * w_from[k, at, :] + hb[k, at, :]
                ) - coef[2, at, :] * image
                turned.append(store_state(w_to, t, k, now))
            return turned

        pipeline(chunks, LAG, front, close, store_ahead(w_to))

    def pair(s, _):
        sweep(w, w2)

        @pl.when(s == 1)
        def _():
            turn()

        sweep(w2, w)
        return 0

    lax.fori_loop(0, SWEEPS, pair, 0)


def kernel(
    sizes,
    visc,
    fric,
    drv,
    obs,
    mask,
    tile_block,
    owner_list,
    basis_1,
    basis_2,
    v,
    grad,
    fm,
    mk,
    recv_t,
    diag,
    beside,
    v_in,
    dm,
    pack,
    pack_t,
    fs,
    coef,
    hb,
    w,
    w2,
    vx,
    dens,
    b1,
    b2,
    tb,
    ol,
    send_a,
    recv_a,
    table,
    load_sem,
    halo_send,
    halo_recv,
    phase_send,
    phase_recv,
):
    n_row, n_own, n_col = sizes
    n_line = n_row * n_own
    rows = visc.shape[0]
    chunks = (rows + 2 * HALO) // 8
    row_at, own_at, col = (
        lax.axis_index("row"),
        lax.axis_index("own"),
        lax.axis_index("col"),
    )
    line = row_at * n_own + own_at

    def by(rows_on, owns_on, cols_on):
        return {
            "row": lax.rem(row_at + (rows_on + n_row), n_row),
            "own": lax.rem(own_at + (owns_on + n_own), n_own),
            "col": lax.rem(col + (cols_on + n_col), n_col),
        }

    def next_to(line_on, cols_on):
        to = lax.rem(line + (line_on + n_line), n_line)
        return {
            "row": lax.div(to, n_own),
            "own": lax.rem(to, n_own),
            "col": lax.rem(col + (cols_on + n_col), n_col),
        }

    col_steps = sorted(range(1, n_col), key=lambda i: -around(i, n_col))
    plane_steps = [(i, j) for i in range(n_row) for j in range(n_own) if i or j]
    plane_steps.sort(key=lambda s: -(around(s[0], n_row) + around(s[1], n_own)))

    barrier = pltpu.get_barrier_semaphore()
    greeted = [by(i, j, 0) for i, j in plane_steps]
    greeted += [by(0, 0, i) for i in col_steps]
    greeted += [next_to(i, j) for i in (-1, 1) for j in (-1, 1)]
    for to in greeted:
        pl.semaphore_signal(barrier, inc=1, device_id=to, device_id_type=MESH)

    own_rows = pl.ds(HALO, rows)
    loads = [
        (visc, fm.at[0, own_rows, :]),
        (fric, fm.at[1, own_rows, :]),
        (drv, fm.at[2:4, own_rows, :]),
        (obs, fm.at[4:6, own_rows, :]),
        (mask, mk.at[own_rows, :]),
        (basis_1, b1),
        (basis_2, b2),
        (tile_block, tb),
        (owner_list, ol),
    ]
    loads = [
        pltpu.make_async_copy(src, dst, load_sem.at[i])
        for i, (src, dst) in enumerate(loads)
    ]
    for copy in loads:
        copy.start()

    lane = lax.broadcasted_iota(jnp.int32, (8, LANES), 1)

    for copy in loads[:5]:
        copy.wait()

    def gather(t, _):
        at = pl.ds(HALO + 8 * t, 8)
        found = [fm[f, at, :] for f in range(6)] + [mk[at, :].astype(jnp.float32)]
        return [pltpu.roll(piece, 16 * f + 8, 1) for f, piece in enumerate(found)]

    def merge(t, pieces):
        packed = pieces[0]
        for f in range(1, FIELDS):
            packed = jnp.where(lane < 16 * f, packed, pieces[f])
        pack[8 * t : 8 * t + 8, :] = packed

    pipeline(rows // 8, 4, gather, merge)
    for part in range(rows // LANES):
        block = pack[part * LANES : (part + 1) * LANES, :]
        pack_t[:, :, part * LANES : (part + 1) * LANES] = block.T.reshape(8, 16, LANES)
    recv_t[FIELDS : 16 - FIELDS] = jnp.zeros((2, 8, rows), jnp.float32)

    pl.semaphore_wait(barrier, len(greeted))
    copies = []

    def send(src, dst, to):
        at = len(copies)
        copy = pltpu.make_async_remote_copy(
            src_ref=src,
            dst_ref=dst,
            send_sem=halo_send.at[at],
            recv_sem=halo_recv.at[at],
            device_id=to,
            device_id_type=MESH,
        )
        copy.start()
        copies.append(copy)

    for line_on, source, slot in ((-1, 0, 2), (1, rows - 8, 0)):
        for cols_on in (-1, 1):
            send(
                pack.at[pl.ds(source, 8), :],
                diag.at[slot + (1 if cols_on < 0 else 0)],
                next_to(line_on, cols_on),
            )
    send(pack_t.at[0:FIELDS, 0:8, :], recv_t.at[0:FIELDS], by(0, 0, 1))
    send(pack_t.at[0:FIELDS, 8:16, :], recv_t.at[16 - FIELDS : 16], by(0, 0, -1))
    for line_on, source, target in ((-1, HALO, HALO + rows), (1, rows, 0)):
        to, take = pl.ds(target, HALO), pl.ds(source, HALO)
        send(fm.at[:, take, :], fm.at[:, to, :], next_to(line_on, 0))
        send(mk.at[take, :], mk.at[to, :], next_to(line_on, 0))

    def turn_half(t, _):
        at = pl.ds(HALO + 8 * t, 8)
        found = [fm[f, at, :] for f in range(6)] + [mk[at, :].astype(jnp.float32)]
        return [(x, pltpu.roll(x, 64, 1)) for x in found]

    def put_half(t, pieces):
        for f, (x, turned) in enumerate(pieces):
            beside[f, 8 * t : 8 * t + 8, :] = jnp.where(lane < 32, x, turned)

    pipeline(rows // 8, 2, turn_half, put_half)

    def block_field(f, t):
        return fm[f, HALO + 8 * t : HALO + 8 * t + 8, :]

    def block_keep(t, k, now):
        v_in[k, 8 * t : 8 * t + 8, :] = now

    solve(
        rows // 8,
        (coef, hb, w, w2),
        lambda t: block_field(0, t),
        lambda t: mk[HALO + 8 * t : HALO + 8 * t + 8, :] > 0,
        block_field,
        block_keep,
    )
    for t in range(1, rows // 8 - 1):
        at = slice(8 * t, 8 * t + 8)
        dm[at, :] = block_field(1, t) * (
            w[0, at, :] * v_in[0, at, :] + w[1, at, :] * v_in[1, at, :]
        )

    for copy in copies:
        copy.wait_recv()

    def corners(e, left, right):
        at = pl.ds(8 * e, 8)
        for f in range(FIELDS):
            x = fm[f, at, :] if f < 6 else mk[at, :].astype(jnp.float32)
            own = jnp.where(lane < 32, x, pltpu.roll(x, 64, 1))
            far = jnp.where(
                lane < 96,
                pltpu.roll(right, (56 - 16 * f) % LANES, 1),
                pltpu.roll(left, (120 - 16 * f) % LANES, 1),
            )
            fs[f, at, :] = jnp.where(lane < 64, own, far)

    corners(0, diag[0], diag[1])
    corners(chunks - 1, diag[2], diag[3])
    blocks = [
        recv_t[:, :, part * LANES : (part + 1) * LANES].reshape(LANES, LANES).T
        for part in range(rows // LANES)
    ]

    def spread(t, _):
        packed = blocks[8 * t // LANES][8 * t % LANES : 8 * t % LANES + 8, :]
        return [pltpu.roll(packed, (120 - 8 * f) % LANES, 1) for f in range(FIELDS)]

    def put(t, turned):
        at = slice(8 * t, 8 * t + 8)
        for f in range(FIELDS):
            fs[f, HALO + 8 * t : HALO + 8 * t + 8, :] = jnp.where(
                lane < 64, beside[f, at, :], turned[f]
            )

    pipeline(rows // 8, 4, spread, put)

    ends = [0, 1, 2, chunks - 3, chunks - 2, chunks - 1]
    upper, lower, strips = 1, 4, len(ends)

    def place(t):
        return (fm, ends[t]) if t < strips else (fs, t - strips)

    def field(f, t):
        source, e = place(t)
        return source[f, 8 * e : 8 * e + 8, :]

    strip_inside = (
        (lane < 64)
        | ((lane < 96) & (col < n_col - 1))
        | ((lane >= 96) & (col > 0))
    )

    def inside(t):
        e = place(t)[1]
        mask = strip_inside if t >= strips else None
        if e == 0 or e == chunks - 1:
            there = jnp.broadcast_to(
                line > 0 if e == 0 else line < n_line - 1, (8, LANES)
            )
            mask = there if mask is None else mask & there
        return mask

    def n_of(t):
        mask = inside(t)
        return field(0, t) if mask is None else jnp.where(mask, field(0, t), 0.0)

    def ice_of(t):
        e = place(t)[1]
        ice = mk[8 * e : 8 * e + 8, :] > 0 if t < strips else field(6, t) > 0.5
        mask = inside(t)
        return ice if mask is None else ice & mask

    def keep(t, k, now):
        vx[k, 8 * t : 8 * t + 8, :] = now

    solve(strips + chunks, (coef, hb, w, w2), n_of, ice_of, field, keep)

    def product(t):
        at = slice(8 * t, 8 * t + 8)
        return field(1, t) * (
            w[0, at, :] * vx[0, at, :] + w[1, at, :] * vx[1, at, :]
        )

    def merged(strip, turned, base):
        return jnp.where(lane < 8, strip, jnp.where(lane >= 120, turned, base))

    def strip_product(t, _):
        strip = product(strips + 1 + t)
        return strip, pltpu.roll(strip, 64, 1)

    def put_product(t, given):
        if t == 0 or t == rows // 8 - 1:
            base = product(upper if t == 0 else lower)
        else:
            base = dm[8 * t : 8 * t + 8, :]
        u = 8 * t % TILE
        piece = merged(*given, base)
        if 8 * t < TILE:
            dens[u : u + 8, :] = -piece
        else:
            dens[u : u + 8, :] = dens[u : u + 8, :] - piece

    pipeline(rows // 8, 8, strip_product, put_product)

    for copy in loads[5:]:
        copy.wait()
    first = jnp.dot(
        b1[...], dens[...], precision=HIGHEST, preferred_element_type=jnp.float32
    )
    product_ = jnp.dot(
        first, b2[...], precision=HIGHEST, preferred_element_type=jnp.float32
    )
    part = product_[0:8]
    for i in range(1, PER):
        part = jnp.where(lane < i * MODES, part, product_[8 * i : 8 * i + 8])
    in_second = tb[0, 0] > 2 * line
    parts = jnp.where(in_second, 0.0, part), jnp.where(in_second, part, 0.0)
    per_share = 8 // SHARES
    for i in range(SHARES):
        for j in range(2):
            at = pl.ds(j * per_share, per_share)
            send_a[i, at, :] = parts[j][i * per_share : (i + 1) * per_share, :]

    def start(phase, src, dst, to):
        pltpu.make_async_remote_copy(
            src_ref=src,
            dst_ref=dst,
            send_sem=phase_send.at[phase],
            recv_sem=phase_recv.at[phase],
            device_id=to,
            device_id_type=MESH,
        ).start()

    def arrived(phase, ref):
        pltpu.make_async_copy(ref, ref, phase_recv.at[phase]).wait()

    def departed(phase, ref):
        pltpu.make_async_copy(ref, ref, phase_send.at[phase]).wait()

    share = lax.rem(col, SHARES)
    for i in col_steps:
        to = by(0, 0, i)
        start(0, send_a.at[lax.rem(to["col"], SHARES)], recv_a.at[col], to)
    recv_a[col] = send_a[share]

    def strip_velocity(t, _):
        found = []
        for k in range(2):
            at = 8 * (strips + 1 + t)
            strip = vx[k, at : at + 8, :]
            found.append((strip, pltpu.roll(strip, 64, 1)))
        return found

    def put_velocity(t, given):
        at = slice(8 * t, 8 * t + 8)
        for k in range(2):
            if t == 0 or t == rows // 8 - 1:
                e = 8 * (upper if t == 0 else lower)
                base = vx[k, e : e + 8, :]
            else:
                base = v_in[k, at, :]
            v[k, at, :] = merged(*given[k], base)

    pipeline(rows // 8, 8, strip_velocity, put_velocity)
    arrived(0, recv_a.at[0 : n_col - 1])
    total = recv_a[0]
    for i in range(1, n_col):
        total = total + recv_a[i]

    mine = table.at[pl.ds(2 * line, 2)]
    for j in range(2):
        table[2 * line + j] = total[j * per_share : (j + 1) * per_share, :]
    for i, j in plane_steps:
        start(1, mine, mine, by(i, j, 0))
    arrived(1, table.at[0 : 2 * n_line - 2])

    per_owner = ol.shape[0] // n_own
    width = per_share * LANES
    for k in range(per_owner):
        entry = table[ol[own_at * per_owner + k]]
        for j in range(per_share):
            at = pl.ds(pl.multiple_of(share * width + j * LANES, LANES), LANES)
            grad[0, k : k + 1, at] = entry[j : j + 1, :]

    mine_c = grad.at[0, :, pl.ds(pl.multiple_of(share * width, LANES), width)]
    for i in range(1, SHARES):
        to = {"row": row_at, "own": own_at, "col": lax.bitwise_xor(col, i)}
        start(2, mine_c, mine_c, to)
    arrived(2, grad.at[0, :, 0 : (SHARES - 1) * width])

    for copy in copies:
        copy.wait_send()
    departed(0, recv_a.at[0 : n_col - 1])
    departed(1, table.at[0 : 2 * n_line - 2])
    departed(2, grad.at[0, :, 0 : (SHARES - 1) * width])


def write_out(velocity, gradient, to_velocity, to_gradient, sem):
    copies = [
        pltpu.make_async_copy(velocity, to_velocity, sem.at[0]),
        pltpu.make_async_copy(gradient, to_gradient, sem.at[1]),
    ]
    for copy in copies:
        copy.start()
    for copy in copies:
        copy.wait()


def solution(mesh):
    sizes = tuple(mesh.shape[a] for a in ("row", "own", "col"))
    n_line, n_col = sizes[0] * sizes[1], sizes[2]

    def local(viscosity, friction, driving, observed, ice_mask, tile_block, owner_list):
        rows = viscosity.shape[0]
        ext = rows + 2 * HALO
        first, second = bases()
        per_owner = owner_list.shape[0] // sizes[1]
        f32 = jnp.float32
        vmem = pltpu.VMEM
        fields = (viscosity, friction, driving, observed, ice_mask)
        tile_block = tile_block.reshape(1, -1)
        small = (tile_block, owner_list, jnp.asarray(first), jnp.asarray(second))
        hbm = pl.BlockSpec(memory_space=pltpu.HBM)
        here = pl.BlockSpec(memory_space=pltpu.VMEM)
        dma = pltpu.SemaphoreType.DMA

        def pinned(operands):
            return [pltpu.with_memory_space_constraint(x, pltpu.HBM) for x in operands]

        results = pl.pallas_call(
            functools.partial(kernel, sizes),
            out_shape=(
                jax.ShapeDtypeStruct((2, rows, LANES), f32),
                jax.ShapeDtypeStruct((1, per_owner, MODES * MODES), f32),
            ),
            in_specs=[hbm] * 9,
            out_specs=[here] * 2,
            scratch_shapes=[
                vmem((6, ext, LANES), f32),
                vmem((ext, LANES), jnp.int32),
                vmem((16, 8, rows), f32),
                vmem((4, 8, LANES), f32),
                vmem((FIELDS, rows, LANES), f32),
                vmem((2, rows, LANES), f32),
                vmem((rows, LANES), f32),
                vmem((rows, LANES), f32),
                vmem((8, 16, rows), f32),
                vmem((FIELDS, ext, LANES), f32),
                vmem((4, ext + 48, LANES), f32),
                vmem((2, ext + 48, LANES), f32),
                vmem((4, ext + 56, LANES), f32),
                vmem((4, ext + 56, LANES), f32),
                vmem((2, ext + 48, LANES), f32),
                vmem((TILE, LANES), f32),
                vmem(first.shape, f32),
                vmem(second.shape, f32),
                pltpu.SMEM(tile_block.shape, jnp.int32),
                pltpu.SMEM(owner_list.shape, jnp.int32),
                vmem((SHARES, 2 * 8 // SHARES, LANES), f32),
                vmem((n_col, 2 * 8 // SHARES, LANES), f32),
                vmem((2 * n_line, 8 // SHARES, LANES), f32),
                dma((9,)),
                dma((10,)),
                dma((10,)),
                dma((3,)),
                dma((3,)),
            ],
            compiler_params=pltpu.CompilerParams(
                collective_id=0,
                has_side_effects=True,
                vmem_limit_bytes=32 * 2**20,
            ),
        )(*pinned(fields + small))
        return pl.pallas_call(
            write_out,
            out_shape=[jax.ShapeDtypeStruct(x.shape, f32) for x in results],
            in_specs=[here] * 2,
            out_specs=[hbm] * 2,
            scratch_shapes=[dma((2,))],
            compiler_params=pltpu.CompilerParams(vmem_limit_bytes=2**20),
        )(*results)

    return jax.shard_map(
        local,
        mesh=mesh,
        in_specs=(
            P(("row", "own"), "col"),
            P(("row", "own"), "col"),
            P(None, ("row", "own"), "col"),
            P(None, ("row", "own"), "col"),
            P(("row", "own"), "col"),
            P(("row", "own"), "col"),
            P(),
        ),
        out_specs=(P(None, ("row", "own"), "col"), P("own", None, None)),
        check_vma=False,
    )
```

```python
import functools
import math

import jax
import jax.numpy as jnp
import numpy as np
from jax import lax
from jax.experimental import pallas as pl
from jax.experimental.pallas import tpu as pltpu
from jax.sharding import PartitionSpec as P

TILE = 128
MODES = 32
LANES = 128
HALO = 8
FIELDS = 7
SWEEPS = 3
PER = LANES // MODES
SHARES = 4
LAG = 12
MESH = pl.DeviceIdType.MESH
HIGHEST = lax.Precision.HIGHEST


def bases():
    places = np.arange(TILE) + 0.5
    orders = np.arange(MODES)
    cosine = np.cos(math.pi * orders[:, None] * places[None, :] / TILE)
    first = np.concatenate([cosine[s::PER] for s in range(PER)], axis=0)
    second = np.concatenate([cosine.T / TILE] * PER, axis=1)
    return first.astype(np.float32), second.astype(np.float32)


def around(step, size):
    return min(step % size, -step % size)


def wrapped(x, size):
    if size & (size - 1) == 0:
        return lax.bitwise_and(x, size - 1)
    return lax.rem(x + size, size)


def quotient(x, size):
    if size & (size - 1) == 0:
        return lax.shift_right_logical(x, size.bit_length() - 1)
    return lax.div(x, size)


def pipeline(count, lag, *stages):
    held = {}
    for step in range(count + lag * (len(stages) - 1)):
        for i, stage in reversed(list(enumerate(stages))):
            t = step - i * lag
            if 0 <= t < count:
                held[t] = stage(t, held.pop(t, None))


def solve(chunks, refs, n_of, ice_of, field, keep):
    coef, hb, w, w2 = refs
    first_sub = lax.broadcasted_iota(jnp.int32, (8, LANES), 0) == 0
    zero = jnp.zeros((8, LANES), jnp.float32)

    def rows_of(t):
        return slice(8 * t, 8 * t + 8)

    def down(x, kept):
        turned = pltpu.roll(x, 1, 0)
        return jnp.where(first_sub, kept, turned), turned

    def store_state(to, t, k, now):
        to[k, rows_of(t), :] = now
        return pltpu.roll(now, LANES - 1, 1)

    def store_ahead(to):
        def stage(t, turned):
            for k in range(2):
                to[2 + k, rows_of(t), :] = turned[k]

        return stage

    def open_(t, _):
        n = n_of(t)
        return n, pltpu.roll(n, 1, 1)

    summed_kept = [zero]

    def settle(t, given):
        n, turned = given
        at = rows_of(t)
        summed = n + turned
        moved, summed_kept[0] = down(summed, summed_kept[0])
        f = field(1, t)
        half = jnp.where(ice_of(t), 0.5 / (1.25 * (summed + moved) + f), 0.0)
        coef[0, at, :] = 0.5 * n
        coef[1, at, :] = 0.25 * n
        coef[2, at, :] = half
        coef[3, at, :] = 1.0 - half * f
        out = []
        for k in range(2):
            scaled = half * field(2 + k, t)
            hb[k, at, :] = scaled
            out.append(store_state(w, t, k, scaled + scaled))
        return out

    pipeline(chunks, LAG, open_, settle, store_ahead(w))
    for k in range(4):
        w[k, rows_of(chunks), :] = zero
        w2[k, rows_of(chunks), :] = zero

    def turn():
        def begin(t, _):
            at = rows_of(t)
            out = []
            for k in range(2):
                now = w2[k, at, :]
                keep(t, k, now)
                scaled = coef[2, at, :] * (now - field(4 + k, t))
                hb[k, at, :] = scaled
                out.append(store_state(w2, t, k, scaled + scaled))
            return out

        pipeline(chunks, LAG, begin, store_ahead(w2))

    def sweep(w_from, w_to):
        kept = [zero] * 4

        def front(t, _):
            at, after = rows_of(t), slice(8 * t + 1, 8 * t + 9)
            dx, dy = [], []
            for k in range(2):
                here, here_next = w_from[k, at, :], w_from[2 + k, at, :]
                below, below_next = w_from[k, after, :], w_from[2 + k, after, :]
                dx.append((below - here) + (below_next - here_next))
                dy.append((here_next + below_next) - (here + below))
            m, q = coef[0, at, :], coef[1, at, :]
            total = dx[0] + dy[1]
            one = m * (total + dx[0])
            two = m * (total + dy[1])
            shear = q * (dy[0] + dx[1])
            fields = (one + shear, one - shear, two + shear, shear - two)
            moved = []
            for i in range(4):
                got, kept[i] = down(fields[i], kept[i])
                moved.append(got)
            stay = (moved[1] - fields[0], moved[3] - fields[2])
            go = (moved[0] - fields[1], moved[2] - fields[3])
            return stay, tuple(pltpu.roll(x, 1, 1) for x in go)

        def close(t, given):
            at = rows_of(t)
            turned = []
            for k in range(2):
                image = given[0][k] + given[1][k]
                now = (
                    coef[3, at, :] * w_from[k, at, :] + hb[k, at, :]
                ) - coef[2, at, :] * image
                turned.append(store_state(w_to, t, k, now))
            return turned

        pipeline(chunks, LAG, front, close, store_ahead(w_to))

    def pair(s, _):
        sweep(w, w2)

        @pl.when(s == 1)
        def _():
            turn()

        sweep(w2, w)
        return 0

    lax.fori_loop(0, SWEEPS, pair, 0)


def kernel(
    sizes,
    visc,
    fric,
    drv,
    obs,
    mask,
    tile_block,
    owner_list,
    basis_1,
    basis_2,
    v,
    grad,
    fm,
    mk,
    recv_t,
    diag,
    beside,
    v_in,
    dm,
    pack,
    pack_t,
    fs,
    coef,
    hb,
    w,
    w2,
    vx,
    dens,
    b1,
    b2,
    tb,
    ol,
    send_a,
    recv_a,
    table,
    load_sem,
    halo_send,
    halo_recv,
    phase_send,
    phase_recv,
):
    n_row, n_own, n_col = sizes
    n_line = n_row * n_own
    rows = visc.shape[0]
    chunks = (rows + 2 * HALO) // 8
    row_at, own_at, col = (
        lax.axis_index("row"),
        lax.axis_index("own"),
        lax.axis_index("col"),
    )
    line = row_at * n_own + own_at

    row_by = [wrapped(row_at + i, n_row) for i in range(n_row)]
    own_by = [wrapped(own_at + i, n_own) for i in range(n_own)]
    col_by = [wrapped(col + i, n_col) for i in range(n_col)]

    def by(rows_on, owns_on, cols_on):
        return {
            "row": row_by[rows_on],
            "own": own_by[owns_on],
            "col": col_by[cols_on],
        }

    line_by = {i: wrapped(line + i, n_line) for i in (-1, 1)}
    line_by = {
        i: (quotient(to, n_own), wrapped(to, n_own)) for i, to in line_by.items()
    }

    def next_to(line_on, cols_on):
        return {
            "row": line_by[line_on][0],
            "own": line_by[line_on][1],
            "col": col_by[cols_on],
        }

    col_steps = sorted(range(1, n_col), key=lambda i: -around(i, n_col))
    plane_steps = [(i, j) for i in range(n_row) for j in range(n_own) if i or j]
    plane_steps.sort(key=lambda s: -(around(s[0], n_row) + around(s[1], n_own)))

    barrier = pltpu.get_barrier_semaphore()
    greeted = [by(i, j, 0) for i, j in plane_steps]
    greeted += [by(0, 0, i) for i in col_steps]
    greeted += [next_to(i, j) for i in (-1, 1) for j in (-1, 1)]
    for to in greeted:
        pl.semaphore_signal(barrier, inc=1, device_id=to, device_id_type=MESH)

    own_rows = pl.ds(HALO, rows)
    loads = [
        (visc, fm.at[0, own_rows, :]),
        (fric, fm.at[1, own_rows, :]),
        (drv, fm.at[2:4, own_rows, :]),
        (obs, fm.at[4:6, own_rows, :]),
        (mask, mk.at[own_rows, :]),
        (basis_1, b1),
        (basis_2, b2),
        (tile_block, tb),
        (owner_list, ol),
    ]
    loads = [
        pltpu.make_async_copy(src, dst, load_sem.at[i])
        for i, (src, dst) in enumerate(loads)
    ]
    for copy in loads:
        copy.start()

    lane = lax.broadcasted_iota(jnp.int32, (8, LANES), 1)

    for copy in loads[:5]:
        copy.wait()

    def gather(t, _):
        at = pl.ds(HALO + 8 * t, 8)
        found = [fm[f, at, :] for f in range(6)] + [mk[at, :].astype(jnp.float32)]
        return [pltpu.roll(piece, 16 * f + 8, 1) for f, piece in enumerate(found)]

    def merge(t, pieces):
        packed = pieces[0]
        for f in range(1, FIELDS):
            packed = jnp.where(lane < 16 * f, packed, pieces[f])
        pack[8 * t : 8 * t + 8, :] = packed

    pipeline(rows // 8, 4, gather, merge)
    for part in range(rows // LANES):
        block = pack[part * LANES : (part + 1) * LANES, :]
        pack_t[:, :, part * LANES : (part + 1) * LANES] = block.T.reshape(8, 16, LANES)
    recv_t[FIELDS : 16 - FIELDS] = jnp.zeros((2, 8, rows), jnp.float32)

    pl.semaphore_wait(barrier, len(greeted))
    copies = []

    def send(src, dst, to):
        at = len(copies)
        copy = pltpu.make_async_remote_copy(
            src_ref=src,
            dst_ref=dst,
            send_sem=halo_send.at[at],
            recv_sem=halo_recv.at[at],
            device_id=to,
            device_id_type=MESH,
        )
        copy.start()
        copies.append(copy)

    for line_on, source, slot in ((-1, 0, 2), (1, rows - 8, 0)):
        for cols_on in (-1, 1):
            send(
                pack.at[pl.ds(source, 8), :],
                diag.at[slot + (1 if cols_on < 0 else 0)],
                next_to(line_on, cols_on),
            )
    send(pack_t.at[0:FIELDS, 0:8, :], recv_t.at[0:FIELDS], by(0, 0, 1))
    send(pack_t.at[0:FIELDS, 8:16, :], recv_t.at[16 - FIELDS : 16], by(0, 0, -1))
    for line_on, source, target in ((-1, HALO, HALO + rows), (1, rows, 0)):
        to, take = pl.ds(target, HALO), pl.ds(source, HALO)
        send(fm.at[:, take, :], fm.at[:, to, :], next_to(line_on, 0))
        send(mk.at[take, :], mk.at[to, :], next_to(line_on, 0))

    def turn_half(t, _):
        at = pl.ds(HALO + 8 * t, 8)
        found = [fm[f, at, :] for f in range(6)] + [mk[at, :].astype(jnp.float32)]
        return [(x, pltpu.roll(x, 64, 1)) for x in found]

    def put_half(t, pieces):
        for f, (x, turned) in enumerate(pieces):
            beside[f, 8 * t : 8 * t + 8, :] = jnp.where(lane < 32, x, turned)

    pipeline(rows // 8, 2, turn_half, put_half)

    def block_field(f, t):
        return fm[f, HALO + 8 * t : HALO + 8 * t + 8, :]

    def block_keep(t, k, now):
        v_in[k, 8 * t : 8 * t + 8, :] = now

    solve(
        rows // 8,
        (coef, hb, w, w2),
        lambda t: block_field(0, t),
        lambda t: mk[HALO + 8 * t : HALO + 8 * t + 8, :] > 0,
        block_field,
        block_keep,
    )
    for t in range(1, rows // 8 - 1):
        at = slice(8 * t, 8 * t + 8)
        dm[at, :] = block_field(1, t) * (
            w[0, at, :] * v_in[0, at, :] + w[1, at, :] * v_in[1, at, :]
        )

    for copy in copies:
        copy.wait_recv()

    def corners(e, left, right):
        at = pl.ds(8 * e, 8)
        for f in range(FIELDS):
            x = fm[f, at, :] if f < 6 else mk[at, :].astype(jnp.float32)
            own = jnp.where(lane < 32, x, pltpu.roll(x, 64, 1))
            far = jnp.where(
                lane < 96,
                pltpu.roll(right, (56 - 16 * f) % LANES, 1),
                pltpu.roll(left, (120 - 16 * f) % LANES, 1),
            )
            fs[f, at, :] = jnp.where(lane < 64, own, far)

    corners(0, diag[0], diag[1])
    corners(chunks - 1, diag[2], diag[3])
    blocks = [
        recv_t[:, :, part * LANES : (part + 1) * LANES].reshape(LANES, LANES).T
        for part in range(rows // LANES)
    ]

    def spread(t, _):
        packed = blocks[8 * t // LANES][8 * t % LANES : 8 * t % LANES + 8, :]
        return [pltpu.roll(packed, (120 - 8 * f) % LANES, 1) for f in range(FIELDS)]

    def put(t, turned):
        at = slice(8 * t, 8 * t + 8)
        for f in range(FIELDS):
            fs[f, HALO + 8 * t : HALO + 8 * t + 8, :] = jnp.where(
                lane < 64, beside[f, at, :], turned[f]
            )

    pipeline(rows // 8, 4, spread, put)

    ends = [0, 1, 2, chunks - 3, chunks - 2, chunks - 1]
    upper, lower, strips = 1, 4, len(ends)

    def place(t):
        return (fm, ends[t]) if t < strips else (fs, t - strips)

    def field(f, t):
        source, e = place(t)
        return source[f, 8 * e : 8 * e + 8, :]

    strip_inside = (
        (lane < 64)
        | ((lane < 96) & (col < n_col - 1))
        | ((lane >= 96) & (col > 0))
    )

    def inside(t):
        e = place(t)[1]
        mask = strip_inside if t >= strips else None
        if e == 0 or e == chunks - 1:
            there = jnp.broadcast_to(
                line > 0 if e == 0 else line < n_line - 1, (8, LANES)
            )
            mask = there if mask is None else mask & there
        return mask

    def n_of(t):
        mask = inside(t)
        return field(0, t) if mask is None else jnp.where(mask, field(0, t), 0.0)

    def ice_of(t):
        e = place(t)[1]
        ice = mk[8 * e : 8 * e + 8, :] > 0 if t < strips else field(6, t) > 0.5
        mask = inside(t)
        return ice if mask is None else ice & mask

    def keep(t, k, now):
        vx[k, 8 * t : 8 * t + 8, :] = now

    solve(strips + chunks, (coef, hb, w, w2), n_of, ice_of, field, keep)

    def product(t):
        at = slice(8 * t, 8 * t + 8)
        return field(1, t) * (
            w[0, at, :] * vx[0, at, :] + w[1, at, :] * vx[1, at, :]
        )

    def merged(strip, turned, base):
        return jnp.where(lane < 8, strip, jnp.where(lane >= 120, turned, base))

    def strip_product(t, _):
        strip = product(strips + 1 + t)
        return strip, pltpu.roll(strip, 64, 1)

    def put_product(t, given):
        if t == 0 or t == rows // 8 - 1:
            base = product(upper if t == 0 else lower)
        else:
            base = dm[8 * t : 8 * t + 8, :]
        u = 8 * t % TILE
        piece = merged(*given, base)
        if 8 * t < TILE:
            dens[u : u + 8, :] = -piece
        else:
            dens[u : u + 8, :] = dens[u : u + 8, :] - piece

    pipeline(rows // 8, 8, strip_product, put_product)

    for copy in loads[5:]:
        copy.wait()
    first = jnp.dot(
        b1[...], dens[...], precision=HIGHEST, preferred_element_type=jnp.float32
    )
    product_ = jnp.dot(
        first, b2[...], precision=HIGHEST, preferred_element_type=jnp.float32
    )
    part = product_[0:8]
    for i in range(1, PER):
        part = jnp.where(lane < i * MODES, part, product_[8 * i : 8 * i + 8])
    in_second = tb[0, 0] > 2 * line
    parts = jnp.where(in_second, 0.0, part), jnp.where(in_second, part, 0.0)
    per_share = 8 // SHARES
    for i in range(SHARES):
        for j in range(2):
            at = pl.ds(j * per_share, per_share)
            send_a[i, at, :] = parts[j][i * per_share : (i + 1) * per_share, :]

    def start(phase, src, dst, to):
        pltpu.make_async_remote_copy(
            src_ref=src,
            dst_ref=dst,
            send_sem=phase_send.at[phase],
            recv_sem=phase_recv.at[phase],
            device_id=to,
            device_id_type=MESH,
        ).start()

    def arrived(phase, ref):
        pltpu.make_async_copy(ref, ref, phase_recv.at[phase]).wait()

    def departed(phase, ref):
        pltpu.make_async_copy(ref, ref, phase_send.at[phase]).wait()

    share = wrapped(col, SHARES)
    for i in col_steps:
        to = by(0, 0, i)
        start(0, send_a.at[wrapped(to["col"], SHARES)], recv_a.at[col], to)
    recv_a[col] = send_a[share]

    def strip_velocity(t, _):
        found = []
        for k in range(2):
            at = 8 * (strips + 1 + t)
            strip = vx[k, at : at + 8, :]
            found.append((strip, pltpu.roll(strip, 64, 1)))
        return found

    def put_velocity(t, given):
        at = slice(8 * t, 8 * t + 8)
        for k in range(2):
            if t == 0 or t == rows // 8 - 1:
                e = 8 * (upper if t == 0 else lower)
                base = vx[k, e : e + 8, :]
            else:
                base = v_in[k, at, :]
            v[k, at, :] = merged(*given[k], base)

    pipeline(rows // 8, 8, strip_velocity, put_velocity)
    arrived(0, recv_a.at[0 : n_col - 1])
    total = recv_a[0]
    for i in range(1, n_col):
        total = total + recv_a[i]

    mine = table.at[pl.ds(2 * line, 2)]
    for j in range(2):
        table[2 * line + j] = total[j * per_share : (j + 1) * per_share, :]
    for i, j in plane_steps:
        start(1, mine, mine, by(i, j, 0))
    arrived(1, table.at[0 : 2 * n_line - 2])

    per_owner = ol.shape[0] // n_own
    width = per_share * LANES
    for k in range(per_owner):
        entry = table[ol[own_at * per_owner + k]]
        for j in range(per_share):
            at = pl.ds(pl.multiple_of(share * width + j * LANES, LANES), LANES)
            grad[0, k : k + 1, at] = entry[j : j + 1, :]

    mine_c = grad.at[0, :, pl.ds(pl.multiple_of(share * width, LANES), width)]
    for i in range(1, SHARES):
        to = {"row": row_at, "own": own_at, "col": lax.bitwise_xor(col, i)}
        start(2, mine_c, mine_c, to)
    arrived(2, grad.at[0, :, 0 : (SHARES - 1) * width])

    for copy in copies:
        copy.wait_send()
    departed(0, recv_a.at[0 : n_col - 1])
    departed(1, table.at[0 : 2 * n_line - 2])
    departed(2, grad.at[0, :, 0 : (SHARES - 1) * width])


def write_out(velocity, gradient, to_velocity, to_gradient, sem):
    copies = [
        pltpu.make_async_copy(velocity, to_velocity, sem.at[0]),
        pltpu.make_async_copy(gradient, to_gradient, sem.at[1]),
    ]
    for copy in copies:
        copy.start()
    for copy in copies:
        copy.wait()


def solution(mesh):
    sizes = tuple(mesh.shape[a] for a in ("row", "own", "col"))
    n_line, n_col = sizes[0] * sizes[1], sizes[2]

    def local(viscosity, friction, driving, observed, ice_mask, tile_block, owner_list):
        rows = viscosity.shape[0]
        ext = rows + 2 * HALO
        first, second = bases()
        per_owner = owner_list.shape[0] // sizes[1]
        f32 = jnp.float32
        vmem = pltpu.VMEM
        fields = (viscosity, friction, driving, observed, ice_mask)
        tile_block = tile_block.reshape(1, -1)
        small = (tile_block, owner_list, jnp.asarray(first), jnp.asarray(second))
        hbm = pl.BlockSpec(memory_space=pltpu.HBM)
        here = pl.BlockSpec(memory_space=pltpu.VMEM)
        dma = pltpu.SemaphoreType.DMA

        def pinned(operands):
            return [pltpu.with_memory_space_constraint(x, pltpu.HBM) for x in operands]

        results = pl.pallas_call(
            functools.partial(kernel, sizes),
            out_shape=(
                jax.ShapeDtypeStruct((2, rows, LANES), f32),
                jax.ShapeDtypeStruct((1, per_owner, MODES * MODES), f32),
            ),
            in_specs=[hbm] * 9,
            out_specs=[here] * 2,
            scratch_shapes=[
                vmem((6, ext, LANES), f32),
                vmem((ext, LANES), jnp.int32),
                vmem((16, 8, rows), f32),
                vmem((4, 8, LANES), f32),
                vmem((FIELDS, rows, LANES), f32),
                vmem((2, rows, LANES), f32),
                vmem((rows, LANES), f32),
                vmem((rows, LANES), f32),
                vmem((8, 16, rows), f32),
                vmem((FIELDS, ext, LANES), f32),
                vmem((4, ext + 48, LANES), f32),
                vmem((2, ext + 48, LANES), f32),
                vmem((4, ext + 56, LANES), f32),
                vmem((4, ext + 56, LANES), f32),
                vmem((2, ext + 48, LANES), f32),
                vmem((TILE, LANES), f32),
                vmem(first.shape, f32),
                vmem(second.shape, f32),
                pltpu.SMEM(tile_block.shape, jnp.int32),
                pltpu.SMEM(owner_list.shape, jnp.int32),
                vmem((SHARES, 2 * 8 // SHARES, LANES), f32),
                vmem((n_col, 2 * 8 // SHARES, LANES), f32),
                vmem((2 * n_line, 8 // SHARES, LANES), f32),
                dma((9,)),
                dma((10,)),
                dma((10,)),
                dma((3,)),
                dma((3,)),
            ],
            compiler_params=pltpu.CompilerParams(
                collective_id=0,
                has_side_effects=True,
                vmem_limit_bytes=32 * 2**20,
            ),
        )(*pinned(fields + small))
        return pl.pallas_call(
            write_out,
            out_shape=[jax.ShapeDtypeStruct(x.shape, f32) for x in results],
            in_specs=[here] * 2,
            out_specs=[hbm] * 2,
            scratch_shapes=[dma((2,))],
            compiler_params=pltpu.CompilerParams(vmem_limit_bytes=2**20),
        )(*results)

    return jax.shard_map(
        local,
        mesh=mesh,
        in_specs=(
            P(("row", "own"), "col"),
            P(("row", "own"), "col"),
            P(None, ("row", "own"), "col"),
            P(None, ("row", "own"), "col"),
            P(("row", "own"), "col"),
            P(("row", "own"), "col"),
            P(),
        ),
        out_specs=(P(None, ("row", "own"), "col"), P("own", None, None)),
        check_vma=False,
    )
```

```python
import functools
import math

import jax
import jax.numpy as jnp
import numpy as np
from jax import lax
from jax.experimental import pallas as pl
from jax.experimental.pallas import tpu as pltpu
from jax.sharding import PartitionSpec as P

TILE = 128
MODES = 32
LANES = 128
HALO = 8
FIELDS = 7
SWEEPS = 3
PER = LANES // MODES
SHARES = 4
LAG = 12
MESH = pl.DeviceIdType.MESH
HIGHEST = lax.Precision.HIGHEST


def bases():
    places = np.arange(TILE) + 0.5
    orders = np.arange(MODES)
    cosine = np.cos(math.pi * orders[:, None] * places[None, :] / TILE)
    first = np.concatenate([cosine[s::PER] for s in range(PER)], axis=0)
    second = np.concatenate([cosine.T / TILE] * PER, axis=1)
    return first.astype(np.float32), second.astype(np.float32)


def around(step, size):
    return min(step % size, -step % size)


def wrapped(x, size):
    if size & (size - 1) == 0:
        return lax.bitwise_and(x, size - 1)
    return lax.rem(x + size, size)


def quotient(x, size):
    if size & (size - 1) == 0:
        return lax.shift_right_logical(x, size.bit_length() - 1)
    return lax.div(x, size)


def pipeline(count, lag, *stages):
    held = {}
    for step in range(count + lag * (len(stages) - 1)):
        for i, stage in reversed(list(enumerate(stages))):
            t = step - i * lag
            if 0 <= t < count:
                held[t] = stage(t, held.pop(t, None))


def solve(chunks, refs, n_of, ice_of, field, keep):
    coef, hb, w, w2 = refs
    first_sub = lax.broadcasted_iota(jnp.int32, (8, LANES), 0) == 0
    zero = jnp.zeros((8, LANES), jnp.float32)

    def rows_of(t):
        return slice(8 * t, 8 * t + 8)

    def down(x, kept):
        turned = pltpu.roll(x, 1, 0)
        return jnp.where(first_sub, kept, turned), turned

    def store_state(to, t, k, now):
        to[k, rows_of(t), :] = now
        return pltpu.roll(now, LANES - 1, 1)

    def store_ahead(to):
        def stage(t, turned):
            for k in range(2):
                to[2 + k, rows_of(t), :] = turned[k]

        return stage

    def open_(t, _):
        n = n_of(t)
        return n, pltpu.roll(n, 1, 1)

    summed_kept = [zero]

    def settle(t, given):
        n, turned = given
        at = rows_of(t)
        summed = n + turned
        moved, summed_kept[0] = down(summed, summed_kept[0])
        f = field(1, t)
        half = jnp.where(ice_of(t), 0.5 / (1.25 * (summed + moved) + f), 0.0)
        coef[0, at, :] = 0.5 * n
        coef[1, at, :] = 0.25 * n
        coef[2, at, :] = half
        coef[3, at, :] = 1.0 - half * f
        out = []
        for k in range(2):
            scaled = half * field(2 + k, t)
            hb[k, at, :] = scaled
            out.append(store_state(w, t, k, scaled + scaled))
        return out

    pipeline(chunks, LAG, open_, settle, store_ahead(w))
    for k in range(4):
        w[k, rows_of(chunks), :] = zero
        w2[k, rows_of(chunks), :] = zero

    def turn():
        def begin(t, _):
            at = rows_of(t)
            out = []
            for k in range(2):
                now = w2[k, at, :]
                keep(t, k, now)
                scaled = coef[2, at, :] * (now - field(4 + k, t))
                hb[k, at, :] = scaled
                out.append(store_state(w2, t, k, scaled + scaled))
            return out

        pipeline(chunks, LAG, begin, store_ahead(w2))

    def sweep(w_from, w_to):
        kept = [zero] * 4

        def front(t, _):
            at, after = rows_of(t), slice(8 * t + 1, 8 * t + 9)
            dx, dy = [], []
            for k in range(2):
                here, here_next = w_from[k, at, :], w_from[2 + k, at, :]
                below, below_next = w_from[k, after, :], w_from[2 + k, after, :]
                dx.append((below - here) + (below_next - here_next))
                dy.append((here_next + below_next) - (here + below))
            m, q = coef[0, at, :], coef[1, at, :]
            total = dx[0] + dy[1]
            one = m * (total + dx[0])
            two = m * (total + dy[1])
            shear = q * (dy[0] + dx[1])
            fields = (one + shear, one - shear, two + shear, shear - two)
            moved = []
            for i in range(4):
                got, kept[i] = down(fields[i], kept[i])
                moved.append(got)
            stay = (moved[1] - fields[0], moved[3] - fields[2])
            go = (moved[0] - fields[1], moved[2] - fields[3])
            return stay, tuple(pltpu.roll(x, 1, 1) for x in go)

        def close(t, given):
            at = rows_of(t)
            turned = []
            for k in range(2):
                image = given[0][k] + given[1][k]
                now = (
                    coef[3, at, :] * w_from[k, at, :] + hb[k, at, :]
                ) - coef[2, at, :] * image
                turned.append(store_state(w_to, t, k, now))
            return turned

        pipeline(chunks, LAG, front, close, store_ahead(w_to))

    def pair(s, _):
        sweep(w, w2)

        @pl.when(s == 1)
        def _():
            turn()

        sweep(w2, w)
        return 0

    lax.fori_loop(0, SWEEPS, pair, 0)


def exchange(
    sizes,
    visc,
    fric,
    drv,
    obs,
    mask,
    fm,
    mk,
    recv_t,
    diag,
    beside,
    v,
    dm,
    pack,
    pack_t,
    coef,
    hb,
    w,
    w2,
    load_sem,
    halo_send,
    halo_recv,
):
    n_row, n_own, n_col = sizes
    n_line = n_row * n_own
    rows = visc.shape[0]
    row_at, own_at, col = (
        lax.axis_index("row"),
        lax.axis_index("own"),
        lax.axis_index("col"),
    )
    line = row_at * n_own + own_at

    row_by = [wrapped(row_at + i, n_row) for i in range(n_row)]
    own_by = [wrapped(own_at + i, n_own) for i in range(n_own)]
    col_by = [wrapped(col + i, n_col) for i in range(n_col)]

    def by(rows_on, owns_on, cols_on):
        return {
            "row": row_by[rows_on],
            "own": own_by[owns_on],
            "col": col_by[cols_on],
        }

    line_by = {i: wrapped(line + i, n_line) for i in (-1, 1)}
    line_by = {
        i: (quotient(to, n_own), wrapped(to, n_own)) for i, to in line_by.items()
    }

    def next_to(line_on, cols_on):
        return {
            "row": line_by[line_on][0],
            "own": line_by[line_on][1],
            "col": col_by[cols_on],
        }

    own_rows = pl.ds(HALO, rows)
    loads = [
        (visc, fm.at[0, own_rows, :]),
        (fric, fm.at[1, own_rows, :]),
        (drv, fm.at[2:4, own_rows, :]),
        (obs, fm.at[4:6, own_rows, :]),
        (mask, mk.at[own_rows, :]),
    ]
    loads = [
        pltpu.make_async_copy(src, dst, load_sem.at[i])
        for i, (src, dst) in enumerate(loads)
    ]
    for copy in loads:
        copy.start()

    barrier = pltpu.get_barrier_semaphore()
    greeted = [next_to(i, j) for i in (-1, 1) for j in (-1, 0, 1)]
    greeted += [by(0, 0, i) for i in (-1, 1)]
    for to in greeted:
        pl.semaphore_signal(barrier, inc=1, device_id=to, device_id_type=MESH)

    lane = lax.broadcasted_iota(jnp.int32, (8, LANES), 1)

    for copy in loads:
        copy.wait()

    def gather(t, _):
        at = pl.ds(HALO + 8 * t, 8)
        found = [fm[f, at, :] for f in range(6)] + [mk[at, :].astype(jnp.float32)]
        return [pltpu.roll(piece, 16 * f + 8, 1) for f, piece in enumerate(found)]

    def merge(t, pieces):
        packed = pieces[0]
        for f in range(1, FIELDS):
            packed = jnp.where(lane < 16 * f, packed, pieces[f])
        pack[8 * t : 8 * t + 8, :] = packed

    pipeline(rows // 8, 4, gather, merge)
    for part in range(rows // LANES):
        block = pack[part * LANES : (part + 1) * LANES, :]
        pack_t[:, :, part * LANES : (part + 1) * LANES] = block.T.reshape(8, 16, LANES)
    recv_t[FIELDS : 16 - FIELDS] = jnp.zeros((2, 8, rows), jnp.float32)

    pl.semaphore_wait(barrier, len(greeted))
    copies = []

    def send(src, dst, to):
        at = len(copies)
        copy = pltpu.make_async_remote_copy(
            src_ref=src,
            dst_ref=dst,
            send_sem=halo_send.at[at],
            recv_sem=halo_recv.at[at],
            device_id=to,
            device_id_type=MESH,
        )
        copy.start()
        copies.append(copy)

    for line_on, source, slot in ((-1, 0, 2), (1, rows - 8, 0)):
        for cols_on in (-1, 1):
            send(
                pack.at[pl.ds(source, 8), :],
                diag.at[slot + (1 if cols_on < 0 else 0)],
                next_to(line_on, cols_on),
            )
    send(pack_t.at[0:FIELDS, 0:8, :], recv_t.at[0:FIELDS], by(0, 0, 1))
    send(pack_t.at[0:FIELDS, 8:16, :], recv_t.at[16 - FIELDS : 16], by(0, 0, -1))
    for line_on, source, target in ((-1, HALO, HALO + rows), (1, rows, 0)):
        to, take = pl.ds(target, HALO), pl.ds(source, HALO)
        send(fm.at[:, take, :], fm.at[:, to, :], next_to(line_on, 0))
        send(mk.at[take, :], mk.at[to, :], next_to(line_on, 0))

    def turn_half(t, _):
        at = pl.ds(HALO + 8 * t, 8)
        found = [fm[f, at, :] for f in range(6)] + [mk[at, :].astype(jnp.float32)]
        return [(x, pltpu.roll(x, 64, 1)) for x in found]

    def put_half(t, pieces):
        for f, (x, turned) in enumerate(pieces):
            beside[f, 8 * t : 8 * t + 8, :] = jnp.where(lane < 32, x, turned)

    pipeline(rows // 8, 2, turn_half, put_half)

    def field(f, t):
        return fm[f, HALO + 8 * t : HALO + 8 * t + 8, :]

    def keep(t, k, now):
        v[k, 8 * t : 8 * t + 8, :] = now

    solve(
        rows // 8,
        (coef, hb, w, w2),
        lambda t: field(0, t),
        lambda t: mk[HALO + 8 * t : HALO + 8 * t + 8, :] > 0,
        field,
        keep,
    )
    for t in range(1, rows // 8 - 1):
        at = slice(8 * t, 8 * t + 8)
        dm[at, :] = field(1, t) * (
            w[0, at, :] * v[0, at, :] + w[1, at, :] * v[1, at, :]
        )

    for copy in copies:
        copy.wait()


def kernel(
    sizes,
    fm,
    mk,
    recv_t,
    diag,
    beside,
    v_in,
    dm,
    tile_block,
    owner_list,
    basis_1,
    basis_2,
    v,
    grad,
    fs,
    coef,
    hb,
    w,
    w2,
    vx,
    dens,
    b1,
    b2,
    tb,
    ol,
    send_a,
    recv_a,
    table,
    load_sem,
    phase_send,
    phase_recv,
):
    n_row, n_own, n_col = sizes
    n_line = n_row * n_own
    rows = fm.shape[1] - 2 * HALO
    chunks = (rows + 2 * HALO) // 8
    row_at, own_at, col = (
        lax.axis_index("row"),
        lax.axis_index("own"),
        lax.axis_index("col"),
    )
    line = row_at * n_own + own_at

    row_by = [wrapped(row_at + i, n_row) for i in range(n_row)]
    own_by = [wrapped(own_at + i, n_own) for i in range(n_own)]
    col_by = [wrapped(col + i, n_col) for i in range(n_col)]

    def by(rows_on, owns_on, cols_on):
        return {
            "row": row_by[rows_on],
            "own": own_by[owns_on],
            "col": col_by[cols_on],
        }

    col_steps = sorted(range(1, n_col), key=lambda i: -around(i, n_col))
    plane_steps = [(i, j) for i in range(n_row) for j in range(n_own) if i or j]
    plane_steps.sort(key=lambda s: -(around(s[0], n_row) + around(s[1], n_own)))

    barrier = pltpu.get_barrier_semaphore()
    greeted = [by(i, j, 0) for i, j in plane_steps]
    greeted += [by(0, 0, i) for i in col_steps]
    for to in greeted:
        pl.semaphore_signal(barrier, inc=1, device_id=to, device_id_type=MESH)

    loads = [
        (basis_1, b1),
        (basis_2, b2),
        (tile_block, tb),
        (owner_list, ol),
    ]
    loads = [
        pltpu.make_async_copy(src, dst, load_sem.at[i])
        for i, (src, dst) in enumerate(loads)
    ]
    for copy in loads:
        copy.start()

    lane = lax.broadcasted_iota(jnp.int32, (8, LANES), 1)

    def corners(e, left, right):
        at = pl.ds(8 * e, 8)
        for f in range(FIELDS):
            x = fm[f, at, :] if f < 6 else mk[at, :].astype(jnp.float32)
            own = jnp.where(lane < 32, x, pltpu.roll(x, 64, 1))
            far = jnp.where(
                lane < 96,
                pltpu.roll(right, (56 - 16 * f) % LANES, 1),
                pltpu.roll(left, (120 - 16 * f) % LANES, 1),
            )
            fs[f, at, :] = jnp.where(lane < 64, own, far)

    corners(0, diag[0], diag[1])
    corners(chunks - 1, diag[2], diag[3])
    blocks = [
        recv_t[:, :, part * LANES : (part + 1) * LANES].reshape(LANES, LANES).T
        for part in range(rows // LANES)
    ]

    def spread(t, _):
        packed = blocks[8 * t // LANES][8 * t % LANES : 8 * t % LANES + 8, :]
        return [pltpu.roll(packed, (120 - 8 * f) % LANES, 1) for f in range(FIELDS)]

    def put(t, turned):
        at = slice(8 * t, 8 * t + 8)
        for f in range(FIELDS):
            fs[f, HALO + 8 * t : HALO + 8 * t + 8, :] = jnp.where(
                lane < 64, beside[f, at, :], turned[f]
            )

    pipeline(rows // 8, 4, spread, put)

    ends = [0, 1, 2, chunks - 3, chunks - 2, chunks - 1]
    upper, lower, strips = 1, 4, len(ends)

    def place(t):
        return (fm, ends[t]) if t < strips else (fs, t - strips)

    def field(f, t):
        source, e = place(t)
        return source[f, 8 * e : 8 * e + 8, :]

    strip_inside = (
        (lane < 64)
        | ((lane < 96) & (col < n_col - 1))
        | ((lane >= 96) & (col > 0))
    )

    def inside(t):
        e = place(t)[1]
        mask = strip_inside if t >= strips else None
        if e == 0 or e == chunks - 1:
            there = jnp.broadcast_to(
                line > 0 if e == 0 else line < n_line - 1, (8, LANES)
            )
            mask = there if mask is None else mask & there
        return mask

    def n_of(t):
        mask = inside(t)
        return field(0, t) if mask is None else jnp.where(mask, field(0, t), 0.0)

    def ice_of(t):
        e = place(t)[1]
        ice = mk[8 * e : 8 * e + 8, :] > 0 if t < strips else field(6, t) > 0.5
        mask = inside(t)
        return ice if mask is None else ice & mask

    def keep(t, k, now):
        vx[k, 8 * t : 8 * t + 8, :] = now

    solve(strips + chunks, (coef, hb, w, w2), n_of, ice_of, field, keep)

    def product(t):
        at = slice(8 * t, 8 * t + 8)
        return field(1, t) * (
            w[0, at, :] * vx[0, at, :] + w[1, at, :] * vx[1, at, :]
        )

    def merged(strip, turned, base):
        return jnp.where(lane < 8, strip, jnp.where(lane >= 120, turned, base))

    def strip_product(t, _):
        strip = product(strips + 1 + t)
        return strip, pltpu.roll(strip, 64, 1)

    def put_product(t, given):
        if t == 0 or t == rows // 8 - 1:
            base = product(upper if t == 0 else lower)
        else:
            base = dm[8 * t : 8 * t + 8, :]
        u = 8 * t % TILE
        piece = merged(*given, base)
        if 8 * t < TILE:
            dens[u : u + 8, :] = -piece
        else:
            dens[u : u + 8, :] = dens[u : u + 8, :] - piece

    pipeline(rows // 8, 8, strip_product, put_product)

    for copy in loads:
        copy.wait()
    first = jnp.dot(
        b1[...], dens[...], precision=HIGHEST, preferred_element_type=jnp.float32
    )
    product_ = jnp.dot(
        first, b2[...], precision=HIGHEST, preferred_element_type=jnp.float32
    )
    part = product_[0:8]
    for i in range(1, PER):
        part = jnp.where(lane < i * MODES, part, product_[8 * i : 8 * i + 8])
    in_second = tb[0, 0] > 2 * line
    parts = jnp.where(in_second, 0.0, part), jnp.where(in_second, part, 0.0)
    per_share = 8 // SHARES
    for i in range(SHARES):
        for j in range(2):
            at = pl.ds(j * per_share, per_share)
            send_a[i, at, :] = parts[j][i * per_share : (i + 1) * per_share, :]

    def start(phase, src, dst, to):
        pltpu.make_async_remote_copy(
            src_ref=src,
            dst_ref=dst,
            send_sem=phase_send.at[phase],
            recv_sem=phase_recv.at[phase],
            device_id=to,
            device_id_type=MESH,
        ).start()

    def arrived(phase, ref):
        pltpu.make_async_copy(ref, ref, phase_recv.at[phase]).wait()

    def departed(phase, ref):
        pltpu.make_async_copy(ref, ref, phase_send.at[phase]).wait()

    pl.semaphore_wait(barrier, len(greeted))
    share = wrapped(col, SHARES)
    for i in col_steps:
        to = by(0, 0, i)
        start(0, send_a.at[wrapped(to["col"], SHARES)], recv_a.at[col], to)
    recv_a[col] = send_a[share]

    def strip_velocity(t, _):
        found = []
        for k in range(2):
            at = 8 * (strips + 1 + t)
            strip = vx[k, at : at + 8, :]
            found.append((strip, pltpu.roll(strip, 64, 1)))
        return found

    def put_velocity(t, given):
        at = slice(8 * t, 8 * t + 8)
        for k in range(2):
            if t == 0 or t == rows // 8 - 1:
                e = 8 * (upper if t == 0 else lower)
                base = vx[k, e : e + 8, :]
            else:
                base = v_in[k, at, :]
            v[k, at, :] = merged(*given[k], base)

    pipeline(rows // 8, 8, strip_velocity, put_velocity)
    arrived(0, recv_a.at[0 : n_col - 1])
    total = recv_a[0]
    for i in range(1, n_col):
        total = total + recv_a[i]

    mine = table.at[pl.ds(2 * line, 2)]
    for j in range(2):
        table[2 * line + j] = total[j * per_share : (j + 1) * per_share, :]
    for i, j in plane_steps:
        start(1, mine, mine, by(i, j, 0))
    arrived(1, table.at[0 : 2 * n_line - 2])

    per_owner = ol.shape[0] // n_own
    width = per_share * LANES
    for k in range(per_owner):
        entry = table[ol[own_at * per_owner + k]]
        for j in range(per_share):
            at = pl.ds(pl.multiple_of(share * width + j * LANES, LANES), LANES)
            grad[0, k : k + 1, at] = entry[j : j + 1, :]

    mine_c = grad.at[0, :, pl.ds(pl.multiple_of(share * width, LANES), width)]
    for i in range(1, SHARES):
        to = {"row": row_at, "own": own_at, "col": lax.bitwise_xor(col, i)}
        start(2, mine_c, mine_c, to)
    arrived(2, grad.at[0, :, 0 : (SHARES - 1) * width])

    departed(0, recv_a.at[0 : n_col - 1])
    departed(1, table.at[0 : 2 * n_line - 2])
    departed(2, grad.at[0, :, 0 : (SHARES - 1) * width])


def write_out(velocity, gradient, to_velocity, to_gradient, sem):
    copies = [
        pltpu.make_async_copy(velocity, to_velocity, sem.at[0]),
        pltpu.make_async_copy(gradient, to_gradient, sem.at[1]),
    ]
    for copy in copies:
        copy.start()
    for copy in copies:
        copy.wait()


def solution(mesh):
    sizes = tuple(mesh.shape[a] for a in ("row", "own", "col"))
    n_line, n_col = sizes[0] * sizes[1], sizes[2]

    def local(viscosity, friction, driving, observed, ice_mask, tile_block, owner_list):
        rows = viscosity.shape[0]
        ext = rows + 2 * HALO
        first, second = bases()
        per_owner = owner_list.shape[0] // sizes[1]
        f32 = jnp.float32
        vmem = pltpu.VMEM
        fields = (viscosity, friction, driving, observed, ice_mask)
        tile_block = tile_block.reshape(1, -1)
        small = (tile_block, owner_list, jnp.asarray(first), jnp.asarray(second))
        hbm = pl.BlockSpec(memory_space=pltpu.HBM)
        here = pl.BlockSpec(memory_space=pltpu.VMEM)
        dma = pltpu.SemaphoreType.DMA

        def pinned(operands):
            return [pltpu.with_memory_space_constraint(x, pltpu.HBM) for x in operands]

        padded = pl.pallas_call(
            functools.partial(exchange, sizes),
            out_shape=(
                jax.ShapeDtypeStruct((6, ext, LANES), f32),
                jax.ShapeDtypeStruct((ext, LANES), jnp.int32),
                jax.ShapeDtypeStruct((16, 8, rows), f32),
                jax.ShapeDtypeStruct((4, 8, LANES), f32),
                jax.ShapeDtypeStruct((FIELDS, rows, LANES), f32),
                jax.ShapeDtypeStruct((2, rows, LANES), f32),
                jax.ShapeDtypeStruct((rows, LANES), f32),
            ),
            in_specs=[hbm] * 5,
            out_specs=[here] * 7,
            scratch_shapes=[
                vmem((rows, LANES), f32),
                vmem((8, 16, rows), f32),
                vmem((4, rows, LANES), f32),
                vmem((2, rows, LANES), f32),
                vmem((4, rows + 8, LANES), f32),
                vmem((4, rows + 8, LANES), f32),
                dma((5,)),
                dma((10,)),
                dma((10,)),
            ],
            compiler_params=pltpu.CompilerParams(
                collective_id=0,
                has_side_effects=True,
                vmem_limit_bytes=16 * 2**20,
            ),
        )(*pinned(fields))
        results = pl.pallas_call(
            functools.partial(kernel, sizes),
            out_shape=(
                jax.ShapeDtypeStruct((2, rows, LANES), f32),
                jax.ShapeDtypeStruct((1, per_owner, MODES * MODES), f32),
            ),
            in_specs=[here] * 7 + [hbm] * 4,
            out_specs=[here] * 2,
            scratch_shapes=[
                vmem((FIELDS, ext, LANES), f32),
                vmem((4, ext + 48, LANES), f32),
                vmem((2, ext + 48, LANES), f32),
                vmem((4, ext + 56, LANES), f32),
                vmem((4, ext + 56, LANES), f32),
                vmem((2, ext + 48, LANES), f32),
                vmem((TILE, LANES), f32),
                vmem(first.shape, f32),
                vmem(second.shape, f32),
                pltpu.SMEM(tile_block.shape, jnp.int32),
                pltpu.SMEM(owner_list.shape, jnp.int32),
                vmem((SHARES, 2 * 8 // SHARES, LANES), f32),
                vmem((n_col, 2 * 8 // SHARES, LANES), f32),
                vmem((2 * n_line, 8 // SHARES, LANES), f32),
                dma((4,)),
                dma((3,)),
                dma((3,)),
            ],
            compiler_params=pltpu.CompilerParams(
                collective_id=1,
                has_side_effects=True,
                vmem_limit_bytes=32 * 2**20,
            ),
        )(*padded, *pinned(small))
        return pl.pallas_call(
            write_out,
            out_shape=[jax.ShapeDtypeStruct(x.shape, f32) for x in results],
            in_specs=[here] * 2,
            out_specs=[hbm] * 2,
            scratch_shapes=[dma((2,))],
            compiler_params=pltpu.CompilerParams(vmem_limit_bytes=2**20),
        )(*results)

    return jax.shard_map(
        local,
        mesh=mesh,
        in_specs=(
            P(("row", "own"), "col"),
            P(("row", "own"), "col"),
            P(None, ("row", "own"), "col"),
            P(None, ("row", "own"), "col"),
            P(("row", "own"), "col"),
            P(("row", "own"), "col"),
            P(),
        ),
        out_specs=(P(None, ("row", "own"), "col"), P("own", None, None)),
        check_vma=False,
    )
```

```python
import functools
import math

import jax
import jax.numpy as jnp
import numpy as np
from jax import lax
from jax.experimental import pallas as pl
from jax.experimental.pallas import tpu as pltpu
from jax.sharding import PartitionSpec as P

TILE = 128
MODES = 32
LANES = 128
HALO = 8
FIELDS = 7
SWEEPS = 3
PER = LANES // MODES
SHARES = 4
LAG = 12
MESH = pl.DeviceIdType.MESH
HIGHEST = lax.Precision.HIGHEST


def bases():
    places = np.arange(TILE) + 0.5
    orders = np.arange(MODES)
    cosine = np.cos(math.pi * orders[:, None] * places[None, :] / TILE)
    first = np.concatenate([cosine[s::PER] for s in range(PER)], axis=0)
    second = np.concatenate([cosine.T / TILE] * PER, axis=1)
    return first.astype(np.float32), second.astype(np.float32)


def around(step, size):
    return min(step % size, -step % size)


def wrapped(x, size):
    if size & (size - 1) == 0:
        return lax.bitwise_and(x, size - 1)
    return lax.rem(x + size, size)


def quotient(x, size):
    if size & (size - 1) == 0:
        return lax.shift_right_logical(x, size.bit_length() - 1)
    return lax.div(x, size)


def pipeline(count, lag, *stages):
    held = {}
    for step in range(count + lag * (len(stages) - 1)):
        for i, stage in reversed(list(enumerate(stages))):
            t = step - i * lag
            if 0 <= t < count:
                held[t] = stage(t, held.pop(t, None))


def solve(chunks, refs, n_of, ice_of, field, keep):
    coef, hb, w, w2 = refs
    first_sub = lax.broadcasted_iota(jnp.int32, (8, LANES), 0) == 0
    zero = jnp.zeros((8, LANES), jnp.float32)

    def rows_of(t):
        return slice(8 * t, 8 * t + 8)

    def down(x, kept):
        turned = pltpu.roll(x, 1, 0)
        return jnp.where(first_sub, kept, turned), turned

    def store_state(to, t, k, now):
        to[k, rows_of(t), :] = now
        return pltpu.roll(now, LANES - 1, 1)

    def store_ahead(to):
        def stage(t, turned):
            for k in range(2):
                to[2 + k, rows_of(t), :] = turned[k]

        return stage

    def open_(t, _):
        n = n_of(t)
        return n, pltpu.roll(n, 1, 1)

    summed_kept = [zero]

    def settle(t, given):
        n, turned = given
        at = rows_of(t)
        summed = n + turned
        moved, summed_kept[0] = down(summed, summed_kept[0])
        f = field(1, t)
        half = jnp.where(ice_of(t), 0.5 / (1.25 * (summed + moved) + f), 0.0)
        coef[0, at, :] = 0.5 * n
        coef[1, at, :] = 0.25 * n
        coef[2, at, :] = half
        coef[3, at, :] = 1.0 - half * f
        out = []
        for k in range(2):
            scaled = half * field(2 + k, t)
            hb[k, at, :] = scaled
            out.append(store_state(w, t, k, scaled + scaled))
        return out

    pipeline(chunks, LAG, open_, settle, store_ahead(w))
    for k in range(4):
        w[k, rows_of(chunks), :] = zero
        w2[k, rows_of(chunks), :] = zero

    def turn():
        def begin(t, _):
            at = rows_of(t)
            out = []
            for k in range(2):
                now = w2[k, at, :]
                keep(t, k, now)
                scaled = coef[2, at, :] * (now - field(4 + k, t))
                hb[k, at, :] = scaled
                out.append(store_state(w2, t, k, scaled + scaled))
            return out

        pipeline(chunks, LAG, begin, store_ahead(w2))

    def sweep(w_from, w_to):
        kept = [zero] * 4

        def front(t, _):
            at, after = rows_of(t), slice(8 * t + 1, 8 * t + 9)
            dx, dy = [], []
            for k in range(2):
                here, here_next = w_from[k, at, :], w_from[2 + k, at, :]
                below, below_next = w_from[k, after, :], w_from[2 + k, after, :]
                dx.append((below - here) + (below_next - here_next))
                dy.append((here_next + below_next) - (here + below))
            m, q = coef[0, at, :], coef[1, at, :]
            total = dx[0] + dy[1]
            one = m * (total + dx[0])
            two = m * (total + dy[1])
            shear = q * (dy[0] + dx[1])
            fields = (one + shear, one - shear, two + shear, shear - two)
            moved = []
            for i in range(4):
                got, kept[i] = down(fields[i], kept[i])
                moved.append(got)
            stay = (moved[1] - fields[0], moved[3] - fields[2])
            go = (moved[0] - fields[1], moved[2] - fields[3])
            return stay, tuple(pltpu.roll(x, 1, 1) for x in go)

        def close(t, given):
            at = rows_of(t)
            turned = []
            for k in range(2):
                image = given[0][k] + given[1][k]
                now = (
                    coef[3, at, :] * w_from[k, at, :] + hb[k, at, :]
                ) - coef[2, at, :] * image
                turned.append(store_state(w_to, t, k, now))
            return turned

        pipeline(chunks, LAG, front, close, store_ahead(w_to))

    def pair(s, _):
        sweep(w, w2)

        @pl.when(s == 1)
        def _():
            turn()

        sweep(w2, w)
        return 0

    lax.fori_loop(0, SWEEPS, pair, 0)


def exchange(
    sizes,
    visc,
    fric,
    drv,
    obs,
    mask,
    fm,
    mk,
    recv_t,
    diag,
    beside,
    v,
    dm,
    pack,
    pack_t,
    coef,
    hb,
    w,
    w2,
    load_sem,
    halo_send,
    halo_recv,
):
    n_row, n_own, n_col = sizes
    n_line = n_row * n_own
    rows = visc.shape[0]
    row_at, own_at, col = (
        lax.axis_index("row"),
        lax.axis_index("own"),
        lax.axis_index("col"),
    )
    line = row_at * n_own + own_at

    row_by = [wrapped(row_at + i, n_row) for i in range(n_row)]
    own_by = [wrapped(own_at + i, n_own) for i in range(n_own)]
    col_by = [wrapped(col + i, n_col) for i in range(n_col)]

    def by(rows_on, owns_on, cols_on):
        return {
            "row": row_by[rows_on],
            "own": own_by[owns_on],
            "col": col_by[cols_on],
        }

    line_by = {i: wrapped(line + i, n_line) for i in (-1, 1)}
    line_by = {
        i: (quotient(to, n_own), wrapped(to, n_own)) for i, to in line_by.items()
    }

    def next_to(line_on, cols_on):
        return {
            "row": line_by[line_on][0],
            "own": line_by[line_on][1],
            "col": col_by[cols_on],
        }

    barrier = pltpu.get_barrier_semaphore()
    greeted = [next_to(i, j) for i in (-1, 1) for j in (-1, 0, 1)]
    greeted += [by(0, 0, i) for i in (-1, 1)]
    for to in greeted:
        pl.semaphore_signal(barrier, inc=1, device_id=to, device_id_type=MESH)

    own_rows = pl.ds(HALO, rows)
    loads = [
        (visc, fm.at[0, own_rows, :]),
        (fric, fm.at[1, own_rows, :]),
        (drv, fm.at[2:4, own_rows, :]),
        (obs, fm.at[4:6, own_rows, :]),
        (mask, mk.at[own_rows, :]),
    ]
    loads = [
        pltpu.make_async_copy(src, dst, load_sem.at[i])
        for i, (src, dst) in enumerate(loads)
    ]
    for copy in loads:
        copy.start()

    lane = lax.broadcasted_iota(jnp.int32, (8, LANES), 1)

    for copy in loads:
        copy.wait()

    def gather(t, _):
        at = pl.ds(HALO + 8 * t, 8)
        found = [fm[f, at, :] for f in range(6)] + [mk[at, :].astype(jnp.float32)]
        return [pltpu.roll(piece, 16 * f + 8, 1) for f, piece in enumerate(found)]

    def merge(t, pieces):
        packed = pieces[0]
        for f in range(1, FIELDS):
            packed = jnp.where(lane < 16 * f, packed, pieces[f])
        pack[8 * t : 8 * t + 8, :] = packed

    pipeline(rows // 8, 4, gather, merge)
    for part in range(rows // LANES):
        block = pack[part * LANES : (part + 1) * LANES, :]
        pack_t[:, :, part * LANES : (part + 1) * LANES] = block.T.reshape(8, 16, LANES)
    recv_t[FIELDS : 16 - FIELDS] = jnp.zeros((2, 8, rows), jnp.float32)

    pl.semaphore_wait(barrier, len(greeted))
    copies = []

    def send(src, dst, to):
        at = len(copies)
        copy = pltpu.make_async_remote_copy(
            src_ref=src,
            dst_ref=dst,
            send_sem=halo_send.at[at],
            recv_sem=halo_recv.at[at],
            device_id=to,
            device_id_type=MESH,
        )
        copy.start()
        copies.append(copy)

    for line_on, source, slot in ((-1, 0, 2), (1, rows - 8, 0)):
        for cols_on in (-1, 1):
            send(
                pack.at[pl.ds(source, 8), :],
                diag.at[slot + (1 if cols_on < 0 else 0)],
                next_to(line_on, cols_on),
            )
    send(pack_t.at[0:FIELDS, 0:8, :], recv_t.at[0:FIELDS], by(0, 0, 1))
    send(pack_t.at[0:FIELDS, 8:16, :], recv_t.at[16 - FIELDS : 16], by(0, 0, -1))
    for line_on, source, target in ((-1, HALO, HALO + rows), (1, rows, 0)):
        to, take = pl.ds(target, HALO), pl.ds(source, HALO)
        send(fm.at[:, take, :], fm.at[:, to, :], next_to(line_on, 0))
        send(mk.at[take, :], mk.at[to, :], next_to(line_on, 0))

    def turn_half(t, _):
        at = pl.ds(HALO + 8 * t, 8)
        found = [fm[f, at, :] for f in range(6)] + [mk[at, :].astype(jnp.float32)]
        return [(x, pltpu.roll(x, 64, 1)) for x in found]

    def put_half(t, pieces):
        for f, (x, turned) in enumerate(pieces):
            beside[f, 8 * t : 8 * t + 8, :] = jnp.where(lane < 32, x, turned)

    pipeline(rows // 8, 2, turn_half, put_half)

    def field(f, t):
        return fm[f, HALO + 8 * t : HALO + 8 * t + 8, :]

    def keep(t, k, now):
        v[k, 8 * t : 8 * t + 8, :] = now

    solve(
        rows // 8,
        (coef, hb, w, w2),
        lambda t: field(0, t),
        lambda t: mk[HALO + 8 * t : HALO + 8 * t + 8, :] > 0,
        field,
        keep,
    )
    for t in range(1, rows // 8 - 1):
        at = slice(8 * t, 8 * t + 8)
        dm[at, :] = field(1, t) * (
            w[0, at, :] * v[0, at, :] + w[1, at, :] * v[1, at, :]
        )

    for copy in copies:
        copy.wait()


def kernel(
    sizes,
    fm,
    mk,
    recv_t,
    diag,
    beside,
    v_in,
    dm,
    tile_block,
    owner_list,
    basis_1,
    basis_2,
    v,
    grad,
    fs,
    coef,
    hb,
    w,
    w2,
    vx,
    dens,
    b1,
    b2,
    tb,
    ol,
    send_a,
    recv_a,
    table,
    load_sem,
    phase_send,
    phase_recv,
):
    n_row, n_own, n_col = sizes
    n_line = n_row * n_own
    rows = fm.shape[1] - 2 * HALO
    chunks = (rows + 2 * HALO) // 8
    row_at, own_at, col = (
        lax.axis_index("row"),
        lax.axis_index("own"),
        lax.axis_index("col"),
    )
    line = row_at * n_own + own_at

    row_by = [wrapped(row_at + i, n_row) for i in range(n_row)]
    own_by = [wrapped(own_at + i, n_own) for i in range(n_own)]
    col_by = [wrapped(col + i, n_col) for i in range(n_col)]

    def by(rows_on, owns_on, cols_on):
        return {
            "row": row_by[rows_on],
            "own": own_by[owns_on],
            "col": col_by[cols_on],
        }

    col_steps = sorted(range(1, n_col), key=lambda i: -around(i, n_col))
    plane_steps = [(i, j) for i in range(n_row) for j in range(n_own) if i or j]
    plane_steps.sort(key=lambda s: -(around(s[0], n_row) + around(s[1], n_own)))

    barrier = pltpu.get_barrier_semaphore()
    greeted = [by(i, j, 0) for i, j in plane_steps]
    greeted += [by(0, 0, i) for i in col_steps]
    for to in greeted:
        pl.semaphore_signal(barrier, inc=1, device_id=to, device_id_type=MESH)

    loads = [
        (basis_1, b1),
        (basis_2, b2),
        (tile_block, tb),
        (owner_list, ol),
    ]
    loads = [
        pltpu.make_async_copy(src, dst, load_sem.at[i])
        for i, (src, dst) in enumerate(loads)
    ]
    for copy in loads:
        copy.start()

    lane = lax.broadcasted_iota(jnp.int32, (8, LANES), 1)

    def corners(e, left, right):
        at = pl.ds(8 * e, 8)
        for f in range(FIELDS):
            x = fm[f, at, :] if f < 6 else mk[at, :].astype(jnp.float32)
            own = jnp.where(lane < 32, x, pltpu.roll(x, 64, 1))
            far = jnp.where(
                lane < 96,
                pltpu.roll(right, (56 - 16 * f) % LANES, 1),
                pltpu.roll(left, (120 - 16 * f) % LANES, 1),
            )
            fs[f, at, :] = jnp.where(lane < 64, own, far)

    corners(0, diag[0], diag[1])
    corners(chunks - 1, diag[2], diag[3])
    blocks = [
        recv_t[:, :, part * LANES : (part + 1) * LANES].reshape(LANES, LANES).T
        for part in range(rows // LANES)
    ]

    def spread(t, _):
        packed = blocks[8 * t // LANES][8 * t % LANES : 8 * t % LANES + 8, :]
        return [pltpu.roll(packed, (120 - 8 * f) % LANES, 1) for f in range(FIELDS)]

    def put(t, turned):
        at = slice(8 * t, 8 * t + 8)
        for f in range(FIELDS):
            fs[f, HALO + 8 * t : HALO + 8 * t + 8, :] = jnp.where(
                lane < 64, beside[f, at, :], turned[f]
            )

    pipeline(rows // 8, 4, spread, put)

    ends = [0, 1, 2, chunks - 3, chunks - 2, chunks - 1]
    upper, lower, strips = 1, 4, len(ends)

    def place(t):
        return (fm, ends[t]) if t < strips else (fs, t - strips)

    def field(f, t):
        source, e = place(t)
        return source[f, 8 * e : 8 * e + 8, :]

    strip_inside = (
        (lane < 64)
        | ((lane < 96) & (col < n_col - 1))
        | ((lane >= 96) & (col > 0))
    )

    def inside(t):
        e = place(t)[1]
        mask = strip_inside if t >= strips else None
        if e == 0 or e == chunks - 1:
            there = jnp.broadcast_to(
                line > 0 if e == 0 else line < n_line - 1, (8, LANES)
            )
            mask = there if mask is None else mask & there
        return mask

    def n_of(t):
        mask = inside(t)
        return field(0, t) if mask is None else jnp.where(mask, field(0, t), 0.0)

    def ice_of(t):
        e = place(t)[1]
        ice = mk[8 * e : 8 * e + 8, :] > 0 if t < strips else field(6, t) > 0.5
        mask = inside(t)
        return ice if mask is None else ice & mask

    def keep(t, k, now):
        vx[k, 8 * t : 8 * t + 8, :] = now

    solve(strips + chunks, (coef, hb, w, w2), n_of, ice_of, field, keep)

    def product(t):
        at = slice(8 * t, 8 * t + 8)
        return field(1, t) * (
            w[0, at, :] * vx[0, at, :] + w[1, at, :] * vx[1, at, :]
        )

    def merged(strip, turned, base):
        return jnp.where(lane < 8, strip, jnp.where(lane >= 120, turned, base))

    def strip_product(t, _):
        strip = product(strips + 1 + t)
        return strip, pltpu.roll(strip, 64, 1)

    def put_product(t, given):
        if t == 0 or t == rows // 8 - 1:
            base = product(upper if t == 0 else lower)
        else:
            base = dm[8 * t : 8 * t + 8, :]
        u = 8 * t % TILE
        piece = merged(*given, base)
        if 8 * t < TILE:
            dens[u : u + 8, :] = -piece
        else:
            dens[u : u + 8, :] = dens[u : u + 8, :] - piece

    pipeline(rows // 8, 8, strip_product, put_product)

    for copy in loads:
        copy.wait()
    first = jnp.dot(
        b1[...], dens[...], precision=HIGHEST, preferred_element_type=jnp.float32
    )
    product_ = jnp.dot(
        first, b2[...], precision=HIGHEST, preferred_element_type=jnp.float32
    )
    part = product_[0:8]
    for i in range(1, PER):
        part = jnp.where(lane < i * MODES, part, product_[8 * i : 8 * i + 8])
    in_second = tb[0, 0] > 2 * line
    parts = jnp.where(in_second, 0.0, part), jnp.where(in_second, part, 0.0)
    per_share = 8 // SHARES
    for i in range(SHARES):
        for j in range(2):
            at = pl.ds(j * per_share, per_share)
            send_a[i, at, :] = parts[j][i * per_share : (i + 1) * per_share, :]

    def start(phase, src, dst, to):
        pltpu.make_async_remote_copy(
            src_ref=src,
            dst_ref=dst,
            send_sem=phase_send.at[phase],
            recv_sem=phase_recv.at[phase],
            device_id=to,
            device_id_type=MESH,
        ).start()

    def arrived(phase, ref):
        pltpu.make_async_copy(ref, ref, phase_recv.at[phase]).wait()

    def departed(phase, ref):
        pltpu.make_async_copy(ref, ref, phase_send.at[phase]).wait()

    pl.semaphore_wait(barrier, len(greeted))
    share = wrapped(col, SHARES)
    for i in col_steps:
        to = by(0, 0, i)
        start(0, send_a.at[wrapped(to["col"], SHARES)], recv_a.at[col], to)
    recv_a[col] = send_a[share]

    def strip_velocity(t, _):
        found = []
        for k in range(2):
            at = 8 * (strips + 1 + t)
            strip = vx[k, at : at + 8, :]
            found.append((strip, pltpu.roll(strip, 64, 1)))
        return found

    def put_velocity(t, given):
        at = slice(8 * t, 8 * t + 8)
        for k in range(2):
            if t == 0 or t == rows // 8 - 1:
                e = 8 * (upper if t == 0 else lower)
                base = vx[k, e : e + 8, :]
            else:
                base = v_in[k, at, :]
            v[k, at, :] = merged(*given[k], base)

    pipeline(rows // 8, 8, strip_velocity, put_velocity)
    arrived(0, recv_a.at[0 : n_col - 1])
    total = recv_a[0]
    for i in range(1, n_col):
        total = total + recv_a[i]

    mine = table.at[pl.ds(2 * line, 2)]
    for j in range(2):
        table[2 * line + j] = total[j * per_share : (j + 1) * per_share, :]
    for i, j in plane_steps:
        start(1, mine, mine, by(i, j, 0))
    arrived(1, table.at[0 : 2 * n_line - 2])

    per_owner = ol.shape[0] // n_own
    width = per_share * LANES
    for k in range(per_owner):
        entry = table[ol[own_at * per_owner + k]]
        for j in range(per_share):
            at = pl.ds(pl.multiple_of(share * width + j * LANES, LANES), LANES)
            grad[0, k : k + 1, at] = entry[j : j + 1, :]

    mine_c = grad.at[0, :, pl.ds(pl.multiple_of(share * width, LANES), width)]
    for i in range(1, SHARES):
        to = {"row": row_at, "own": own_at, "col": lax.bitwise_xor(col, i)}
        start(2, mine_c, mine_c, to)
    arrived(2, grad.at[0, :, 0 : (SHARES - 1) * width])

    departed(0, recv_a.at[0 : n_col - 1])
    departed(1, table.at[0 : 2 * n_line - 2])
    departed(2, grad.at[0, :, 0 : (SHARES - 1) * width])


def write_out(velocity, gradient, to_velocity, to_gradient, sem):
    copies = [
        pltpu.make_async_copy(velocity, to_velocity, sem.at[0]),
        pltpu.make_async_copy(gradient, to_gradient, sem.at[1]),
    ]
    for copy in copies:
        copy.start()
    for copy in copies:
        copy.wait()


def solution(mesh):
    sizes = tuple(mesh.shape[a] for a in ("row", "own", "col"))
    n_line, n_col = sizes[0] * sizes[1], sizes[2]

    def local(viscosity, friction, driving, observed, ice_mask, tile_block, owner_list):
        rows = viscosity.shape[0]
        ext = rows + 2 * HALO
        first, second = bases()
        per_owner = owner_list.shape[0] // sizes[1]
        f32 = jnp.float32
        vmem = pltpu.VMEM
        fields = (viscosity, friction, driving, observed, ice_mask)
        tile_block = tile_block.reshape(1, -1)
        small = (tile_block, owner_list, jnp.asarray(first), jnp.asarray(second))
        hbm = pl.BlockSpec(memory_space=pltpu.HBM)
        here = pl.BlockSpec(memory_space=pltpu.VMEM)
        dma = pltpu.SemaphoreType.DMA

        def pinned(operands):
            return [pltpu.with_memory_space_constraint(x, pltpu.HBM) for x in operands]

        padded = pl.pallas_call(
            functools.partial(exchange, sizes),
            out_shape=(
                jax.ShapeDtypeStruct((6, ext, LANES), f32),
                jax.ShapeDtypeStruct((ext, LANES), jnp.int32),
                jax.ShapeDtypeStruct((16, 8, rows), f32),
                jax.ShapeDtypeStruct((4, 8, LANES), f32),
                jax.ShapeDtypeStruct((FIELDS, rows, LANES), f32),
                jax.ShapeDtypeStruct((2, rows, LANES), f32),
                jax.ShapeDtypeStruct((rows, LANES), f32),
            ),
            in_specs=[hbm] * 5,
            out_specs=[here] * 7,
            scratch_shapes=[
                vmem((rows, LANES), f32),
                vmem((8, 16, rows), f32),
                vmem((4, rows, LANES), f32),
                vmem((2, rows, LANES), f32),
                vmem((4, rows + 8, LANES), f32),
                vmem((4, rows + 8, LANES), f32),
                dma((5,)),
                dma((10,)),
                dma((10,)),
            ],
            compiler_params=pltpu.CompilerParams(
                collective_id=0,
                has_side_effects=True,
                vmem_limit_bytes=16 * 2**20,
            ),
        )(*pinned(fields))
        results = pl.pallas_call(
            functools.partial(kernel, sizes),
            out_shape=(
                jax.ShapeDtypeStruct((2, rows, LANES), f32),
                jax.ShapeDtypeStruct((1, per_owner, MODES * MODES), f32),
            ),
            in_specs=[here] * 7 + [hbm] * 4,
            out_specs=[here] * 2,
            scratch_shapes=[
                vmem((FIELDS, ext, LANES), f32),
                vmem((4, ext + 48, LANES), f32),
                vmem((2, ext + 48, LANES), f32),
                vmem((4, ext + 56, LANES), f32),
                vmem((4, ext + 56, LANES), f32),
                vmem((2, ext + 48, LANES), f32),
                vmem((TILE, LANES), f32),
                vmem(first.shape, f32),
                vmem(second.shape, f32),
                pltpu.SMEM(tile_block.shape, jnp.int32),
                pltpu.SMEM(owner_list.shape, jnp.int32),
                vmem((SHARES, 2 * 8 // SHARES, LANES), f32),
                vmem((n_col, 2 * 8 // SHARES, LANES), f32),
                vmem((2 * n_line, 8 // SHARES, LANES), f32),
                dma((4,)),
                dma((3,)),
                dma((3,)),
            ],
            compiler_params=pltpu.CompilerParams(
                collective_id=1,
                has_side_effects=True,
                vmem_limit_bytes=32 * 2**20,
            ),
        )(*padded, *pinned(small))
        return pl.pallas_call(
            write_out,
            out_shape=[jax.ShapeDtypeStruct(x.shape, f32) for x in results],
            in_specs=[here] * 2,
            out_specs=[hbm] * 2,
            scratch_shapes=[dma((2,))],
            compiler_params=pltpu.CompilerParams(vmem_limit_bytes=2**20),
        )(*results)

    return jax.shard_map(
        local,
        mesh=mesh,
        in_specs=(
            P(("row", "own"), "col"),
            P(("row", "own"), "col"),
            P(None, ("row", "own"), "col"),
            P(None, ("row", "own"), "col"),
            P(("row", "own"), "col"),
            P(("row", "own"), "col"),
            P(),
        ),
        out_specs=(P(None, ("row", "own"), "col"), P("own", None, None)),
        check_vma=False,
    )
```
